32 devices in a mesh: req: 16 (over z, y, x), tp: 2 (over core).
Axes of the slice: x: 2, y: 2, z: 4, core: 2. Of those that a mesh axis runs over, the one named last changes fastest.
Arguments:
- hidden_in: bfloat16 [4, 64, 3072], P(None, 'req', 'tp'), may hold values from -6 to 6
- norm_gain: float32 [3072], replicated, may hold values from 0.1 to 1.9
- w_query: bfloat16 [3072, 2048], P(None, 'tp'), may hold values from -1 to 1
- w_key: bfloat16 [3072, 1024], P(None, 'tp'), may hold values from -1 to 1
- w_value: bfloat16 [3072, 1024], P(None, 'tp'), may hold values from -0.109375 to 0.109375
- w_out: bfloat16 [2048, 3072], P('tp'), may hold values from -0.125 to 0.125
- prompt_keys: bfloat16 [16, 512, 1024], P('req', None, 'tp'), may hold values from -100 to 100
- prompt_values: bfloat16 [16, 512, 1024], P('req', None, 'tp'), may hold values from -8 to 8
- gen_keys: bfloat16 [64, 64, 1024], P('req', None, 'tp'), may hold values from -9 to 9
- gen_values: bfloat16 [64, 64, 1024], P('req', None, 'tp'), may hold values from -8 to 8
- lengths: int32 [8], replicated, may hold values from 768 to 1024, as said below
- parents: int32 [4, 64], replicated, may hold values from 0 to 7
Outputs:
- attended: bfloat16 [4, 64, 3072], P(None, 'req', 'tp')
The draws below stay inside these ranges and needn't reach their ends.
Inputs may be any that keep to these rules, and one draw needn't show every extreme that they name: `lengths`: one request has a prompt of exactly 1024 tokens.
All inputs are finite; a program needn't handle non-finite values.
Results may differ from the reference program's by a relative error of at most 0.028.
Values may be sent and summed in bfloat16 or wider, within the bound.
No kernel may reach another device: no remote copies, remote signals or barrier semaphores. Data moves between devices by JAX's collectives and lax.ppermute only.
A program may use at most 64 MiB of HBM per device.

```python
import jax
import jax.numpy as jnp
from jax import lax

D = 3072
KVH = 8
HD = 128
QH = 16
BEAMS = 8
STEPS = 4
PROMPT_MAX = 1024
GEN0 = 64
REQUESTS = 8
HALF = 512


def draw_lengths(key, part):
    drawn = jax.random.randint(key, (REQUESTS,), 3 * PROMPT_MAX // 4, PROMPT_MAX + 1, dtype=jnp.int32)
    longest = jax.random.randint(jax.random.fold_in(key, 7), (), 0, REQUESTS, dtype=jnp.int32)
    return jnp.where(jnp.arange(REQUESTS, dtype=jnp.int32) == longest, PROMPT_MAX, drawn).astype(jnp.int32)


def shared_query(key):
    return jax.random.truncated_normal(jax.random.fold_in(key, 11), -4.0, 4.0, (D, QH * HD), jnp.float32) * D ** (-0.5)


def draw_w_query(key, part):
    return shared_query(key).astype(jnp.bfloat16)


def draw_w_key(key, part):
    q_group = QH // KVH
    query_heads = shared_query(key).reshape(D, KVH, q_group, HD)
    picked = jax.random.randint(jax.random.fold_in(key, 13), (KVH,), 0, q_group, dtype=jnp.int32)
    chosen = jnp.take_along_axis(query_heads, picked[None, :, None, None], axis=2)[:, :, 0, :]
    mixing = jax.random.uniform(jax.random.fold_in(key, 17), (KVH,), jnp.float32, 0.35, 0.75)
    rest = jnp.sqrt(1.0 - mixing * mixing)
    noise = jax.random.truncated_normal(jax.random.fold_in(key, 19), -4.0, 4.0, (D, KVH, HD), jnp.float32) * D ** (-0.5)
    mixed = mixing[None, :, None] * chosen + rest[None, :, None] * noise
    return mixed.reshape(D, KVH * HD).astype(jnp.bfloat16)


def draw_prompt_keys(key, part):
    shape = (REQUESTS * 2, HALF, KVH * HD)
    base = 1.5 * jax.random.truncated_normal(key, -6.0, 6.0, shape, jnp.float32)
    return base.astype(jnp.bfloat16)


def set_ends(entries, stream_key, least, high):
    extent = entries.shape
    index_at = [jax.random.randint(jax.random.fold_in(stream_key, axis), (), 0, extent[axis]) for axis in range(len(extent))]
    entries = entries.at[tuple(index_at)].set(least)
    longest = extent.index(max(extent))
    index_at[longest] = (index_at[longest] + 1) % extent[longest]
    return entries.at[tuple(index_at)].set(high)


def block_levels(rng, shape, pieces, low, top_value):
    level = 1.0
    for position, parts in pieces:
        heights = jax.random.uniform(jax.random.fold_in(jax.random.fold_in(rng, 6), position), (parts,), jnp.float32, low / len(pieces), top_value / len(pieces))
        level = level * jnp.repeat(jnp.exp(heights), shape[position] // parts).reshape((-1,) + (1,) * (len(shape) - 1 - position))
    return level


def bell_draw(rng, extent, scale, limit, pieces=(), kind=jnp.bfloat16):
    result = scale * jax.random.normal(rng, extent, jnp.float32)
    if pieces:
        result = result * block_levels(rng, extent, pieces, -0.22, 0.18)
    return jnp.clip(result, -limit, limit).astype(kind)


def setup_inputs(seed: int = 0) -> dict:
    key_list = jax.random.split(jax.random.key(seed), 13)
    hidden_in = bell_draw(key_list[0], (STEPS, REQUESTS * BEAMS, D), 1.0, 6.0, ((1, 16), (2, 2)))
    norm_gain = jnp.clip(1.0 + 0.18 * jax.random.normal(key_list[1], (D,), jnp.float32), 0.1, 1.9)
    w_query = draw_w_query(jax.random.fold_in(key_list[12], 71), 0)
    w_key = draw_w_key(jax.random.fold_in(key_list[12], 71), 0)
    w_value = bell_draw(key_list[4], (D, KVH * HD), D ** -0.5, 0.109375, ((1, 2),))
    w_out = bell_draw(key_list[5], (QH * HD, D), (QH * HD) ** -0.5, 0.125, ((0, 2),))
    prompt_keys = draw_prompt_keys(jax.random.fold_in(key_list[12], 71), 0)
    prompt_values = bell_draw(key_list[7], (REQUESTS * 2, HALF, KVH * HD), 2.0, 8.0, ((0, 16), (2, 2)))
    gen_keys = bell_draw(key_list[8], (REQUESTS * BEAMS, GEN0, KVH * HD), 1.5, 9.0, ((0, 16), (2, 2)))
    gen_values = bell_draw(key_list[9], (REQUESTS * BEAMS, GEN0, KVH * HD), 2.0, 8.0, ((0, 16), (2, 2)))
    lengths = draw_lengths(jax.random.fold_in(key_list[12], 71), 0)
    parents = set_ends(jax.random.randint(key_list[11], (STEPS, REQUESTS * BEAMS), 0, BEAMS), jax.random.fold_in(key_list[11], 1), 0, BEAMS - 1).astype(jnp.int32)
    return dict(hidden_in=hidden_in, norm_gain=norm_gain, w_query=w_query, w_key=w_key, w_value=w_value, w_out=w_out, prompt_keys=prompt_keys, prompt_values=prompt_values, gen_keys=gen_keys, gen_values=gen_values, lengths=lengths, parents=parents)


norm_eps = 1e-05
masked_score = -1e+30
rope_base = 500000.0

def rotate(vectors, positions):
    half_dim = vectors.shape[-1] // 2
    inverse = rope_base ** (-jnp.arange(half_dim, dtype=jnp.float32) / half_dim)
    angles = positions.astype(jnp.float32)[:, None, None] * inverse
    cosine = jnp.cos(angles)
    sine_part = jnp.sin(angles)
    first = vectors[..., :half_dim]
    second = vectors[..., half_dim:]
    return jnp.concatenate([first * cosine - second * sine_part, second * cosine + first * sine_part], axis=-1)

def reference(hidden_in, norm_gain, w_query, w_key, w_value, w_out, prompt_keys, prompt_values, gen_keys, gen_values, lengths, parents):
    beam_rows = hidden_in.shape[1]
    requests = beam_rows // BEAMS
    q_group = QH // KVH
    scaling = HD ** (-0.5)
    prompt_k = prompt_keys.reshape(requests, 2 * HALF, KVH, HD).astype(jnp.float32)
    prompt_v = prompt_values.reshape(requests, 2 * HALF, KVH, HD).astype(jnp.float32)
    cache_k = gen_keys.reshape(requests, BEAMS, GEN0, KVH, HD)
    cache_v = gen_values.reshape(requests, BEAMS, GEN0, KVH, HD)
    usable = jnp.arange(2 * HALF, dtype=jnp.int32)[None, :] < lengths[:, None]
    choose = jax.vmap(lambda table, index: table[index])
    results = []
    for step in range(STEPS):
        inputs = hidden_in[step].astype(jnp.float32)
        inverse = lax.rsqrt(lax.optimization_barrier(jnp.mean(inputs * inputs, axis=-1, keepdims=True)) + norm_eps)
        normed = (inputs * inverse * norm_gain).astype(jnp.bfloat16)
        positions = jnp.repeat(lengths + GEN0 + step, BEAMS).astype(jnp.int32)
        queries = jnp.dot(normed, w_query, preferred_element_type=jnp.float32).reshape(beam_rows, QH, HD)
        queries = rotate(queries, positions).astype(jnp.bfloat16).reshape(requests, BEAMS, KVH, q_group, HD)
        new_k = jnp.dot(normed, w_key, preferred_element_type=jnp.float32).reshape(beam_rows, KVH, HD)
        new_k = rotate(new_k, positions).astype(jnp.bfloat16).reshape(requests, BEAMS, KVH, HD)
        new_v = jnp.dot(normed, w_value, preferred_element_type=jnp.float32).astype(jnp.bfloat16).reshape(requests, BEAMS, KVH, HD)
        chosen = parents[step].reshape(requests, BEAMS)
        cache_k = jnp.concatenate([choose(cache_k, chosen), new_k[:, :, None]], axis=2)
        cache_v = jnp.concatenate([choose(cache_v, chosen), new_v[:, :, None]], axis=2)
        query_f = queries.astype(jnp.float32)
        prompt_scores = jnp.einsum('rbkgd,rpkd->rbkgp', query_f, prompt_k) * scaling
        prompt_scores = jnp.where(usable[:, None, None, None, :], prompt_scores, masked_score)
        cache_scores = jnp.einsum('rbkgd,rbtkd->rbkgt', query_f, cache_k.astype(jnp.float32)) * scaling
        weights = jax.nn.softmax(jnp.concatenate([prompt_scores, cache_scores], axis=-1), axis=-1)
        weights = lax.optimization_barrier(weights.astype(jnp.bfloat16)).astype(jnp.float32)
        context = jnp.einsum('rbkgp,rpkd->rbkgd', weights[..., :2 * HALF], prompt_v)
        context = context + jnp.einsum('rbkgt,rbtkd->rbkgd', weights[..., 2 * HALF:], cache_v.astype(jnp.float32))
        context = context.astype(jnp.bfloat16).reshape(beam_rows, QH * HD)
        results.append(jnp.dot(context, w_out, preferred_element_type=jnp.float32).astype(jnp.bfloat16))
    return jnp.stack(results)
```

```python
import functools
import math

import jax
import jax.numpy as jnp
from jax import lax
from jax.experimental import pallas as pl
from jax.experimental.pallas import tpu as pltpu
from jax.sharding import PartitionSpec as P

HD = 128
BEAMS = 8

norm_eps = 1e-05
masked_score = -1e30
rope_base = 500000.0


def permute_by(value, axis, distance):
    pairs = [(source, source ^ distance) for source in range(lax.axis_size(axis))]
    return lax.ppermute(value, axis, pairs)


def across(value, beam_distance, tp_distance):
    req, tp = lax.axis_size("req"), lax.axis_size("tp")
    pairs = [
        (r * tp + t, (r ^ beam_distance) * tp + (t ^ tp_distance))
        for r in range(req)
        for t in range(tp)
    ]
    return lax.ppermute(value, ("req", "tp"), pairs)


def attend_kernel(
    sizes, lengths_ref, parents_ref, gain_ref, inverse_ref, *refs
):
    steps, own, tp, kv, group, half_len, history = sizes
    pieces = refs[: 2 * tp]
    (wq, wk, wv, pk, pv, gk, gv, kept_ref, kept_lse_ref, sent_ref) = refs[2 * tp : 2 * tp + 10]
    (x_s, xn_s, w_s, pk_s, pv_s, gk_s, gv_s, q_s, k_s, v_s, sems) = refs[2 * tp + 10 :]
    rows = steps * own
    part = pieces[0].shape[-1]
    qw = group * HD
    device = lax.axis_index("req")
    request = device // 2
    parity = device % 2
    me_tp = lax.axis_index("tp")

    copies = []
    for g in range(kv):
        copies.append(
            [
                pltpu.make_async_copy(
                    wq.at[:, pl.ds(g * qw, qw)], w_s.at[g, :, pl.ds(0, qw)], sems.at[3 * g]
                ),
                pltpu.make_async_copy(
                    wk.at[:, pl.ds(g * HD, HD)], w_s.at[g, :, pl.ds(qw, HD)], sems.at[3 * g + 1]
                ),
                pltpu.make_async_copy(
                    wv.at[:, pl.ds(g * HD, HD)],
                    w_s.at[g, :, pl.ds(qw + HD, HD)],
                    sems.at[3 * g + 2],
                ),
            ]
        )
    cache_copies = [
        pltpu.make_async_copy(source, target, sems.at[3 * kv + n])
        for n, (source, target) in enumerate(((pk, pk_s), (pv, pv_s), (gk, gk_s), (gv, gv_s)))
    ]
    for group_copies in copies:
        for copy in group_copies:
            copy.start()
    for copy in cache_copies:
        copy.start()

    squares = []
    for b in range(2):
        total = jnp.zeros((rows, HD), jnp.float32)
        for t in range(tp):
            block = me_tp ^ t
            column = pl.multiple_of(block * part, HD)
            for s in range(steps):
                x_s[pl.ds(b * rows + s * own, own), pl.ds(column, part)] = pieces[b * tp + t][
                    s
                ].astype(jnp.float32)
            mine = x_s[pl.ds(b * rows, rows), pl.ds(column, part)]
            mine = mine * mine
            for c in range(part // HD):
                total = total + mine[:, c * HD : (c + 1) * HD]
        squares.append(jnp.sum(total, axis=-1, keepdims=True))
    width = part * tp
    scale = lax.rsqrt(jnp.concatenate(squares, axis=0) / width + norm_eps)
    xn_s[...] = (x_s[...] * scale * gain_ref[...]).astype(jnp.bfloat16)

    length = lengths_ref[request]
    row = lax.broadcasted_iota(jnp.int32, (2 * rows, HD), 0)
    step = (row % rows) // own
    angle = (length + history + step).astype(jnp.float32) * inverse_ref[...]
    lane = lax.broadcasted_iota(jnp.int32, (2 * rows, HD), 1)
    cosine = jnp.cos(angle)
    sine = jnp.where(lane < HD // 2, -jnp.sin(angle), jnp.sin(angle))

    def rotate(x):
        return x * cosine + pltpu.roll(x, HD // 2, 1) * sine

    count = group * 2 * rows

    def parent_of(s, beam):
        out = jnp.zeros_like(beam)
        for j in range(BEAMS):
            out = jnp.where(beam == j, parents_ref[s, request * BEAMS + j], out)
        return out

    row = lax.broadcasted_iota(jnp.int32, (count, HD), 0) % (2 * rows)
    row_step = (row % rows) // own
    row_parity = jnp.where(row < rows, parity, 1 - parity)
    beam = row_parity * own + row % own
    ancestors = [None] * steps
    at = beam
    for s in reversed(range(steps)):
        if s < steps - 1:
            at = jnp.where(row_step > s, parent_of(s + 1, at), beam)
        ancestors[s] = jnp.where(row_step >= s, at, -1)
    origin = parent_of(0, at)
    lane = lax.broadcasted_iota(jnp.int32, (count, HD), 1)

    zero = jnp.zeros((count, HD), jnp.float32)
    gen_bias = []
    per = HD // history if history < HD else 1
    for c in range(own * history // HD):
        key_beam = parity * own + (c * HD + lane) // history
        gen_bias.append(jnp.where(key_beam == origin, zero, masked_score))
    gen_bias = jnp.concatenate(gen_bias, axis=1)
    new_bias = zero + masked_score
    for s in range(steps):
        hit = (lane // own == s) & (ancestors[s] == parity * own + lane % own)
        new_bias = jnp.where(hit, 0.0, new_bias)
    new_bias = new_bias[:, :rows]
    place = parity * half_len + lax.broadcasted_iota(jnp.int32, (1, half_len), 1)
    prompt_bias = jnp.where(place < length, 0.0, masked_score)

    for g in range(kv):
        for copy in copies[g]:
            copy.wait()
        out = jnp.dot(xn_s[...], w_s[g], preferred_element_type=jnp.float32)
        for j in range(group):
            q_s[g, pl.ds(j * 2 * rows, 2 * rows), :] = rotate(
                out[:, j * HD : (j + 1) * HD]
            ).astype(jnp.bfloat16)
        k_s[g] = rotate(out[:, qw : qw + HD]).astype(jnp.bfloat16)
        v_s[g] = out[:, qw + HD :].astype(jnp.bfloat16)
    for copy in cache_copies:
        copy.wait()

    scaling = HD**-0.5
    contract = (((1,), (1,)), ((), ()))
    lse_lane = lax.broadcasted_iota(jnp.int32, (rows, HD), 1)
    kept_lse = jnp.zeros((rows, HD), jnp.float32)
    sent_lse = jnp.zeros((rows, HD), jnp.float32)
    for g in range(kv):
        cols = pl.ds(g * HD, HD)
        q = q_s[g]
        s_prompt = (
            lax.dot_general(q, pk_s[0, :, cols], contract, preferred_element_type=jnp.float32)
            * scaling
            + prompt_bias
        )
        s_gen = (
            lax.dot_general(
                q,
                gk_s[:, :, cols].reshape(own * history, HD),
                contract,
                preferred_element_type=jnp.float32,
            )
            * scaling
            + gen_bias
        )
        s_new = (
            lax.dot_general(
                q, k_s[g, pl.ds(0, rows), :], contract, preferred_element_type=jnp.float32
            )
            * scaling
            + new_bias
        )
        top = jnp.maximum(
            jnp.maximum(
                jnp.max(s_prompt, axis=-1, keepdims=True), jnp.max(s_gen, axis=-1, keepdims=True)
            ),
            jnp.max(s_new, axis=-1, keepdims=True),
        )
        e_prompt = jnp.exp(s_prompt - top)
        e_gen = jnp.exp(s_gen - top)
        e_new = jnp.exp(s_new - top)
        total = (
            jnp.sum(e_prompt, axis=-1, keepdims=True)
            + jnp.sum(e_gen, axis=-1, keepdims=True)
            + jnp.sum(e_new, axis=-1, keepdims=True)
        )
        mixed = (
            jnp.dot(
                e_prompt.astype(jnp.bfloat16),
                pv_s[0, :, cols],
                preferred_element_type=jnp.float32,
            )
            + jnp.dot(
                e_gen.astype(jnp.bfloat16),
                gv_s[:, :, cols].reshape(own * history, HD),
                preferred_element_type=jnp.float32,
            )
            + jnp.dot(
                e_new.astype(jnp.bfloat16),
                v_s[g, pl.ds(0, rows), :],
                preferred_element_type=jnp.float32,
            )
        )
        mixed = mixed / total
        lse = top + jnp.log(total)
        for j in range(group):
            h = g * group + j
            lower = j * 2 * rows
            kept_ref[:, pl.ds(h * HD, HD)] = mixed[lower : lower + rows]
            sent_ref[:, pl.ds(h * HD, HD)] = mixed[lower + rows : lower + 2 * rows].astype(
                jnp.bfloat16
            )
            kept_lse = jnp.where(lse_lane == h, lse[lower : lower + rows], kept_lse)
            sent_lse = jnp.where(lse_lane == h, lse[lower + rows : lower + 2 * rows], sent_lse)
    kept_lse_ref[...] = kept_lse
    base = kv * group * HD
    rest = sent_lse
    for n in range(3):
        term = rest.astype(jnp.bfloat16)
        sent_ref[:, pl.ds(base + n * HD, HD)] = term
        rest = rest - term.astype(jnp.float32)


def project_kernel(sizes, kept_ref, kept_lse_ref, got_ref, w_out, *refs):
    steps, own, tp, heads, chunk = sizes
    outs = refs[:tp]
    w_s, ctx_s, sems = refs[tp:]
    me_tp = lax.axis_index("tp")
    part = outs[0].shape[-1]
    per = part // chunk
    copies = []
    for d in list(range(1, tp)) + [0]:
        for c in range(per):
            column = pl.multiple_of((me_tp ^ d) * part + c * chunk, HD)
            slot = d * per + c
            copies.append(
                (
                    d,
                    c,
                    slot,
                    pltpu.make_async_copy(
                        w_out.at[:, pl.ds(column, chunk)], w_s.at[slot], sems.at[slot]
                    ),
                )
            )
    for _, _, _, copy in copies:
        copy.start()
    base = heads * HD
    lse_mine = kept_lse_ref[...]
    lse_got = (
        got_ref[:, pl.ds(base, HD)].astype(jnp.float32)
        + got_ref[:, pl.ds(base + HD, HD)].astype(jnp.float32)
        + got_ref[:, pl.ds(base + 2 * HD, HD)].astype(jnp.float32)
    )
    top = jnp.maximum(lse_mine, lse_got)
    mine = jnp.exp(lse_mine - top)
    got = jnp.exp(lse_got - top)
    share = mine / (mine + got)
    for h in range(heads):
        cols = pl.ds(h * HD, HD)
        w = share[:, h : h + 1]
        ctx_s[:, cols] = (
            kept_ref[:, cols] * w + got_ref[:, cols].astype(jnp.float32) * (1.0 - w)
        ).astype(jnp.bfloat16)
    for d, c, slot, copy in copies:
        copy.wait()
        out = jnp.dot(ctx_s[...], w_s[slot], preferred_element_type=jnp.float32)
        for s in range(steps):
            outs[d][s, :, pl.ds(c * chunk, chunk)] = out[s * own : (s + 1) * own].astype(
                outs[d].dtype
            )


def body(
    hidden_in,
    norm_gain,
    w_query,
    w_key,
    w_value,
    w_out,
    prompt_keys,
    prompt_values,
    gen_keys,
    gen_values,
    lengths,
    parents,
):
    steps, own, part = hidden_in.shape
    tp = lax.axis_size("tp")
    rows = steps * own
    width = w_query.shape[0]
    kv = w_key.shape[1] // HD
    group = w_query.shape[1] // w_key.shape[1]
    heads = kv * group
    half_len = prompt_keys.shape[1]
    history = gen_keys.shape[1]

    pieces = [
        hidden_in if (b, t) == (0, 0) else across(hidden_in, b, t)
        for b in range(2)
        for t in range(tp)
    ]
    half_dim = HD // 2
    inverse = rope_base ** (-jnp.arange(half_dim, dtype=jnp.float32) / half_dim)
    inverse = jnp.concatenate([inverse, inverse])[None, :]

    smem = pl.BlockSpec(memory_space=pltpu.SMEM)
    vmem = pl.BlockSpec(memory_space=pltpu.VMEM)
    hbm = pl.BlockSpec(memory_space=pl.ANY)
    sizes = (steps, own, tp, kv, group, half_len, history)
    kept, kept_lse, sent = pl.pallas_call(
        functools.partial(attend_kernel, sizes),
        out_shape=(
            jax.ShapeDtypeStruct((rows, heads * HD), jnp.float32),
            jax.ShapeDtypeStruct((rows, HD), jnp.float32),
            jax.ShapeDtypeStruct((rows, heads * HD + 3 * HD), jnp.bfloat16),
        ),
        in_specs=[smem, smem, vmem, vmem] + [vmem] * (2 * tp) + [hbm] * 7,
        out_specs=(vmem, vmem, vmem),
        scratch_shapes=[
            pltpu.VMEM((2 * rows, width), jnp.float32),
            pltpu.VMEM((2 * rows, width), jnp.bfloat16),
            pltpu.VMEM((kv, width, (group + 2) * HD), jnp.bfloat16),
            pltpu.VMEM(prompt_keys.shape, jnp.bfloat16),
            pltpu.VMEM(prompt_values.shape, jnp.bfloat16),
            pltpu.VMEM(gen_keys.shape, jnp.bfloat16),
            pltpu.VMEM(gen_values.shape, jnp.bfloat16),
            pltpu.VMEM((kv, group * 2 * rows, HD), jnp.bfloat16),
            pltpu.VMEM((kv, 2 * rows, HD), jnp.bfloat16),
            pltpu.VMEM((kv, 2 * rows, HD), jnp.bfloat16),
            pltpu.SemaphoreType.DMA((3 * kv + 4,)),
        ],
        compiler_params=pltpu.CompilerParams(vmem_limit_bytes=40 * 2**20),
        name="attend",
    )(
        lengths,
        parents,
        norm_gain[None, :],
        inverse,
        *pieces,
        w_query,
        w_key,
        w_value,
        prompt_keys,
        prompt_values,
        gen_keys,
        gen_values,
    )

    got = permute_by(sent, "req", 1)

    chunk = math.gcd(part, 512)
    out_types = [jnp.float32] + [jnp.bfloat16] * (tp - 1)
    sums = pl.pallas_call(
        functools.partial(project_kernel, (steps, own, tp, heads, chunk)),
        out_shape=tuple(jax.ShapeDtypeStruct((steps, own, part), kind) for kind in out_types),
        in_specs=[vmem, vmem, vmem, hbm],
        out_specs=(vmem,) * tp,
        scratch_shapes=[
            pltpu.VMEM((width // chunk, heads * HD, chunk), jnp.bfloat16),
            pltpu.VMEM((rows, heads * HD), jnp.bfloat16),
            pltpu.SemaphoreType.DMA((width // chunk,)),
        ],
        compiler_params=pltpu.CompilerParams(vmem_limit_bytes=40 * 2**20),
        name="project",
    )(kept, kept_lse, got, w_out)
    total = sums[0]
    for t in range(1, tp):
        total = total + across(sums[t], 0, t).astype(jnp.float32)
    return total.astype(jnp.bfloat16)


def solution(mesh):
    in_specs = (
        P(None, "req", "tp"),
        P(),
        P(None, "tp"),
        P(None, "tp"),
        P(None, "tp"),
        P("tp", None),
        P("req", None, "tp"),
        P("req", None, "tp"),
        P("req", None, "tp"),
        P("req", None, "tp"),
        P(),
        P(),
    )
    out_specs = P(None, "req", "tp")
    return jax.shard_map(body, mesh=mesh, in_specs=in_specs, out_specs=out_specs, check_vma=False)
```

```python
import functools
import math

import jax
import jax.numpy as jnp
from jax import lax
from jax.experimental import pallas as pl
from jax.experimental.pallas import tpu as pltpu
from jax.sharding import PartitionSpec as P

HD = 128
BEAMS = 8

norm_eps = 1e-05
masked_score = -1e30
rope_base = 500000.0


def permute_by(value, axis, distance):
    pairs = [(source, source ^ distance) for source in range(lax.axis_size(axis))]
    return lax.ppermute(value, axis, pairs)


def across(value, beam_distance, tp_distance):
    req, tp = lax.axis_size("req"), lax.axis_size("tp")
    pairs = [
        (r * tp + t, (r ^ beam_distance) * tp + (t ^ tp_distance))
        for r in range(req)
        for t in range(tp)
    ]
    return lax.ppermute(value, ("req", "tp"), pairs)


def load_kernel(
    sizes,
    lengths,
    parents,
    gain,
    hidden,
    wq,
    wk,
    wv,
    pk,
    pv,
    gk,
    gv,
    gain_ref,
    x_ref,
    wq_ref,
    wk_ref,
    wv_ref,
    pk_ref,
    pv_ref,
    gk_ref,
    gv_ref,
    cosine_ref,
    sine_ref,
    prompt_bias_ref,
    gen_bias_ref,
    new_bias_ref,
    lengths_s,
    parents_s,
    hidden_s,
    sems,
):
    steps, own, group, half_len, history = sizes
    rows = steps * own
    device = lax.axis_index("req")
    request = device // 2
    parity = device % 2

    small = [
        pltpu.make_async_copy(source, target, sems.at[n])
        for n, (source, target) in enumerate(
            ((lengths, lengths_s), (parents, parents_s), (gain, gain_ref), (hidden, hidden_s))
        )
    ]
    large = []
    for source, target, parts in (
        (wq, wq_ref, 4),
        (wk, wk_ref, 2),
        (wv, wv_ref, 2),
    ):
        size = source.shape[0] // parts
        for n in range(parts):
            place = pl.ds(n * size, size)
            large.append((source.at[place], target.at[place]))
    large += [(pk, pk_ref), (pv, pv_ref), (gk, gk_ref), (gv, gv_ref)]
    large = [
        pltpu.make_async_copy(source, target, sems.at[len(small) + n])
        for n, (source, target) in enumerate(large)
    ]
    for copy in small + large:
        copy.start()
    for copy in small:
        copy.wait()

    for s in range(steps):
        x_ref[pl.ds(s * own, own), :] = hidden_s[s].astype(jnp.float32)

    length = lengths_s[request]
    row = lax.broadcasted_iota(jnp.int32, (2 * rows, HD), 0)
    lane = lax.broadcasted_iota(jnp.int32, (2 * rows, HD), 1)
    half_dim = HD // 2
    inverse = jnp.exp((lane % half_dim).astype(jnp.float32) * (-math.log(rope_base) / half_dim))
    step = (row % rows) // own
    angle = (length + history + step).astype(jnp.float32) * inverse
    sine = jnp.sin(angle)
    cosine_ref[...] = jnp.cos(angle)
    sine_ref[...] = jnp.where(lane < half_dim, -sine, sine)

    count = group * 2 * rows

    def parent_of(s, beam):
        out = jnp.zeros_like(beam)
        for j in range(BEAMS):
            out = jnp.where(beam == j, parents_s[s, request * BEAMS + j], out)
        return out

    row = lax.broadcasted_iota(jnp.int32, (count, HD), 0) % (2 * rows)
    row_step = (row % rows) // own
    row_parity = jnp.where(row < rows, parity, 1 - parity)
    beam = row_parity * own + row % own
    ancestors = [None] * steps
    at = beam
    for s in reversed(range(steps)):
        if s < steps - 1:
            at = jnp.where(row_step > s, parent_of(s + 1, at), beam)
        ancestors[s] = jnp.where(row_step >= s, at, -1)
    origin = parent_of(0, at)
    lane = lax.broadcasted_iota(jnp.int32, (count, HD), 1)

    for c in range(own * history // HD):
        key_beam = parity * own + (c * HD + lane) // history
        gen_bias_ref[:, pl.ds(c * HD, HD)] = jnp.where(key_beam == origin, 0.0, masked_score)
    new_bias = jnp.full((count, HD), masked_score, jnp.float32)
    for s in range(steps):
        hit = (lane // own == s) & (ancestors[s] == parity * own + lane % own)
        new_bias = jnp.where(hit, 0.0, new_bias)
    new_bias_ref[...] = new_bias
    place = parity * half_len + lax.broadcasted_iota(jnp.int32, prompt_bias_ref.shape, 1)
    prompt_bias_ref[...] = jnp.where(place < length, 0.0, masked_score)
    for copy in large:
        copy.wait()


def attend_kernel(
    sizes,
    gain_ref,
    x_ref,
    wq_ref,
    wk_ref,
    wv_ref,
    pk_ref,
    pv_ref,
    gk_ref,
    gv_ref,
    cosine_ref,
    sine_ref,
    prompt_bias_ref,
    gen_bias_ref,
    new_bias_ref,
    w_out,
    *refs,
):
    steps, own, tp, kv, group, history = sizes
    pieces = (None,) + refs[: 2 * tp - 1]
    kept_ref, kept_lse_ref, sent_ref, w_out_ref, x_s, xn_s, sems = refs[2 * tp - 1 :]
    rows = steps * own
    part = x_ref.shape[-1]
    width = part * tp
    heads = kv * group
    me_tp = lax.axis_index("tp")

    copies = [
        pltpu.make_async_copy(
            w_out.at[:, pl.ds(pl.multiple_of((me_tp ^ d) * part, HD), part)],
            w_out_ref.at[d],
            sems.at[d],
        )
        for d in range(tp)
    ]
    for copy in copies:
        copy.start()

    squares = []
    for b in range(2):
        total = jnp.zeros((rows, HD), jnp.float32)
        for t in range(tp):
            column = pl.multiple_of((me_tp ^ t) * part, HD)
            if (b, t) == (0, 0):
                mine = x_ref[...]
            else:
                for s in range(steps):
                    x_s[b * tp + t, pl.ds(s * own, own), :] = pieces[b * tp + t][s].astype(
                        jnp.float32
                    )
                mine = x_s[b * tp + t]
            xn_s[pl.ds(b * rows, rows), pl.ds(column, part)] = (
                mine * gain_ref[:, pl.ds(column, part)]
            ).astype(jnp.bfloat16)
            mine = mine * mine
            for c in range(part // HD):
                total = total + mine[:, c * HD : (c + 1) * HD]
        squares.append(jnp.sum(total, axis=-1, keepdims=True))
    scale = lax.rsqrt(jnp.concatenate(squares, axis=0) / width + norm_eps)
    cosine = cosine_ref[...] * scale
    sine = sine_ref[...] * scale

    def rotate(x):
        return x * cosine + pltpu.roll(x, HD // 2, 1) * sine

    def project(w_ref, lower, size):
        return jnp.dot(
            xn_s[...], w_ref[:, pl.ds(lower, size)], preferred_element_type=jnp.float32
        )

    def heads_of(w_ref, finish):
        size = math.gcd(w_ref.shape[1], 2 * HD)
        out = []
        for lower in range(0, w_ref.shape[1], size):
            block = project(w_ref, lower, size)
            for c in range(size // HD):
                out.append(finish(block[:, c * HD : (c + 1) * HD]).astype(jnp.bfloat16))
        return out

    queries = heads_of(wq_ref, rotate)
    new_keys = heads_of(wk_ref, rotate)
    new_values = heads_of(wv_ref, lambda x: x * scale)

    scaling = HD**-0.5
    contract = (((1,), (1,)), ((), ()))
    lane = lax.broadcasted_iota(jnp.int32, (rows, HD), 1)
    kept_lse = jnp.zeros((rows, HD), jnp.float32)
    sent_lse = jnp.zeros((rows, HD), jnp.float32)
    for g in range(kv):
        cols = pl.ds(g * HD, HD)
        q = jnp.concatenate(queries[g * group : (g + 1) * group], axis=0)
        keys = (
            pk_ref[0, :, cols],
            gk_ref[:, :, cols].reshape(own * history, HD),
            new_keys[g][:rows],
        )
        values = (
            pv_ref[0, :, cols],
            gv_ref[:, :, cols].reshape(own * history, HD),
            new_values[g][:rows],
        )
        biases = (prompt_bias_ref[...], gen_bias_ref[...], new_bias_ref[:, pl.ds(0, rows)])
        scores = [
            lax.dot_general(q, k, contract, preferred_element_type=jnp.float32) * scaling + bias
            for k, bias in zip(keys, biases)
        ]
        top = functools.reduce(
            jnp.maximum, [jnp.max(x, axis=-1, keepdims=True) for x in scores]
        )
        powers = [jnp.exp(x - top) for x in scores]
        total = sum(jnp.sum(x, axis=-1, keepdims=True) for x in powers)
        mixed = sum(
            jnp.dot(x.astype(jnp.bfloat16), v, preferred_element_type=jnp.float32)
            for x, v in zip(powers, values)
        )
        mixed = mixed / total
        lse = top + jnp.log(total)
        for j in range(group):
            h = g * group + j
            lower = j * 2 * rows
            kept_ref[:, pl.ds(h * HD, HD)] = mixed[lower : lower + rows]
            sent_ref[:, pl.ds(h * HD, HD)] = mixed[lower + rows : lower + 2 * rows].astype(
                jnp.bfloat16
            )
            kept_lse = jnp.where(lane == h, lse[lower : lower + rows], kept_lse)
            sent_lse = jnp.where(lane % heads == h, lse[lower + rows : lower + 2 * rows], sent_lse)
    kept_lse_ref[...] = kept_lse
    terms = jnp.zeros((rows, HD), jnp.float32)
    rest = sent_lse
    for n in range(3):
        term = rest.astype(jnp.bfloat16).astype(jnp.float32)
        terms = jnp.where(lane // heads == n, term, terms)
        rest = rest - term
    sent_ref[:, pl.ds(heads * HD, HD)] = terms.astype(jnp.bfloat16)
    for copy in copies:
        copy.wait()


def project_kernel(sizes, kept_ref, kept_lse_ref, got_ref, w_out_ref, *refs):
    steps, own, tp, heads, chunk = sizes
    outs = refs[:tp]
    (ctx_s,) = refs[tp:]
    part = outs[0].shape[-1]
    base = heads * HD
    lse_mine = kept_lse_ref[...]
    terms = got_ref[:, pl.ds(base, HD)].astype(jnp.float32)
    lse_got = terms + pltpu.roll(terms, HD - heads, 1) + pltpu.roll(terms, HD - 2 * heads, 1)
    top = jnp.maximum(lse_mine, lse_got)
    mine = jnp.exp(lse_mine - top)
    got = jnp.exp(lse_got - top)
    share = mine / (mine + got)
    for h in range(heads):
        cols = pl.ds(h * HD, HD)
        w = share[:, h : h + 1]
        ctx_s[:, cols] = (
            kept_ref[:, cols] * w + got_ref[:, cols].astype(jnp.float32) * (1.0 - w)
        ).astype(jnp.bfloat16)
    for d in list(range(1, tp)) + [0]:
        for lower in range(0, part, chunk):
            cols = pl.ds(lower, chunk)
            out = jnp.dot(ctx_s[...], w_out_ref[d, :, cols], preferred_element_type=jnp.float32)
            for s in range(steps):
                outs[d][s, :, cols] = out[s * own : (s + 1) * own].astype(outs[d].dtype)


def body(
    hidden_in,
    norm_gain,
    w_query,
    w_key,
    w_value,
    w_out,
    prompt_keys,
    prompt_values,
    gen_keys,
    gen_values,
    lengths,
    parents,
):
    steps, own, part = hidden_in.shape
    tp = lax.axis_size("tp")
    rows = steps * own
    width = w_query.shape[0]
    kv = w_key.shape[1] // HD
    group = w_query.shape[1] // w_key.shape[1]
    heads = kv * group
    half_len = prompt_keys.shape[1]
    history = gen_keys.shape[1]

    pieces = [
        across(hidden_in, b, t) for b in range(2) for t in range(tp) if (b, t) != (0, 0)
    ]

    def in_hbm(x):
        return pltpu.with_memory_space_constraint(x, pltpu.HBM)

    vmem = pl.BlockSpec(memory_space=pltpu.VMEM)
    hbm = pl.BlockSpec(memory_space=pltpu.HBM)
    params = pltpu.CompilerParams(vmem_limit_bytes=16 * 2**20)
    f32, bf16 = jnp.float32, jnp.bfloat16
    big = (w_query, w_key, w_value, prompt_keys, prompt_values, gen_keys, gen_values)
    loaded = pl.pallas_call(
        functools.partial(load_kernel, (steps, own, group, half_len, history)),
        out_shape=(
            jax.ShapeDtypeStruct((1, width), f32),
            jax.ShapeDtypeStruct((rows, part), f32),
            *(jax.ShapeDtypeStruct(x.shape, x.dtype) for x in big),
            jax.ShapeDtypeStruct((2 * rows, HD), f32),
            jax.ShapeDtypeStruct((2 * rows, HD), f32),
            jax.ShapeDtypeStruct((1, half_len), f32),
            jax.ShapeDtypeStruct((group * 2 * rows, own * history), f32),
            jax.ShapeDtypeStruct((group * 2 * rows, HD), f32),
        ),
        in_specs=[hbm] * 11,
        out_specs=(vmem,) * 14,
        scratch_shapes=[
            pltpu.SMEM(lengths.shape, jnp.int32),
            pltpu.SMEM(parents.shape, jnp.int32),
            pltpu.VMEM(hidden_in.shape, bf16),
            pltpu.SemaphoreType.DMA((16,)),
        ],
        compiler_params=params,
        name="load",
    )(*(in_hbm(x) for x in (lengths, parents, norm_gain[None, :], hidden_in, *big)))

    kept, kept_lse, sent, w_out_near = pl.pallas_call(
        functools.partial(attend_kernel, (steps, own, tp, kv, group, history)),
        out_shape=(
            jax.ShapeDtypeStruct((rows, heads * HD), f32),
            jax.ShapeDtypeStruct((rows, HD), f32),
            jax.ShapeDtypeStruct((rows, heads * HD + HD), bf16),
            jax.ShapeDtypeStruct((tp, heads * HD, part), bf16),
        ),
        in_specs=[vmem] * 14 + [hbm] + [vmem] * (2 * tp - 1),
        out_specs=(vmem,) * 4,
        scratch_shapes=[
            pltpu.VMEM((2 * tp, rows, part), f32),
            pltpu.VMEM((2 * rows, width), bf16),
            pltpu.SemaphoreType.DMA((tp,)),
        ],
        compiler_params=params,
        name="attend",
    )(*loaded, in_hbm(w_out), *pieces)

    got = permute_by(sent, "req", 1)

    out_types = [f32] + [bf16] * (tp - 1)
    sums = pl.pallas_call(
        functools.partial(project_kernel, (steps, own, tp, heads, math.gcd(part, 512))),
        out_shape=tuple(jax.ShapeDtypeStruct((steps, own, part), kind) for kind in out_types),
        in_specs=[vmem] * 4,
        out_specs=(vmem,) * tp,
        scratch_shapes=[pltpu.VMEM((rows, heads * HD), bf16)],
        compiler_params=params,
        name="project",
    )(kept, kept_lse, got, w_out_near)
    total = sums[0]
    for t in range(1, tp):
        total = total + across(sums[t], 0, t).astype(f32)
    return total.astype(bf16)


def solution(mesh):
    in_specs = (
        P(None, "req", "tp"),
        P(),
        P(None, "tp"),
        P(None, "tp"),
        P(None, "tp"),
        P("tp", None),
        P("req", None, "tp"),
        P("req", None, "tp"),
        P("req", None, "tp"),
        P("req", None, "tp"),
        P(),
        P(),
    )
    out_specs = P(None, "req", "tp")
    return jax.shard_map(body, mesh=mesh, in_specs=in_specs, out_specs=out_specs, check_vma=False)
```

```python
import functools
import math

import jax
import jax.numpy as jnp
from jax import lax
from jax.experimental import pallas as pl
from jax.experimental.pallas import tpu as pltpu
from jax.sharding import PartitionSpec as P

HD = 128
BEAMS = 8

norm_eps = 1e-05
masked_score = -1e30
rope_base = 500000.0


def permute_by(value, axis, distance):
    pairs = [(source, source ^ distance) for source in range(lax.axis_size(axis))]
    return lax.ppermute(value, axis, pairs)


def across(value, beam_distance, tp_distance):
    req, tp = lax.axis_size("req"), lax.axis_size("tp")
    pairs = [
        (r * tp + t, (r ^ beam_distance) * tp + (t ^ tp_distance))
        for r in range(req)
        for t in range(tp)
    ]
    return lax.ppermute(value, ("req", "tp"), pairs)


def load_kernel(
    sizes,
    lengths,
    parents,
    gain,
    hidden,
    wq,
    wk,
    pk,
    pv,
    gk,
    gv,
    gain_ref,
    x_ref,
    wq_ref,
    wk_ref,
    keys_ref,
    values_ref,
    cosine_ref,
    sine_ref,
    bias_ref,
    lengths_s,
    parents_s,
    hidden_s,
    sems,
):
    steps, own, kv, group, history = sizes
    rows = steps * own
    blocks = pk.shape[0]
    half_len = blocks * history
    device = lax.axis_index("req")
    request = device // 2
    parity = device % 2

    small = [
        (lengths, lengths_s),
        (parents, parents_s),
        (gain, gain_ref),
        (hidden, hidden_s),
    ]
    large = []
    for g in range(kv):
        cols = pl.ds(g * HD, HD)
        for prompt, gen, target in ((pk, gk, keys_ref), (pv, gv, values_ref)):
            large.append((prompt.at[:, :, cols], target.at[g, pl.ds(0, blocks), :, pl.ds(0, HD)]))
            large.append((gen.at[:, :, cols], target.at[g, pl.ds(blocks, own), :, pl.ds(0, HD)]))
    for source, target, parts in ((wk, wk_ref, 4), (wq, wq_ref, 8)):
        size = source.shape[0] // parts
        for n in range(parts):
            place = pl.ds(n * size, size)
            large.append((source.at[place], target.at[place]))
    copies = [
        pltpu.make_async_copy(source, target, sems.at[n])
        for n, (source, target) in enumerate(small + large)
    ]
    for copy in copies:
        copy.start()
    for g in range(kv):
        values_ref[g, :, :, pl.ds(HD, HD)] = jnp.ones((blocks + own, history, HD), jnp.bfloat16)
    for copy in copies[: len(small)]:
        copy.wait()

    for s in range(steps):
        x_ref[pl.ds(s * own, own), :] = hidden_s[s].astype(jnp.float32)

    length = lengths_s[request]
    row = lax.broadcasted_iota(jnp.int32, (2 * rows, HD), 0)
    lane = lax.broadcasted_iota(jnp.int32, (2 * rows, HD), 1)
    half_dim = HD // 2
    inverse = jnp.exp((lane % half_dim).astype(jnp.float32) * (-math.log(rope_base) / half_dim))
    step = (row % rows) // own
    angle = (length + history + step).astype(jnp.float32) * inverse
    sine = jnp.sin(angle)
    cosine_ref[...] = jnp.cos(angle)
    sine_ref[...] = jnp.where(lane < half_dim, -sine, sine)

    count = group * 2 * rows

    def parent_of(s, beam):
        out = jnp.zeros_like(beam)
        for j in range(BEAMS):
            out = jnp.where(beam == j, parents_s[s, request * BEAMS + j], out)
        return out

    row = lax.broadcasted_iota(jnp.int32, (count, HD), 0) % (2 * rows)
    row_step = (row % rows) // own
    row_parity = jnp.where(row < rows, parity, 1 - parity)
    beam = row_parity * own + row % own
    ancestors = [None] * steps
    at = beam
    for s in reversed(range(steps)):
        if s < steps - 1:
            at = jnp.where(row_step > s, parent_of(s + 1, at), beam)
        ancestors[s] = jnp.where(row_step >= s, at, -1)
    origin = parent_of(0, at)
    lane = lax.broadcasted_iota(jnp.int32, (count, HD), 1)

    for c in range(half_len // HD):
        place = parity * half_len + c * HD + lane
        bias_ref[:, pl.ds(c * HD, HD)] = jnp.where(place < length, 0.0, masked_score)
    for c in range(own * history // HD):
        key_beam = parity * own + (c * HD + lane) // history
        bias_ref[:, pl.ds(half_len + c * HD, HD)] = jnp.where(
            key_beam == origin, 0.0, masked_score
        )
    new_bias = jnp.full((count, HD), masked_score, jnp.float32)
    for s in range(steps):
        hit = (lane // own == s) & (ancestors[s] == parity * own + lane % own)
        new_bias = jnp.where(hit, 0.0, new_bias)
    bias_ref[:, pl.ds(half_len + own * history, HD)] = new_bias
    for copy in copies[len(small) :]:
        copy.wait()


def attend_kernel(
    sizes,
    gain_ref,
    x_ref,
    wq_ref,
    wk_ref,
    keys_ref,
    values_ref,
    cosine_ref,
    sine_ref,
    bias_ref,
    wv,
    w_out,
    *refs,
):
    steps, own, tp, kv, group = sizes
    pieces = (None,) + refs[: 2 * tp - 1]
    kept_ref, kept_lse_ref, sent_ref, w_out_ref, x_s, xn_s, wv_s, sems = refs[2 * tp - 1 :]
    rows = steps * own
    part = x_ref.shape[-1]
    width = part * tp
    heads = kv * group
    old = keys_ref.shape[1] * keys_ref.shape[2]
    me_tp = lax.axis_index("tp")

    copies = [pltpu.make_async_copy(wv, wv_s, sems.at[tp])]
    copies += [
        pltpu.make_async_copy(
            w_out.at[:, pl.ds(pl.multiple_of((me_tp ^ d) * part, HD), part)],
            w_out_ref.at[d],
            sems.at[d],
        )
        for d in range(tp)
    ]
    for copy in copies:
        copy.start()

    squares = []
    for b in range(2):
        total = jnp.zeros((rows, HD), jnp.float32)
        for t in range(tp):
            column = pl.multiple_of((me_tp ^ t) * part, HD)
            if (b, t) == (0, 0):
                mine = x_ref[...]
            else:
                for s in range(steps):
                    x_s[b * tp + t, pl.ds(s * own, own), :] = pieces[b * tp + t][s].astype(
                        jnp.float32
                    )
                mine = x_s[b * tp + t]
            xn_s[pl.ds(b * rows, rows), pl.ds(column, part)] = (
                mine * gain_ref[:, pl.ds(column, part)]
            ).astype(jnp.bfloat16)
            mine = mine * mine
            for c in range(part // HD):
                total = total + mine[:, c * HD : (c + 1) * HD]
        squares.append(jnp.sum(total, axis=-1, keepdims=True))
    scale = lax.rsqrt(jnp.concatenate(squares, axis=0) / width + norm_eps)
    key_tables = (cosine_ref[...] * scale, sine_ref[...] * scale)
    query_tables = tuple(x * HD**-0.5 for x in key_tables)

    def rotate(x, tables):
        return (x * tables[0] + pltpu.roll(x, HD // 2, 1) * tables[1]).astype(jnp.bfloat16)

    def project(w_ref, lower, size):
        block = jnp.dot(
            xn_s[...], w_ref[:, pl.ds(lower, size)], preferred_element_type=jnp.float32
        )
        return [block[:, c * HD : (c + 1) * HD] for c in range(size // HD)]

    def project_all(w_ref):
        size = math.gcd(w_ref.shape[1], 2 * HD)
        return [x for c in range(0, w_ref.shape[1], size) for x in project(w_ref, c, size)]

    pad = jnp.zeros((HD - rows, HD), jnp.bfloat16)
    ones = jnp.ones((HD, HD), jnp.bfloat16)
    contract = (((1,), (1,)), ((), ()))
    new_keys = [
        jnp.concatenate([rotate(x, key_tables)[:rows], pad], axis=0) for x in project_all(wk_ref)
    ]

    def score(g):
        q = jnp.concatenate(
            [rotate(x, query_tables) for x in project(wq_ref, g * group * HD, group * HD)], axis=0
        )
        before = lax.dot_general(
            q, keys_ref[g].reshape(old, HD), contract, preferred_element_type=jnp.float32
        )
        now = lax.dot_general(q, new_keys[g], contract, preferred_element_type=jnp.float32)
        return before + bias_ref[:, pl.ds(0, old)], now + bias_ref[:, pl.ds(old, HD)]

    def soften(before, now):
        most = now
        for c in range(old // HD):
            most = jnp.maximum(most, before[:, c * HD : (c + 1) * HD])
        top = jnp.max(most, axis=-1, keepdims=True)
        return (
            jnp.exp(before - top).astype(jnp.bfloat16),
            jnp.exp(now - top).astype(jnp.bfloat16),
            top,
        )

    scores, soft = [], []
    for g in range(kv):
        scores.append(score(g))
        if g > 0:
            soft.append(soften(*scores[g - 1]))
    soft.append(soften(*scores[kv - 1]))

    copies[0].wait()
    new_values = [
        jnp.concatenate([(x * scale).astype(jnp.bfloat16)[:rows], pad], axis=0)
        for x in project_all(wv_s)
    ]
    lane = lax.broadcasted_iota(jnp.int32, (rows, HD), 1)
    kept_lse = jnp.zeros((rows, HD), jnp.float32)
    sent_lse = jnp.zeros((rows, HD), jnp.float32)
    for g in range(kv):
        before, now, top = soft[g]
        mixed = jnp.dot(
            before, values_ref[g].reshape(old, 2 * HD), preferred_element_type=jnp.float32
        ) + jnp.dot(
            now,
            jnp.concatenate([new_values[g], ones], axis=1),
            preferred_element_type=jnp.float32,
        )
        total = mixed[:, HD:]
        mixed = mixed[:, :HD] / total
        lse = top + jnp.log(total)
        for j in range(group):
            h = g * group + j
            lower = j * 2 * rows
            kept_ref[:, pl.ds(h * HD, HD)] = mixed[lower : lower + rows]
            sent_ref[:, pl.ds(h * HD, HD)] = mixed[lower + rows : lower + 2 * rows].astype(
                jnp.bfloat16
            )
            kept_lse = jnp.where(lane == h, lse[lower : lower + rows], kept_lse)
            sent_lse = jnp.where(lane % heads == h, lse[lower + rows : lower + 2 * rows], sent_lse)
    kept_lse_ref[...] = kept_lse
    terms = jnp.zeros((rows, HD), jnp.float32)
    rest = sent_lse
    for n in range(3):
        term = rest.astype(jnp.bfloat16).astype(jnp.float32)
        terms = jnp.where(lane // heads == n, term, terms)
        rest = rest - term
    sent_ref[:, pl.ds(heads * HD, HD)] = terms.astype(jnp.bfloat16)
    for copy in copies[1:]:
        copy.wait()


def project_kernel(sizes, kept_ref, kept_lse_ref, got_ref, w_out_ref, *refs):
    steps, own, tp, heads, chunk = sizes
    outs = refs[:tp]
    (ctx_s,) = refs[tp:]
    part = outs[0].shape[-1]
    base = heads * HD
    lse_mine = kept_lse_ref[...]
    terms = got_ref[:, pl.ds(base, HD)].astype(jnp.float32)
    lse_got = terms + pltpu.roll(terms, HD - heads, 1) + pltpu.roll(terms, HD - 2 * heads, 1)
    top = jnp.maximum(lse_mine, lse_got)
    mine = jnp.exp(lse_mine - top)
    got = jnp.exp(lse_got - top)
    share = mine / (mine + got)
    for h in range(heads):
        cols = pl.ds(h * HD, HD)
        w = share[:, h : h + 1]
        ctx_s[:, cols] = (
            kept_ref[:, cols] * w + got_ref[:, cols].astype(jnp.float32) * (1.0 - w)
        ).astype(jnp.bfloat16)
    for d in list(range(1, tp)) + [0]:
        for lower in range(0, part, chunk):
            cols = pl.ds(lower, chunk)
            out = jnp.dot(ctx_s[...], w_out_ref[d, :, cols], preferred_element_type=jnp.float32)
            for s in range(steps):
                outs[d][s, :, cols] = out[s * own : (s + 1) * own].astype(outs[d].dtype)


def body(
    hidden_in,
    norm_gain,
    w_query,
    w_key,
    w_value,
    w_out,
    prompt_keys,
    prompt_values,
    gen_keys,
    gen_values,
    lengths,
    parents,
):
    steps, own, part = hidden_in.shape
    tp = lax.axis_size("tp")
    rows = steps * own
    width = w_query.shape[0]
    kv = w_key.shape[1] // HD
    group = w_query.shape[1] // w_key.shape[1]
    heads = kv * group
    history = gen_keys.shape[1]

    pieces = [
        across(hidden_in, b, t) for b in range(2) for t in range(tp) if (b, t) != (0, 0)
    ]

    def in_hbm(x):
        return pltpu.with_memory_space_constraint(x, pltpu.HBM)

    vmem = pl.BlockSpec(memory_space=pltpu.VMEM)
    hbm = pl.BlockSpec(memory_space=pltpu.HBM)
    params = pltpu.CompilerParams(vmem_limit_bytes=16 * 2**20)
    f32, bf16 = jnp.float32, jnp.bfloat16
    blocks = prompt_keys.shape[1] // history
    old = (kv, blocks + own, history)
    loaded = pl.pallas_call(
        functools.partial(load_kernel, (steps, own, kv, group, history)),
        out_shape=(
            jax.ShapeDtypeStruct((1, width), f32),
            jax.ShapeDtypeStruct((rows, part), f32),
            jax.ShapeDtypeStruct(w_query.shape, bf16),
            jax.ShapeDtypeStruct(w_key.shape, bf16),
            jax.ShapeDtypeStruct((*old, HD), bf16),
            jax.ShapeDtypeStruct((*old, 2 * HD), bf16),
            jax.ShapeDtypeStruct((2 * rows, HD), f32),
            jax.ShapeDtypeStruct((2 * rows, HD), f32),
            jax.ShapeDtypeStruct((group * 2 * rows, (blocks + own) * history + HD), f32),
        ),
        in_specs=[hbm] * 10,
        out_specs=(vmem,) * 9,
        scratch_shapes=[
            pltpu.SMEM(lengths.shape, jnp.int32),
            pltpu.SMEM(parents.shape, jnp.int32),
            pltpu.VMEM(hidden_in.shape, bf16),
            pltpu.SemaphoreType.DMA((16 + 4 * kv,)),
        ],
        compiler_params=params,
        name="load",
    )(
        *(
            in_hbm(x)
            for x in (
                lengths,
                parents,
                norm_gain[None, :],
                hidden_in,
                w_query,
                w_key,
                prompt_keys.reshape(blocks, history, kv * HD),
                prompt_values.reshape(blocks, history, kv * HD),
                gen_keys,
                gen_values,
            )
        )
    )

    kept, kept_lse, sent, w_out_near = pl.pallas_call(
        functools.partial(attend_kernel, (steps, own, tp, kv, group)),
        out_shape=(
            jax.ShapeDtypeStruct((rows, heads * HD), f32),
            jax.ShapeDtypeStruct((rows, HD), f32),
            jax.ShapeDtypeStruct((rows, heads * HD + HD), bf16),
            jax.ShapeDtypeStruct((tp, heads * HD, part), bf16),
        ),
        in_specs=[vmem] * 9 + [hbm] * 2 + [vmem] * (2 * tp - 1),
        out_specs=(vmem,) * 4,
        scratch_shapes=[
            pltpu.VMEM((2 * tp, rows, part), f32),
            pltpu.VMEM((2 * rows, width), bf16),
            pltpu.VMEM(w_value.shape, bf16),
            pltpu.SemaphoreType.DMA((tp + 1,)),
        ],
        compiler_params=params,
        name="attend",
    )(*loaded, in_hbm(w_value), in_hbm(w_out), *pieces)

    got = permute_by(sent, "req", 1)

    out_types = [f32] + [bf16] * (tp - 1)
    sums = pl.pallas_call(
        functools.partial(project_kernel, (steps, own, tp, heads, math.gcd(part, 512))),
        out_shape=tuple(jax.ShapeDtypeStruct((steps, own, part), kind) for kind in out_types),
        in_specs=[vmem] * 4,
        out_specs=(vmem,) * tp,
        scratch_shapes=[pltpu.VMEM((rows, heads * HD), bf16)],
        compiler_params=params,
        name="project",
    )(kept, kept_lse, got, w_out_near)
    total = sums[0]
    for t in range(1, tp):
        total = total + across(sums[t], 0, t).astype(f32)
    return total.astype(bf16)


def solution(mesh):
    in_specs = (
        P(None, "req", "tp"),
        P(),
        P(None, "tp"),
        P(None, "tp"),
        P(None, "tp"),
        P("tp", None),
        P("req", None, "tp"),
        P("req", None, "tp"),
        P("req", None, "tp"),
        P("req", None, "tp"),
        P(),
        P(),
    )
    out_specs = P(None, "req", "tp")
    return jax.shard_map(body, mesh=mesh, in_specs=in_specs, out_specs=out_specs, check_vma=False)
```

```python
import functools
import math

import jax
import jax.numpy as jnp
from jax import lax
from jax.experimental import pallas as pl
from jax.experimental.pallas import tpu as pltpu
from jax.sharding import PartitionSpec as P

HD = 128
BEAMS = 8

norm_eps = 1e-05
masked_score = -1e30
rope_base = 500000.0


def quotient(x, size):
    return x >> (size.bit_length() - 1) if size & (size - 1) == 0 else x // size


def remainder(x, size):
    return x & (size - 1) if size & (size - 1) == 0 else x % size


def permute_by(value, axis, distance):
    pairs = [(source, source ^ distance) for source in range(lax.axis_size(axis))]
    return lax.ppermute(value, axis, pairs)


def across(value, beam_distance, tp_distance):
    req, tp = lax.axis_size("req"), lax.axis_size("tp")
    pairs = [
        (r * tp + t, (r ^ beam_distance) * tp + (t ^ tp_distance))
        for r in range(req)
        for t in range(tp)
    ]
    return lax.ppermute(value, ("req", "tp"), pairs)


def load_kernel(
    sizes,
    lengths,
    parents,
    gain,
    hidden,
    wq,
    wk,
    pk,
    pv,
    gk,
    gv,
    gain_ref,
    x_ref,
    wq_ref,
    wk_ref,
    keys_ref,
    values_ref,
    cosine_ref,
    sine_ref,
    bias_ref,
    lengths_s,
    parents_s,
    hidden_s,
    sems,
):
    steps, own, kv, group, history = sizes
    rows = steps * own
    blocks = pk.shape[0]
    half_len = blocks * history
    device = lax.axis_index("req")
    request = device // 2
    parity = device % 2

    small = [
        (lengths, lengths_s),
        (parents, parents_s),
        (gain, gain_ref),
        (hidden, hidden_s),
    ]
    large = []
    for prompt, gen, target in ((pk, gk, keys_ref), (pv, gv, values_ref)):
        large.append((prompt, target.at[pl.ds(0, blocks)]))
        large.append((gen, target.at[pl.ds(blocks, own)]))
    for source, target, parts in ((wk, wk_ref, 4), (wq, wq_ref, 4)):
        size = source.shape[0] // parts
        for n in range(parts):
            place = pl.ds(n * size, size)
            large.append((source.at[place, pl.ds(0, target.shape[1])], target.at[place]))
    copies = [
        pltpu.make_async_copy(source, target, sems.at[n])
        for n, (source, target) in enumerate(small + large)
    ]
    for copy in copies:
        copy.start()
    for copy in copies[: len(small)]:
        copy.wait()

    for s in range(steps):
        x_ref[pl.ds(s * own, own), :] = hidden_s[s].astype(jnp.float32)

    length = lengths_s[request]
    row = lax.broadcasted_iota(jnp.int32, (2 * rows, HD), 0)
    lane = lax.broadcasted_iota(jnp.int32, (2 * rows, HD), 1)
    half_dim = HD // 2
    inverse = jnp.exp(remainder(lane, half_dim).astype(jnp.float32) * (-math.log(rope_base) / half_dim))
    step = quotient(remainder(row, rows), own)
    angle = (length + history + step).astype(jnp.float32) * inverse
    sine = jnp.sin(angle)
    cosine_ref[...] = jnp.cos(angle)
    sine_ref[...] = jnp.where(lane < half_dim, -sine, sine)

    count = group * 2 * rows

    def parent_of(s, beam):
        out = jnp.zeros_like(beam)
        for j in range(BEAMS):
            out = jnp.where(beam == j, parents_s[s, request * BEAMS + j], out)
        return out

    row = remainder(lax.broadcasted_iota(jnp.int32, (count, HD), 0), 2 * rows)
    row_step = quotient(remainder(row, rows), own)
    row_parity = jnp.where(row < rows, parity, 1 - parity)
    beam = row_parity * own + remainder(row, own)
    ancestors = [None] * steps
    at = beam
    for s in reversed(range(steps)):
        if s < steps - 1:
            at = jnp.where(row_step > s, parent_of(s + 1, at), beam)
        ancestors[s] = jnp.where(row_step >= s, at, -1)
    origin = parent_of(0, at)
    lane = lax.broadcasted_iota(jnp.int32, (count, HD), 1)

    for c in range(half_len // HD):
        place = parity * half_len + c * HD + lane
        bias_ref[:, pl.ds(c * HD, HD)] = jnp.where(place < length, 0.0, masked_score)
    for c in range(own * history // HD):
        key_beam = parity * own + quotient(c * HD + lane, history)
        bias_ref[:, pl.ds(half_len + c * HD, HD)] = jnp.where(
            key_beam == origin, 0.0, masked_score
        )
    new_bias = jnp.full((count, HD), masked_score, jnp.float32)
    for s in range(steps):
        hit = (quotient(lane, own) == s) & (
            ancestors[s] == parity * own + remainder(lane, own)
        )
        new_bias = jnp.where(hit, 0.0, new_bias)
    bias_ref[:, pl.ds(half_len + own * history, HD)] = new_bias
    for copy in copies[len(small) :]:
        copy.wait()


def attend_kernel(
    sizes,
    gain_ref,
    x_ref,
    wq_ref,
    wk_ref,
    keys_ref,
    values_ref,
    cosine_ref,
    sine_ref,
    bias_ref,
    wq,
    wv,
    *refs,
):
    steps, own, tp, kv, group = sizes
    pieces = (None,) + refs[: 2 * tp - 1]
    kept_ref, kept_lse_ref, sent_ref, x_s, xn_s, wq_s, wv_s, sems = refs[2 * tp - 1 :]
    rows = steps * own
    part = x_ref.shape[-1]
    width = part * tp
    heads = kv * group
    old = keys_ref.shape[0] * keys_ref.shape[1]
    me_tp = lax.axis_index("tp")

    near = wq_ref.shape[1]
    halves = [(wq.at[:, pl.ds(near, wq_s.shape[1])], wq_s)] if near < wq.shape[1] else []
    halves.append((wv, wv_s))
    copies = [
        pltpu.make_async_copy(source, target, sems.at[n])
        for n, (source, target) in enumerate(halves)
    ]
    for copy in copies:
        copy.start()

    squares = []
    for b in range(2):
        total = jnp.zeros((rows, HD), jnp.float32)
        for t in range(tp):
            column = pl.multiple_of((me_tp ^ t) * part, HD)
            if (b, t) == (0, 0):
                mine = x_ref[...]
            else:
                for s in range(steps):
                    x_s[b * tp + t, pl.ds(s * own, own), :] = pieces[b * tp + t][s].astype(
                        jnp.float32
                    )
                mine = x_s[b * tp + t]
            xn_s[pl.ds(b * rows, rows), pl.ds(column, part)] = (
                mine * gain_ref[:, pl.ds(column, part)]
            ).astype(jnp.bfloat16)
            mine = mine * mine
            for c in range(part // HD):
                total = total + mine[:, c * HD : (c + 1) * HD]
        squares.append(jnp.sum(total, axis=-1, keepdims=True))
    scale = lax.rsqrt(jnp.concatenate(squares, axis=0) / width + norm_eps)
    key_tables = (cosine_ref[...] * scale, sine_ref[...] * scale)
    query_tables = tuple(x * HD**-0.5 for x in key_tables)

    def rotate(x, tables):
        return (x * tables[0] + pltpu.roll(x, HD // 2, 1) * tables[1]).astype(jnp.bfloat16)

    def project(w_ref, lower, size):
        block = jnp.dot(
            xn_s[...], w_ref[:, pl.ds(lower, size)], preferred_element_type=jnp.float32
        )
        return [block[:, c * HD : (c + 1) * HD] for c in range(size // HD)]

    def project_all(w_ref):
        size = math.gcd(w_ref.shape[1], 2 * HD)
        return [x for c in range(0, w_ref.shape[1], size) for x in project(w_ref, c, size)]

    pad = jnp.zeros((HD - rows, HD), jnp.bfloat16)
    ones = jnp.ones((HD, HD), jnp.bfloat16)
    old_ones = jnp.ones((old, HD), jnp.bfloat16)
    contract = (((1,), (1,)), ((), ()))
    new_keys = [
        jnp.concatenate([rotate(x, key_tables)[:rows], pad], axis=0) for x in project_all(wk_ref)
    ]

    def score(g):
        lower = g * group * HD
        if lower == near:
            copies[0].wait()
        source, lower = (wq_ref, lower) if lower < near else (wq_s, lower - near)
        q = jnp.concatenate(
            [rotate(x, query_tables) for x in project(source, lower, group * HD)], axis=0
        )
        before = lax.dot_general(
            q,
            keys_ref[:, :, pl.ds(g * HD, HD)].reshape(old, HD),
            contract,
            preferred_element_type=jnp.float32,
        )
        now = lax.dot_general(q, new_keys[g], contract, preferred_element_type=jnp.float32)
        return before + bias_ref[:, pl.ds(0, old)], now + bias_ref[:, pl.ds(old, HD)]

    def soften(before, now):
        most = now
        for c in range(old // HD):
            most = jnp.maximum(most, before[:, c * HD : (c + 1) * HD])
        top = jnp.max(most, axis=-1, keepdims=True)
        return (
            jnp.exp(before - top).astype(jnp.bfloat16),
            jnp.exp(now - top).astype(jnp.bfloat16),
            top,
        )

    scores, soft = [], []
    for g in range(kv):
        scores.append(score(g))
        if g > 0:
            soft.append(soften(*scores[g - 1]))
    soft.append(soften(*scores[kv - 1]))

    copies[-1].wait()
    new_values = [
        jnp.concatenate([(x * scale).astype(jnp.bfloat16)[:rows], pad], axis=0)
        for x in project_all(wv_s)
    ]
    lane = lax.broadcasted_iota(jnp.int32, (rows, HD), 1)
    kept_lse = jnp.zeros((rows, HD), jnp.float32)
    sent_lse = jnp.zeros((rows, HD), jnp.float32)
    for g in range(kv):
        before, now, top = soft[g]
        old_values = values_ref[:, :, pl.ds(g * HD, HD)].reshape(old, HD)
        mixed = jnp.dot(
            before,
            jnp.concatenate([old_values, old_ones], axis=1),
            preferred_element_type=jnp.float32,
        ) + jnp.dot(
            now,
            jnp.concatenate([new_values[g], ones], axis=1),
            preferred_element_type=jnp.float32,
        )
        total = mixed[:, HD:]
        mixed = mixed[:, :HD] / total
        lse = top + jnp.log(total)
        for j in range(group):
            h = g * group + j
            lower = j * 2 * rows
            kept_ref[:, pl.ds(h * HD, HD)] = mixed[lower : lower + rows]
            sent_ref[:, pl.ds(h * HD, HD)] = mixed[lower + rows : lower + 2 * rows].astype(
                jnp.bfloat16
            )
            kept_lse = jnp.where(lane == h, lse[lower : lower + rows], kept_lse)
            sent_lse = jnp.where(lane % heads == h, lse[lower + rows : lower + 2 * rows], sent_lse)
    kept_lse_ref[...] = kept_lse
    terms = jnp.zeros((rows, HD), jnp.float32)
    rest = sent_lse
    for n in range(3):
        term = rest.astype(jnp.bfloat16).astype(jnp.float32)
        terms = jnp.where(lane // heads == n, term, terms)
        rest = rest - term
    sent_ref[:, pl.ds(heads * HD, HD)] = terms.astype(jnp.bfloat16)


def project_kernel(sizes, kept_ref, kept_lse_ref, got_ref, w_out_ref, *refs):
    steps, own, tp, heads, chunk = sizes
    outs = refs[:tp]
    (ctx_s,) = refs[tp:]
    me_tp = lax.axis_index("tp")
    part = outs[0].shape[-1]
    base = heads * HD
    lse_mine = kept_lse_ref[...]
    terms = got_ref[:, pl.ds(base, HD)].astype(jnp.float32)
    lse_got = terms + pltpu.roll(terms, HD - heads, 1) + pltpu.roll(terms, HD - 2 * heads, 1)
    top = jnp.maximum(lse_mine, lse_got)
    mine = jnp.exp(lse_mine - top)
    got = jnp.exp(lse_got - top)
    share = mine / (mine + got)
    for h in range(heads):
        cols = pl.ds(h * HD, HD)
        w = share[:, h : h + 1]
        ctx_s[:, cols] = (
            kept_ref[:, cols] * w + got_ref[:, cols].astype(jnp.float32) * (1.0 - w)
        ).astype(jnp.bfloat16)
    for d in list(range(1, tp)) + [0]:
        for lower in range(0, part, chunk):
            cols = pl.ds(lower, chunk)
            place = pl.ds(pl.multiple_of((me_tp ^ d) * part + lower, HD), chunk)
            out = jnp.dot(ctx_s[...], w_out_ref[:, place], preferred_element_type=jnp.float32)
            for s in range(steps):
                outs[d][s, :, cols] = out[s * own : (s + 1) * own].astype(outs[d].dtype)


def body(
    hidden_in,
    norm_gain,
    w_query,
    w_key,
    w_value,
    w_out,
    prompt_keys,
    prompt_values,
    gen_keys,
    gen_values,
    lengths,
    parents,
):
    steps, own, part = hidden_in.shape
    tp = lax.axis_size("tp")
    rows = steps * own
    width = w_query.shape[0]
    kv = w_key.shape[1] // HD
    group = w_query.shape[1] // w_key.shape[1]
    heads = kv * group
    history = gen_keys.shape[1]

    pieces = [
        across(hidden_in, b, t) for b in range(2) for t in range(tp) if (b, t) != (0, 0)
    ]

    def in_hbm(x):
        return pltpu.with_memory_space_constraint(x, pltpu.HBM)

    vmem = pl.BlockSpec(memory_space=pltpu.VMEM)
    hbm = pl.BlockSpec(memory_space=pltpu.HBM)
    params = pltpu.CompilerParams(vmem_limit_bytes=16 * 2**20)
    f32, bf16 = jnp.float32, jnp.bfloat16
    blocks = prompt_keys.shape[1] // history
    old = (blocks + own, history, kv * HD)
    near = max(kv // 2, 1) * group * HD
    loaded = pl.pallas_call(
        functools.partial(load_kernel, (steps, own, kv, group, history)),
        out_shape=(
            jax.ShapeDtypeStruct((1, width), f32),
            jax.ShapeDtypeStruct((rows, part), f32),
            jax.ShapeDtypeStruct((width, near), bf16),
            jax.ShapeDtypeStruct(w_key.shape, bf16),
            jax.ShapeDtypeStruct(old, bf16),
            jax.ShapeDtypeStruct(old, bf16),
            jax.ShapeDtypeStruct((2 * rows, HD), f32),
            jax.ShapeDtypeStruct((2 * rows, HD), f32),
            jax.ShapeDtypeStruct((group * 2 * rows, (blocks + own) * history + HD), f32),
        ),
        in_specs=[hbm] * 10,
        out_specs=(vmem,) * 9,
        scratch_shapes=[
            pltpu.SMEM(lengths.shape, jnp.int32),
            pltpu.SMEM(parents.shape, jnp.int32),
            pltpu.VMEM(hidden_in.shape, bf16),
            pltpu.SemaphoreType.DMA((16,)),
        ],
        compiler_params=params,
        name="load",
    )(
        *(
            in_hbm(x)
            for x in (
                lengths,
                parents,
                norm_gain[None, :],
                hidden_in,
                w_query,
                w_key,
                prompt_keys.reshape(blocks, history, kv * HD),
                prompt_values.reshape(blocks, history, kv * HD),
                gen_keys,
                gen_values,
            )
        )
    )

    kept, kept_lse, sent = pl.pallas_call(
        functools.partial(attend_kernel, (steps, own, tp, kv, group)),
        out_shape=(
            jax.ShapeDtypeStruct((rows, heads * HD), f32),
            jax.ShapeDtypeStruct((rows, HD), f32),
            jax.ShapeDtypeStruct((rows, heads * HD + HD), bf16),
        ),
        in_specs=[vmem] * 9 + [hbm] * 2 + [vmem] * (2 * tp - 1),
        out_specs=(vmem,) * 3,
        scratch_shapes=[
            pltpu.VMEM((2 * tp, rows, part), f32),
            pltpu.VMEM((2 * rows, width), bf16),
            pltpu.VMEM((width, near), bf16),
            pltpu.VMEM(w_value.shape, bf16),
            pltpu.SemaphoreType.DMA((2,)),
        ],
        compiler_params=params,
        name="attend",
    )(*loaded, in_hbm(w_query), in_hbm(w_value), *pieces)

    got = permute_by(sent, "req", 1)

    out_types = [f32] + [bf16] * (tp - 1)
    sums = pl.pallas_call(
        functools.partial(project_kernel, (steps, own, tp, heads, math.gcd(part, 512))),
        out_shape=tuple(jax.ShapeDtypeStruct((steps, own, part), kind) for kind in out_types),
        in_specs=[vmem] * 4,
        out_specs=(vmem,) * tp,
        scratch_shapes=[pltpu.VMEM((rows, heads * HD), bf16)],
        compiler_params=params,
        name="project",
    )(kept, kept_lse, got, pltpu.with_memory_space_constraint(w_out, pltpu.VMEM))
    total = sums[0]
    for t in range(1, tp):
        total = total + across(sums[t], 0, t).astype(f32)
    return total.astype(bf16)


def solution(mesh):
    in_specs = (
        P(None, "req", "tp"),
        P(),
        P(None, "tp"),
        P(None, "tp"),
        P(None, "tp"),
        P("tp", None),
        P("req", None, "tp"),
        P("req", None, "tp"),
        P("req", None, "tp"),
        P("req", None, "tp"),
        P(),
        P(),
    )
    out_specs = P(None, "req", "tp")
    return jax.shard_map(body, mesh=mesh, in_specs=in_specs, out_specs=out_specs, check_vma=False)
```

```python
import functools
import math

import jax
import jax.numpy as jnp
from jax import lax
from jax.experimental import pallas as pl
from jax.experimental.pallas import tpu as pltpu
from jax.sharding import PartitionSpec as P

HD = 128
BEAMS = 8

norm_eps = 1e-05
masked_score = -1e30
rope_base = 500000.0


def quotient(x, size):
    return x >> (size.bit_length() - 1) if size & (size - 1) == 0 else x // size


def remainder(x, size):
    return x & (size - 1) if size & (size - 1) == 0 else x % size


def permute_by(value, axis, distance):
    pairs = [(source, source ^ distance) for source in range(lax.axis_size(axis))]
    return lax.ppermute(value, axis, pairs)


def across(value, beam_distance, tp_distance):
    req, tp = lax.axis_size("req"), lax.axis_size("tp")
    pairs = [
        (r * tp + t, (r ^ beam_distance) * tp + (t ^ tp_distance))
        for r in range(req)
        for t in range(tp)
    ]
    return lax.ppermute(value, ("req", "tp"), pairs)


def load_kernel(
    sizes,
    lengths,
    parents,
    gain,
    hidden,
    wq,
    wk,
    pk,
    pv,
    gk,
    gv,
    gain_ref,
    x_ref,
    wq_ref,
    wk_ref,
    keys_ref,
    values_ref,
    cosine_ref,
    sine_ref,
    bias_ref,
    lengths_s,
    parents_s,
    hidden_s,
    sems,
):
    steps, own, kv, group, history = sizes
    rows = steps * own
    blocks = pk.shape[0]
    half_len = blocks * history
    device = lax.axis_index("req")
    request = device // 2
    parity = device % 2

    small = [
        (lengths, lengths_s),
        (parents, parents_s),
        (gain, gain_ref),
        (hidden, hidden_s),
    ]
    large = []
    for prompt, gen, target in ((pk, gk, keys_ref), (pv, gv, values_ref)):
        large.append((prompt, target.at[pl.ds(0, blocks)]))
        large.append((gen, target.at[pl.ds(blocks, own)]))
    for source, target, parts in ((wk, wk_ref, 4), (wq, wq_ref, 4)):
        size = source.shape[0] // parts
        for n in range(parts):
            place = pl.ds(n * size, size)
            large.append((source.at[place, pl.ds(0, target.shape[1])], target.at[place]))
    copies = [
        pltpu.make_async_copy(source, target, sems.at[n])
        for n, (source, target) in enumerate(small + large)
    ]
    for copy in copies:
        copy.start()
    for copy in copies[: len(small)]:
        copy.wait()

    for s in range(steps):
        x_ref[pl.ds(s * own, own), :] = hidden_s[s].astype(jnp.float32)

    length = lengths_s[request]
    row = lax.broadcasted_iota(jnp.int32, (2 * rows, HD), 0)
    lane = lax.broadcasted_iota(jnp.int32, (2 * rows, HD), 1)
    half_dim = HD // 2
    inverse = jnp.exp(remainder(lane, half_dim).astype(jnp.float32) * (-math.log(rope_base) / half_dim))
    step = quotient(remainder(row, rows), own)
    angle = (length + history + step).astype(jnp.float32) * inverse
    sine = jnp.sin(angle)
    cosine_ref[...] = jnp.cos(angle)
    sine_ref[...] = jnp.where(lane < half_dim, -sine, sine)

    count = group * 2 * rows

    def parent_of(s, beam):
        out = jnp.zeros_like(beam)
        for j in range(BEAMS):
            out = jnp.where(beam == j, parents_s[s, request * BEAMS + j], out)
        return out

    row = remainder(lax.broadcasted_iota(jnp.int32, (count, HD), 0), 2 * rows)
    row_step = quotient(remainder(row, rows), own)
    row_parity = jnp.where(row < rows, parity, 1 - parity)
    beam = row_parity * own + remainder(row, own)
    ancestors = [None] * steps
    at = beam
    for s in reversed(range(steps)):
        if s < steps - 1:
            at = jnp.where(row_step > s, parent_of(s + 1, at), beam)
        ancestors[s] = jnp.where(row_step >= s, at, -1)
    origin = parent_of(0, at)
    lane = lax.broadcasted_iota(jnp.int32, (count, HD), 1)

    for c in range(half_len // HD):
        place = parity * half_len + c * HD + lane
        bias_ref[:, pl.ds(c * HD, HD)] = jnp.where(place < length, 0.0, masked_score)
    for c in range(own * history // HD):
        key_beam = parity * own + quotient(c * HD + lane, history)
        bias_ref[:, pl.ds(half_len + c * HD, HD)] = jnp.where(
            key_beam == origin, 0.0, masked_score
        )
    new_bias = jnp.full((count, HD), masked_score, jnp.float32)
    for s in range(steps):
        hit = (quotient(lane, own) == s) & (
            ancestors[s] == parity * own + remainder(lane, own)
        )
        new_bias = jnp.where(hit, 0.0, new_bias)
    bias_ref[:, pl.ds(half_len + own * history, HD)] = new_bias
    for copy in copies[len(small) :]:
        copy.wait()


def attend_kernel(
    sizes,
    gain_ref,
    x_ref,
    wq_ref,
    wk_ref,
    keys_ref,
    values_ref,
    cosine_ref,
    sine_ref,
    bias_ref,
    wq,
    wv,
    *refs,
):
    steps, own, tp, kv, group = sizes
    pieces = (None,) + refs[: 2 * tp - 1]
    kept_ref, kept_lse_ref, sent_ref, x_s, xn_s, wq_s, wv_s, sems = refs[2 * tp - 1 :]
    rows = steps * own
    part = x_ref.shape[-1]
    width = part * tp
    heads = kv * group
    old = keys_ref.shape[0] * keys_ref.shape[1]
    me_tp = lax.axis_index("tp")

    near = wq_ref.shape[1]
    halves = [(wq.at[:, pl.ds(near, wq_s.shape[1])], wq_s)] if near < wq.shape[1] else []
    halves.append((wv, wv_s))
    copies = [
        pltpu.make_async_copy(source, target, sems.at[n])
        for n, (source, target) in enumerate(halves)
    ]
    for copy in copies:
        copy.start()

    squares = []
    for b in range(2):
        total = jnp.zeros((rows, HD), jnp.float32)
        for t in range(tp):
            column = pl.multiple_of((me_tp ^ t) * part, HD)
            if (b, t) == (0, 0):
                mine = x_ref[...]
            else:
                for s in range(steps):
                    x_s[b * tp + t, pl.ds(s * own, own), :] = pieces[b * tp + t][s].astype(
                        jnp.float32
                    )
                mine = x_s[b * tp + t]
            xn_s[pl.ds(b * rows, rows), pl.ds(column, part)] = (
                mine * gain_ref[:, pl.ds(column, part)]
            ).astype(jnp.bfloat16)
            mine = mine * mine
            for c in range(part // HD):
                total = total + mine[:, c * HD : (c + 1) * HD]
        squares.append(jnp.sum(total, axis=-1, keepdims=True))
    scale = lax.rsqrt(jnp.concatenate(squares, axis=0) / width + norm_eps)
    key_tables = (cosine_ref[...] * scale, sine_ref[...] * scale)
    query_tables = tuple(x * HD**-0.5 for x in key_tables)

    def rotate(x, tables):
        return (x * tables[0] + pltpu.roll(x, HD // 2, 1) * tables[1]).astype(jnp.bfloat16)

    def project(w_ref, lower, size):
        block = jnp.dot(
            xn_s[...], w_ref[:, pl.ds(lower, size)], preferred_element_type=jnp.float32
        )
        return [block[:, c * HD : (c + 1) * HD] for c in range(size // HD)]

    def project_all(w_ref):
        size = math.gcd(w_ref.shape[1], 2 * HD)
        return [x for c in range(0, w_ref.shape[1], size) for x in project(w_ref, c, size)]

    pad = jnp.zeros((HD - rows, HD), jnp.bfloat16)
    ones = jnp.ones((HD, HD), jnp.bfloat16)
    old_ones = jnp.ones((old, HD), jnp.bfloat16)
    contract = (((1,), (1,)), ((), ()))
    new_keys = [
        jnp.concatenate([rotate(x, key_tables)[:rows], pad], axis=0) for x in project_all(wk_ref)
    ]

    def score(g):
        lower = g * group * HD
        if lower == near:
            copies[0].wait()
        source, lower = (wq_ref, lower) if lower < near else (wq_s, lower - near)
        q = jnp.concatenate(
            [rotate(x, query_tables) for x in project(source, lower, group * HD)], axis=0
        )
        before = lax.dot_general(
            q,
            keys_ref[:, :, pl.ds(g * HD, HD)].reshape(old, HD),
            contract,
            preferred_element_type=jnp.float32,
        )
        now = lax.dot_general(q, new_keys[g], contract, preferred_element_type=jnp.float32)
        return before + bias_ref[:, pl.ds(0, old)], now + bias_ref[:, pl.ds(old, HD)]

    def soften(before, now):
        most = now
        for c in range(old // HD):
            most = jnp.maximum(most, before[:, c * HD : (c + 1) * HD])
        top = jnp.max(most, axis=-1, keepdims=True)
        return (
            jnp.exp(before - top).astype(jnp.bfloat16),
            jnp.exp(now - top).astype(jnp.bfloat16),
            top,
        )

    scores, soft = [], []
    for g in range(kv):
        scores.append(score(g))
        if g > 0:
            soft.append(soften(*scores[g - 1]))
    soft.append(soften(*scores[kv - 1]))

    copies[-1].wait()
    new_values = [
        jnp.concatenate([(x * scale).astype(jnp.bfloat16)[:rows], pad], axis=0)
        for x in project_all(wv_s)
    ]
    lane = lax.broadcasted_iota(jnp.int32, (rows, HD), 1)
    kept_lse = jnp.zeros((rows, HD), jnp.float32)
    sent_lse = jnp.zeros((rows, HD), jnp.float32)
    for g in range(kv):
        before, now, top = soft[g]
        old_values = values_ref[:, :, pl.ds(g * HD, HD)].reshape(old, HD)
        mixed = jnp.dot(
            before,
            jnp.concatenate([old_values, old_ones], axis=1),
            preferred_element_type=jnp.float32,
        ) + jnp.dot(
            now,
            jnp.concatenate([new_values[g], ones], axis=1),
            preferred_element_type=jnp.float32,
        )
        total = mixed[:, HD:]
        mixed = mixed[:, :HD] / total
        lse = top + jnp.log(total)
        for j in range(group):
            h = g * group + j
            lower = j * 2 * rows
            kept_ref[:, pl.ds(h * HD, HD)] = mixed[lower : lower + rows]
            sent_ref[:, pl.ds(h * HD, HD)] = mixed[lower + rows : lower + 2 * rows].astype(
                jnp.bfloat16
            )
            kept_lse = jnp.where(lane == h, lse[lower : lower + rows], kept_lse)
            sent_lse = jnp.where(lane % heads == h, lse[lower + rows : lower + 2 * rows], sent_lse)
    kept_lse_ref[...] = kept_lse
    terms = jnp.zeros((rows, HD), jnp.float32)
    rest = sent_lse
    for n in range(3):
        term = rest.astype(jnp.bfloat16).astype(jnp.float32)
        terms = jnp.where(lane // heads == n, term, terms)
        rest = rest - term
    sent_ref[:, pl.ds(heads * HD, HD)] = terms.astype(jnp.bfloat16)


def fetch_kernel(kept_lse_ref, w_out, kept_lse_out, w_out_ref, sems):
    copies = []
    tp = w_out_ref.shape[0]
    part = w_out_ref.shape[-1]
    me_tp = lax.axis_index("tp")
    for d in range(tp):
        place = pl.ds(pl.multiple_of((me_tp ^ d) * part, HD), part)
        copies.append(pltpu.make_async_copy(w_out.at[:, place], w_out_ref.at[d], sems.at[d]))
    for copy in copies:
        copy.start()
    kept_lse_out[...] = kept_lse_ref[...]
    for copy in copies:
        copy.wait()


def project_kernel(sizes, kept_ref, kept_lse_ref, got_ref, w_out_ref, *refs):
    steps, own, tp, heads, chunk = sizes
    outs = refs[:tp]
    (ctx_s,) = refs[tp:]
    part = outs[0].shape[-1]
    base = heads * HD
    lse_mine = kept_lse_ref[...]
    terms = got_ref[:, pl.ds(base, HD)].astype(jnp.float32)
    lse_got = terms + pltpu.roll(terms, HD - heads, 1) + pltpu.roll(terms, HD - 2 * heads, 1)
    top = jnp.maximum(lse_mine, lse_got)
    mine = jnp.exp(lse_mine - top)
    got = jnp.exp(lse_got - top)
    share = mine / (mine + got)
    for h in range(heads):
        cols = pl.ds(h * HD, HD)
        w = share[:, h : h + 1]
        ctx_s[:, cols] = (
            kept_ref[:, cols] * w + got_ref[:, cols].astype(jnp.float32) * (1.0 - w)
        ).astype(jnp.bfloat16)
    for d in list(range(1, tp)) + [0]:
        for lower in range(0, part, chunk):
            cols = pl.ds(lower, chunk)
            out = jnp.dot(ctx_s[...], w_out_ref[d, :, cols], preferred_element_type=jnp.float32)
            for s in range(steps):
                outs[d][s, :, cols] = out[s * own : (s + 1) * own].astype(outs[d].dtype)


def body(
    hidden_in,
    norm_gain,
    w_query,
    w_key,
    w_value,
    w_out,
    prompt_keys,
    prompt_values,
    gen_keys,
    gen_values,
    lengths,
    parents,
):
    steps, own, part = hidden_in.shape
    tp = lax.axis_size("tp")
    rows = steps * own
    width = w_query.shape[0]
    kv = w_key.shape[1] // HD
    group = w_query.shape[1] // w_key.shape[1]
    heads = kv * group
    history = gen_keys.shape[1]

    pieces = [
        across(hidden_in, b, t) for b in range(2) for t in range(tp) if (b, t) != (0, 0)
    ]

    def in_hbm(x):
        return pltpu.with_memory_space_constraint(x, pltpu.HBM)

    vmem = pl.BlockSpec(memory_space=pltpu.VMEM)
    hbm = pl.BlockSpec(memory_space=pltpu.HBM)
    params = pltpu.CompilerParams(vmem_limit_bytes=16 * 2**20)
    f32, bf16 = jnp.float32, jnp.bfloat16
    blocks = prompt_keys.shape[1] // history
    old = (blocks + own, history, kv * HD)
    near = max(kv // 2, 1) * group * HD
    loaded = pl.pallas_call(
        functools.partial(load_kernel, (steps, own, kv, group, history)),
        out_shape=(
            jax.ShapeDtypeStruct((1, width), f32),
            jax.ShapeDtypeStruct((rows, part), f32),
            jax.ShapeDtypeStruct((width, near), bf16),
            jax.ShapeDtypeStruct(w_key.shape, bf16),
            jax.ShapeDtypeStruct(old, bf16),
            jax.ShapeDtypeStruct(old, bf16),
            jax.ShapeDtypeStruct((2 * rows, HD), f32),
            jax.ShapeDtypeStruct((2 * rows, HD), f32),
            jax.ShapeDtypeStruct((group * 2 * rows, (blocks + own) * history + HD), f32),
        ),
        in_specs=[hbm] * 10,
        out_specs=(vmem,) * 9,
        scratch_shapes=[
            pltpu.SMEM(lengths.shape, jnp.int32),
            pltpu.SMEM(parents.shape, jnp.int32),
            pltpu.VMEM(hidden_in.shape, bf16),
            pltpu.SemaphoreType.DMA((16,)),
        ],
        compiler_params=params,
        name="load",
    )(
        *(
            in_hbm(x)
            for x in (
                lengths,
                parents,
                norm_gain[None, :],
                hidden_in,
                w_query,
                w_key,
                prompt_keys.reshape(blocks, history, kv * HD),
                prompt_values.reshape(blocks, history, kv * HD),
                gen_keys,
                gen_values,
            )
        )
    )

    kept, kept_lse, sent = pl.pallas_call(
        functools.partial(attend_kernel, (steps, own, tp, kv, group)),
        out_shape=(
            jax.ShapeDtypeStruct((rows, heads * HD), f32),
            jax.ShapeDtypeStruct((rows, HD), f32),
            jax.ShapeDtypeStruct((rows, heads * HD + HD), bf16),
        ),
        in_specs=[vmem] * 9 + [hbm] * 2 + [vmem] * (2 * tp - 1),
        out_specs=(vmem,) * 3,
        scratch_shapes=[
            pltpu.VMEM((2 * tp, rows, part), f32),
            pltpu.VMEM((2 * rows, width), bf16),
            pltpu.VMEM((width, near), bf16),
            pltpu.VMEM(w_value.shape, bf16),
            pltpu.SemaphoreType.DMA((2,)),
        ],
        compiler_params=params,
        name="attend",
    )(*loaded, in_hbm(w_query), in_hbm(w_value), *pieces)

    got = permute_by(sent, "req", 1)
    kept_lse, w_out_near = pl.pallas_call(
        fetch_kernel,
        out_shape=(
            jax.ShapeDtypeStruct((rows, HD), f32),
            jax.ShapeDtypeStruct((tp, heads * HD, part), bf16),
        ),
        in_specs=[vmem, hbm],
        out_specs=(vmem, vmem),
        scratch_shapes=[pltpu.SemaphoreType.DMA((tp,))],
        compiler_params=params,
        name="fetch",
    )(kept_lse, in_hbm(w_out))

    out_types = [f32] + [bf16] * (tp - 1)
    sums = pl.pallas_call(
        functools.partial(project_kernel, (steps, own, tp, heads, math.gcd(part, 512))),
        out_shape=tuple(jax.ShapeDtypeStruct((steps, own, part), kind) for kind in out_types),
        in_specs=[vmem] * 4,
        out_specs=(vmem,) * tp,
        scratch_shapes=[pltpu.VMEM((rows, heads * HD), bf16)],
        compiler_params=params,
        name="project",
    )(kept, kept_lse, got, w_out_near)
    total = sums[0]
    for t in range(1, tp):
        total = total + across(sums[t], 0, t).astype(f32)
    return total.astype(bf16)


def solution(mesh):
    in_specs = (
        P(None, "req", "tp"),
        P(),
        P(None, "tp"),
        P(None, "tp"),
        P(None, "tp"),
        P("tp", None),
        P("req", None, "tp"),
        P("req", None, "tp"),
        P("req", None, "tp"),
        P("req", None, "tp"),
        P(),
        P(),
    )
    out_specs = P(None, "req", "tp")
    return jax.shard_map(body, mesh=mesh, in_specs=in_specs, out_specs=out_specs, check_vma=False)
```

```python
import functools
import math

import jax
import jax.numpy as jnp
from jax import lax
from jax.experimental import pallas as pl
from jax.experimental.pallas import tpu as pltpu
from jax.sharding import PartitionSpec as P

HD = 128
BEAMS = 8

norm_eps = 1e-05
masked_score = -1e30
rope_base = 500000.0


def quotient(x, size):
    return x >> (size.bit_length() - 1) if size & (size - 1) == 0 else x // size


def remainder(x, size):
    return x & (size - 1) if size & (size - 1) == 0 else x % size


def permute_by(value, axis, distance):
    pairs = [(source, source ^ distance) for source in range(lax.axis_size(axis))]
    return lax.ppermute(value, axis, pairs)


def across(value, beam_distance, tp_distance):
    req, tp = lax.axis_size("req"), lax.axis_size("tp")
    pairs = [
        (r * tp + t, (r ^ beam_distance) * tp + (t ^ tp_distance))
        for r in range(req)
        for t in range(tp)
    ]
    return lax.ppermute(value, ("req", "tp"), pairs)


def load_kernel(
    sizes,
    lengths,
    parents,
    gain,
    hidden,
    wq,
    wk,
    pk,
    pv,
    gk,
    gv,
    gain_ref,
    x_ref,
    wq_ref,
    wk_ref,
    keys_ref,
    values_ref,
    cosine_ref,
    sine_ref,
    bias_ref,
    lengths_s,
    parents_s,
    hidden_s,
    sems,
):
    steps, own, kv, group, history = sizes
    rows = steps * own
    blocks = pk.shape[0]
    half_len = blocks * history
    device = lax.axis_index("req")
    request = device // 2
    parity = device % 2

    small = [
        (lengths, lengths_s),
        (parents, parents_s),
        (gain, gain_ref),
        (hidden, hidden_s),
    ]
    large = []
    for prompt, gen, target in ((pk, gk, keys_ref), (pv, gv, values_ref)):
        large.append((prompt, target.at[pl.ds(0, blocks)]))
        large.append((gen, target.at[pl.ds(blocks, own)]))
    for source, target, parts in ((wk, wk_ref, 4), (wq, wq_ref, 4)):
        size = source.shape[0] // parts
        for n in range(parts):
            place = pl.ds(n * size, size)
            large.append((source.at[place, pl.ds(0, target.shape[1])], target.at[place]))
    copies = [
        pltpu.make_async_copy(source, target, sems.at[n])
        for n, (source, target) in enumerate(small + large)
    ]
    for copy in copies:
        copy.start()
    for copy in copies[: len(small)]:
        copy.wait()

    for s in range(steps):
        x_ref[pl.ds(s * own, own), :] = hidden_s[s].astype(jnp.float32)

    length = lengths_s[request]
    row = lax.broadcasted_iota(jnp.int32, (2 * rows, HD), 0)
    lane = lax.broadcasted_iota(jnp.int32, (2 * rows, HD), 1)
    half_dim = HD // 2
    inverse = jnp.exp(remainder(lane, half_dim).astype(jnp.float32) * (-math.log(rope_base) / half_dim))
    step = quotient(remainder(row, rows), own)
    angle = (length + history + step).astype(jnp.float32) * inverse
    sine = jnp.sin(angle)
    cosine_ref[...] = jnp.cos(angle)
    sine_ref[...] = jnp.where(lane < half_dim, -sine, sine)

    count = group * 2 * rows

    def parent_of(s, beam):
        out = jnp.zeros_like(beam)
        for j in range(BEAMS):
            out = jnp.where(beam == j, parents_s[s, request * BEAMS + j], out)
        return out

    row = remainder(lax.broadcasted_iota(jnp.int32, (count, HD), 0), 2 * rows)
    row_step = quotient(remainder(row, rows), own)
    row_parity = jnp.where(row < rows, parity, 1 - parity)
    beam = row_parity * own + remainder(row, own)
    ancestors = [None] * steps
    at = beam
    for s in reversed(range(steps)):
        if s < steps - 1:
            at = jnp.where(row_step > s, parent_of(s + 1, at), beam)
        ancestors[s] = jnp.where(row_step >= s, at, -1)
    origin = parent_of(0, at)
    lane = lax.broadcasted_iota(jnp.int32, (count, HD), 1)

    for c in range(half_len // HD):
        place = parity * half_len + c * HD + lane
        bias_ref[:, pl.ds(c * HD, HD)] = jnp.where(place < length, 0.0, masked_score)
    for c in range(own * history // HD):
        key_beam = parity * own + quotient(c * HD + lane, history)
        bias_ref[:, pl.ds(half_len + c * HD, HD)] = jnp.where(
            key_beam == origin, 0.0, masked_score
        )
    new_bias = jnp.full((count, HD), masked_score, jnp.float32)
    for s in range(steps):
        hit = (quotient(lane, own) == s) & (
            ancestors[s] == parity * own + remainder(lane, own)
        )
        new_bias = jnp.where(hit, 0.0, new_bias)
    bias_ref[:, pl.ds(half_len + own * history, HD)] = new_bias
    for copy in copies[len(small) :]:
        copy.wait()


def attend_kernel(
    sizes,
    gain_ref,
    x_ref,
    wq_ref,
    wk_ref,
    keys_ref,
    values_ref,
    cosine_ref,
    sine_ref,
    bias_ref,
    wq,
    wv,
    *refs,
):
    steps, own, tp, kv, group = sizes
    pieces = (None,) + refs[: 2 * tp - 1]
    kept_ref, kept_lse_ref, sent_ref, x_s, xn_s, q_s, wq_s, wv_s, sems = refs[2 * tp - 1 :]
    rows = steps * own
    part = x_ref.shape[-1]
    width = part * tp
    heads = kv * group
    old = keys_ref.shape[0] * keys_ref.shape[1]
    me_tp = lax.axis_index("tp")

    near = wq_ref.shape[1]
    halves = [(wq.at[:, pl.ds(near, wq_s.shape[1])], wq_s)] if near < wq.shape[1] else []
    halves.append((wv, wv_s))
    copies = [
        pltpu.make_async_copy(source, target, sems.at[n])
        for n, (source, target) in enumerate(halves)
    ]
    for copy in copies:
        copy.start()

    squares = []
    for b in range(2):
        total = jnp.zeros((rows, HD), jnp.float32)
        for t in range(tp):
            column = pl.multiple_of((me_tp ^ t) * part, HD)
            if (b, t) == (0, 0):
                mine = x_ref[...]
            else:
                for s in range(steps):
                    x_s[b * tp + t, pl.ds(s * own, own), :] = pieces[b * tp + t][s].astype(
                        jnp.float32
                    )
                mine = x_s[b * tp + t]
            xn_s[pl.ds(b * rows, rows), pl.ds(column, part)] = (
                mine * gain_ref[:, pl.ds(column, part)]
            ).astype(jnp.bfloat16)
            mine = mine * mine
            for c in range(part // HD):
                total = total + mine[:, c * HD : (c + 1) * HD]
        squares.append(jnp.sum(total, axis=-1, keepdims=True))
    scale = lax.rsqrt(jnp.concatenate(squares, axis=0) / width + norm_eps)
    key_tables = (cosine_ref[...] * scale, sine_ref[...] * scale)
    query_tables = tuple(x * HD**-0.5 for x in key_tables)

    def rotate(x, tables):
        return (x * tables[0] + pltpu.roll(x, HD // 2, 1) * tables[1]).astype(jnp.bfloat16)

    def project(w_ref):
        block = jnp.dot(xn_s[...], w_ref[...], preferred_element_type=jnp.float32)
        return [block[:, c * HD : (c + 1) * HD] for c in range(w_ref.shape[1] // HD)]

    pad = jnp.zeros((HD - rows, kv * HD), jnp.bfloat16)
    count = group * 2 * rows
    q_s[...] = jnp.zeros(q_s.shape, jnp.bfloat16)

    def place_queries(blocks, first):
        for n, block in enumerate(blocks):
            g, j = divmod(first + n, group)
            q_s[pl.ds(g * count + j * 2 * rows, 2 * rows), pl.ds(g * HD, HD)] = rotate(
                block, query_tables
            )

    new_keys = jnp.concatenate([rotate(x, key_tables)[:rows] for x in project(wk_ref)], axis=1)
    keys = jnp.concatenate([keys_ref[...].reshape(old, kv * HD), new_keys, pad], axis=0)
    place_queries(project(wq_ref), 0)
    if near < wq.shape[1]:
        copies[0].wait()
        place_queries(project(wq_s), near // HD)

    scores = lax.dot_general(
        q_s[...], keys, (((1,), (1,)), ((), ())), preferred_element_type=jnp.float32
    )
    copies[-1].wait()
    new_values = jnp.concatenate(
        [(x * scale).astype(jnp.bfloat16)[:rows] for x in project(wv_s)], axis=1
    )
    values = jnp.concatenate([values_ref[...].reshape(old, kv * HD), new_values, pad], axis=0)
    powers, tops = [], []
    for g in range(kv):
        score = scores[g * count : (g + 1) * count] + bias_ref[...]
        most = score[:, :HD]
        for c in range(1, old // HD + 1):
            most = jnp.maximum(most, score[:, c * HD : (c + 1) * HD])
        top = jnp.max(most, axis=-1, keepdims=True)
        powers.append(jnp.exp(score - top).astype(jnp.bfloat16))
        tops.append(top)
    mixed = jnp.dot(
        jnp.concatenate(powers, axis=0),
        jnp.concatenate([values, jnp.ones((old + HD, HD), jnp.bfloat16)], axis=1),
        preferred_element_type=jnp.float32,
    )
    lane = lax.broadcasted_iota(jnp.int32, (rows, HD), 1)
    kept_lse = jnp.zeros((rows, HD), jnp.float32)
    sent_lse = jnp.zeros((rows, HD), jnp.float32)
    for g in range(kv):
        mine = mixed[g * count : (g + 1) * count]
        total = mine[:, kv * HD :]
        mine = mine[:, g * HD : (g + 1) * HD] / total
        lse = tops[g] + jnp.log(total)
        for j in range(group):
            h = g * group + j
            lower = j * 2 * rows
            kept_ref[:, pl.ds(h * HD, HD)] = mine[lower : lower + rows]
            sent_ref[:, pl.ds(h * HD, HD)] = mine[lower + rows : lower + 2 * rows].astype(
                jnp.bfloat16
            )
            kept_lse = jnp.where(lane == h, lse[lower : lower + rows], kept_lse)
            sent_lse = jnp.where(
                remainder(lane, heads) == h, lse[lower + rows : lower + 2 * rows], sent_lse
            )
    kept_lse_ref[...] = kept_lse
    terms = jnp.zeros((rows, HD), jnp.float32)
    rest = sent_lse
    for n in range(3):
        term = rest.astype(jnp.bfloat16).astype(jnp.float32)
        terms = jnp.where(quotient(lane, heads) == n, term, terms)
        rest = rest - term
    sent_ref[:, pl.ds(heads * HD, HD)] = terms.astype(jnp.bfloat16)


def fetch_kernel(kept_lse_ref, w_out, kept_lse_out, w_out_ref, sems):
    copies = []
    tp = w_out_ref.shape[0]
    part = w_out_ref.shape[-1]
    me_tp = lax.axis_index("tp")
    for d in range(tp):
        place = pl.ds(pl.multiple_of((me_tp ^ d) * part, HD), part)
        copies.append(pltpu.make_async_copy(w_out.at[:, place], w_out_ref.at[d], sems.at[d]))
    for copy in copies:
        copy.start()
    kept_lse_out[...] = kept_lse_ref[...]
    for copy in copies:
        copy.wait()


def project_kernel(sizes, kept_ref, kept_lse_ref, got_ref, w_out_ref, *refs):
    steps, own, tp, heads, chunk = sizes
    outs = refs[:tp]
    (ctx_s,) = refs[tp:]
    part = outs[0].shape[-1]
    base = heads * HD
    lse_mine = kept_lse_ref[...]
    terms = got_ref[:, pl.ds(base, HD)].astype(jnp.float32)
    lse_got = terms + pltpu.roll(terms, HD - heads, 1) + pltpu.roll(terms, HD - 2 * heads, 1)
    top = jnp.maximum(lse_mine, lse_got)
    mine = jnp.exp(lse_mine - top)
    got = jnp.exp(lse_got - top)
    share = mine / (mine + got)
    for h in range(heads):
        cols = pl.ds(h * HD, HD)
        w = share[:, h : h + 1]
        ctx_s[:, cols] = (
            kept_ref[:, cols] * w + got_ref[:, cols].astype(jnp.float32) * (1.0 - w)
        ).astype(jnp.bfloat16)
    for d in list(range(1, tp)) + [0]:
        for lower in range(0, part, chunk):
            cols = pl.ds(lower, chunk)
            out = jnp.dot(ctx_s[...], w_out_ref[d, :, cols], preferred_element_type=jnp.float32)
            for s in range(steps):
                outs[d][s, :, cols] = out[s * own : (s + 1) * own].astype(outs[d].dtype)


def body(
    hidden_in,
    norm_gain,
    w_query,
    w_key,
    w_value,
    w_out,
    prompt_keys,
    prompt_values,
    gen_keys,
    gen_values,
    lengths,
    parents,
):
    steps, own, part = hidden_in.shape
    tp = lax.axis_size("tp")
    rows = steps * own
    width = w_query.shape[0]
    kv = w_key.shape[1] // HD
    group = w_query.shape[1] // w_key.shape[1]
    heads = kv * group
    history = gen_keys.shape[1]

    pieces = [
        across(hidden_in, b, t) for b in range(2) for t in range(tp) if (b, t) != (0, 0)
    ]

    def in_hbm(x):
        return pltpu.with_memory_space_constraint(x, pltpu.HBM)

    vmem = pl.BlockSpec(memory_space=pltpu.VMEM)
    hbm = pl.BlockSpec(memory_space=pltpu.HBM)
    params = pltpu.CompilerParams(vmem_limit_bytes=16 * 2**20)
    f32, bf16 = jnp.float32, jnp.bfloat16
    blocks = prompt_keys.shape[1] // history
    old = (blocks + own, history, kv * HD)
    near = max(kv // 2, 1) * group * HD
    loaded = pl.pallas_call(
        functools.partial(load_kernel, (steps, own, kv, group, history)),
        out_shape=(
            jax.ShapeDtypeStruct((1, width), f32),
            jax.ShapeDtypeStruct((rows, part), f32),
            jax.ShapeDtypeStruct((width, near), bf16),
            jax.ShapeDtypeStruct(w_key.shape, bf16),
            jax.ShapeDtypeStruct(old, bf16),
            jax.ShapeDtypeStruct(old, bf16),
            jax.ShapeDtypeStruct((2 * rows, HD), f32),
            jax.ShapeDtypeStruct((2 * rows, HD), f32),
            jax.ShapeDtypeStruct((group * 2 * rows, (blocks + own) * history + HD), f32),
        ),
        in_specs=[hbm] * 10,
        out_specs=(vmem,) * 9,
        scratch_shapes=[
            pltpu.SMEM(lengths.shape, jnp.int32),
            pltpu.SMEM(parents.shape, jnp.int32),
            pltpu.VMEM(hidden_in.shape, bf16),
            pltpu.SemaphoreType.DMA((16,)),
        ],
        compiler_params=params,
        name="load",
    )(
        *(
            in_hbm(x)
            for x in (
                lengths,
                parents,
                norm_gain[None, :],
                hidden_in,
                w_query,
                w_key,
                prompt_keys.reshape(blocks, history, kv * HD),
                prompt_values.reshape(blocks, history, kv * HD),
                gen_keys,
                gen_values,
            )
        )
    )

    kept, kept_lse, sent = pl.pallas_call(
        functools.partial(attend_kernel, (steps, own, tp, kv, group)),
        out_shape=(
            jax.ShapeDtypeStruct((rows, heads * HD), f32),
            jax.ShapeDtypeStruct((rows, HD), f32),
            jax.ShapeDtypeStruct((rows, heads * HD + HD), bf16),
        ),
        in_specs=[vmem] * 9 + [hbm] * 2 + [vmem] * (2 * tp - 1),
        out_specs=(vmem,) * 3,
        scratch_shapes=[
            pltpu.VMEM((2 * tp, rows, part), f32),
            pltpu.VMEM((2 * rows, width), bf16),
            pltpu.VMEM((heads * 2 * rows, kv * HD), bf16),
            pltpu.VMEM((width, near), bf16),
            pltpu.VMEM(w_value.shape, bf16),
            pltpu.SemaphoreType.DMA((2,)),
        ],
        compiler_params=params,
        name="attend",
    )(*loaded, in_hbm(w_query), in_hbm(w_value), *pieces)

    got = permute_by(sent, "req", 1)
    kept_lse, w_out_near = pl.pallas_call(
        fetch_kernel,
        out_shape=(
            jax.ShapeDtypeStruct((rows, HD), f32),
            jax.ShapeDtypeStruct((tp, heads * HD, part), bf16),
        ),
        in_specs=[vmem, hbm],
        out_specs=(vmem, vmem),
        scratch_shapes=[pltpu.SemaphoreType.DMA((tp,))],
        compiler_params=params,
        name="fetch",
    )(kept_lse, in_hbm(w_out))

    out_types = [f32] + [bf16] * (tp - 1)
    sums = pl.pallas_call(
        functools.partial(project_kernel, (steps, own, tp, heads, math.gcd(part, 512))),
        out_shape=tuple(jax.ShapeDtypeStruct((steps, own, part), kind) for kind in out_types),
        in_specs=[vmem] * 4,
        out_specs=(vmem,) * tp,
        scratch_shapes=[pltpu.VMEM((rows, heads * HD), bf16)],
        compiler_params=params,
        name="project",
    )(kept, kept_lse, got, w_out_near)
    total = sums[0]
    for t in range(1, tp):
        total = total + across(sums[t], 0, t).astype(f32)
    return total.astype(bf16)


def solution(mesh):
    in_specs = (
        P(None, "req", "tp"),
        P(),
        P(None, "tp"),
        P(None, "tp"),
        P(None, "tp"),
        P("tp", None),
        P("req", None, "tp"),
        P("req", None, "tp"),
        P("req", None, "tp"),
        P("req", None, "tp"),
        P(),
        P(),
    )
    out_specs = P(None, "req", "tp")
    return jax.shard_map(body, mesh=mesh, in_specs=in_specs, out_specs=out_specs, check_vma=False)
```

```python
import functools
import math

import jax
import jax.numpy as jnp
from jax import lax
from jax.experimental import pallas as pl
from jax.experimental.pallas import tpu as pltpu
from jax.sharding import PartitionSpec as P

HD = 128
BEAMS = 8

norm_eps = 1e-05
masked_score = -1e30
rope_base = 500000.0


def quotient(x, size):
    return x >> (size.bit_length() - 1) if size & (size - 1) == 0 else x // size


def remainder(x, size):
    return x & (size - 1) if size & (size - 1) == 0 else x % size


def permute_by(value, axis, distance):
    pairs = [(source, source ^ distance) for source in range(lax.axis_size(axis))]
    return lax.ppermute(value, axis, pairs)


def across(value, beam_distance, tp_distance):
    req, tp = lax.axis_size("req"), lax.axis_size("tp")
    pairs = [
        (r * tp + t, (r ^ beam_distance) * tp + (t ^ tp_distance))
        for r in range(req)
        for t in range(tp)
    ]
    return lax.ppermute(value, ("req", "tp"), pairs)


def lay_out(pieces, gain, x_s, xn_ref, first):
    steps, own, part = pieces[0].shape
    rows = steps * own
    me_tp = lax.axis_index("tp")
    total = jnp.zeros((rows, HD), jnp.float32)
    for t, piece in enumerate(pieces):
        column = pl.multiple_of((me_tp ^ t) * part, HD)
        for s in range(steps):
            x_s[t, pl.ds(s * own, own), :] = piece[s].astype(jnp.float32)
        mine = x_s[t]
        xn_ref[pl.ds(first, rows), pl.ds(column, part)] = (
            mine * gain[:, pl.ds(column, part)]
        ).astype(jnp.bfloat16)
        mine = mine * mine
        for c in range(part // HD):
            total = total + mine[:, c * HD : (c + 1) * HD]
    mean = jnp.sum(total, axis=-1, keepdims=True) / (part * len(pieces))
    return lax.rsqrt(mean + norm_eps)


def rotate(x, cosine, sine):
    return (x * cosine + pltpu.roll(x, HD // 2, 1) * sine).astype(jnp.bfloat16)


def load_kernel(
    sizes,
    lengths,
    parents,
    gain,
    hidden,
    wq,
    wk,
    wv,
    pk,
    pv,
    gk,
    gv,
    *refs,
):
    steps, own, tp, kv, group, history = sizes
    pieces = refs[: tp - 1]
    (
        gain_ref,
        xn_ref,
        scale_ref,
        wq_ref,
        keys_ref,
        values_ref,
        cosine_ref,
        sine_ref,
        bias_ref,
        lengths_s,
        parents_s,
        hidden_s,
        x_s,
        wk_s,
        wv_s,
        sems,
    ) = refs[tp - 1 :]
    rows = steps * own
    blocks = pk.shape[0]
    half_len = blocks * history
    device = lax.axis_index("req")
    request = device // 2
    parity = device % 2

    small = [
        (gain, gain_ref),
        (hidden, hidden_s),
        (lengths, lengths_s),
        (parents, parents_s),
    ]
    large = []
    for source, target, parts in ((wk, wk_s, 2), (wv, wv_s, 2)):
        size = source.shape[0] // parts
        for n in range(parts):
            place = pl.ds(n * size, size)
            large.append((source.at[place], target.at[place]))
    for prompt, gen, target in ((pk, gk, keys_ref), (pv, gv, values_ref)):
        large.append((prompt, target.at[pl.ds(0, blocks)]))
        large.append((gen, target.at[pl.ds(blocks, own)]))
    size = wq.shape[0] // 4
    for n in range(4):
        place = pl.ds(n * size, size)
        large.append((wq.at[place, pl.ds(0, wq_ref.shape[1])], wq_ref.at[place]))
    copies = [
        pltpu.make_async_copy(source, target, sems.at[n])
        for n, (source, target) in enumerate(small + large)
    ]
    for copy in copies:
        copy.start()
    large = copies[len(small) :]
    for copy in copies[: len(small)]:
        copy.wait()

    scale = lay_out((hidden_s, *pieces), gain_ref, x_s, xn_ref, 0)
    scale_ref[...] = jnp.broadcast_to(scale, scale_ref.shape)

    length = lengths_s[request]
    row = lax.broadcasted_iota(jnp.int32, (rows, HD), 0)
    lane = lax.broadcasted_iota(jnp.int32, (rows, HD), 1)
    half_dim = HD // 2
    inverse = jnp.exp(
        remainder(lane, half_dim).astype(jnp.float32) * (-math.log(rope_base) / half_dim)
    )
    angle = (length + history + quotient(row, own)).astype(jnp.float32) * inverse
    sine = jnp.sin(angle)
    sine = jnp.where(lane < half_dim, -sine, sine)
    cosine = jnp.cos(angle)
    cosine_ref[...] = cosine
    sine_ref[...] = sine

    count = group * 2 * rows

    def parent_of(s, beam):
        out = jnp.zeros_like(beam)
        for j in range(BEAMS):
            out = jnp.where(beam == j, parents_s[s, request * BEAMS + j], out)
        return out

    row = remainder(lax.broadcasted_iota(jnp.int32, (count, HD), 0), 2 * rows)
    row_step = quotient(remainder(row, rows), own)
    row_parity = jnp.where(row < rows, parity, 1 - parity)
    beam = row_parity * own + remainder(row, own)
    ancestors = [None] * steps
    at = beam
    for s in reversed(range(steps)):
        if s < steps - 1:
            at = jnp.where(row_step > s, parent_of(s + 1, at), beam)
        ancestors[s] = jnp.where(row_step >= s, at, -1)
    origin = parent_of(0, at)
    lane = lax.broadcasted_iota(jnp.int32, (count, HD), 1)

    for c in range(half_len // HD):
        place = parity * half_len + c * HD + lane
        bias_ref[:, pl.ds(c * HD, HD)] = jnp.where(place < length, 0.0, masked_score)
    for c in range(own * history // HD):
        key_beam = parity * own + quotient(c * HD + lane, history)
        bias_ref[:, pl.ds(half_len + c * HD, HD)] = jnp.where(
            key_beam == origin, 0.0, masked_score
        )
    new_bias = jnp.full((count, HD), masked_score, jnp.float32)
    for s in range(steps):
        hit = (quotient(lane, own) == s) & (
            ancestors[s] == parity * own + remainder(lane, own)
        )
        new_bias = jnp.where(hit, 0.0, new_bias)
    bias_ref[:, pl.ds(half_len + own * history, HD)] = new_bias

    cosine = cosine * scale
    sine = sine * scale
    new = pl.ds(blocks + own, keys_ref.shape[0] - blocks - own)
    for first, w_s, target, finish in (
        (0, wk_s, keys_ref, lambda x: rotate(x, cosine, sine)),
        (2, wv_s, values_ref, lambda x: (x * scale).astype(jnp.bfloat16)),
    ):
        target[new] = jnp.zeros((HD // history, history, kv * HD), jnp.bfloat16)
        for copy in large[first : first + 2]:
            copy.wait()
        fresh = jnp.dot(xn_ref[...], w_s[...], preferred_element_type=jnp.float32)
        for g in range(kv):
            target[blocks + own, pl.ds(0, rows), pl.ds(g * HD, HD)] = finish(
                fresh[:, g * HD : (g + 1) * HD]
            )
    for copy in large[4:]:
        copy.wait()


def attend_kernel(
    sizes,
    gain_ref,
    xn_ref,
    scale_ref,
    wq_ref,
    keys_ref,
    values_ref,
    cosine_ref,
    sine_ref,
    bias_ref,
    wq,
    *refs,
):
    steps, own, tp, kv, group = sizes
    pieces = refs[:tp]
    kept_ref, kept_lse_ref, sent_ref, x_s, xn_s, wq_s, sems = refs[tp:]
    rows = steps * own
    heads = kv * group
    keys_count = keys_ref.shape[0] * keys_ref.shape[1]
    near = wq_ref.shape[1]
    copies = []
    if near < wq.shape[1]:
        size = group * HD
        for n in range((wq.shape[1] - near) // size):
            copies.append(
                pltpu.make_async_copy(
                    wq.at[:, pl.ds(near + n * size, size)], wq_s.at[n], sems.at[n]
                )
            )
    for copy in copies:
        copy.start()

    xn_s[pl.ds(0, rows), :] = xn_ref[...]
    scale = lay_out(pieces, gain_ref, x_s, xn_s, rows)
    scale = jnp.concatenate([scale_ref[...], jnp.broadcast_to(scale, (rows, HD))], axis=0)
    scale = scale * HD**-0.5
    cosine = jnp.concatenate([cosine_ref[...]] * 2, axis=0) * scale
    sine = jnp.concatenate([sine_ref[...]] * 2, axis=0) * scale

    def score(g):
        lower = g * group * HD
        if lower < near:
            w = wq_ref[:, pl.ds(lower, group * HD)]
        else:
            n = (lower - near) // (group * HD)
            copies[n].wait()
            w = wq_s[n]
        q = jnp.dot(xn_s[...], w, preferred_element_type=jnp.float32)
        q = jnp.concatenate(
            [rotate(q[:, j * HD : (j + 1) * HD], cosine, sine) for j in range(group)], axis=0
        )
        keys = keys_ref[:, :, pl.ds(g * HD, HD)].reshape(keys_count, HD)
        return (
            lax.dot_general(q, keys, (((1,), (1,)), ((), ())), preferred_element_type=jnp.float32)
            + bias_ref[...]
        )

    ones = jnp.ones((keys_count, HD), jnp.bfloat16)

    def mix(g, scores):
        most = scores[:, :HD]
        for c in range(1, keys_count // HD):
            most = jnp.maximum(most, scores[:, c * HD : (c + 1) * HD])
        top = jnp.max(most, axis=-1, keepdims=True)
        values = values_ref[:, :, pl.ds(g * HD, HD)].reshape(keys_count, HD)
        mixed = jnp.dot(
            jnp.exp(scores - top).astype(jnp.bfloat16),
            jnp.concatenate([values, ones], axis=1),
            preferred_element_type=jnp.float32,
        )
        return mixed, top

    results, scores = [], None
    for g in range(kv):
        after = score(g)
        if g > 0:
            results.append(mix(g - 1, scores))
        scores = after
    results.append(mix(kv - 1, scores))

    lane = lax.broadcasted_iota(jnp.int32, (rows, HD), 1)
    kept_lse = jnp.zeros((rows, HD), jnp.float32)
    sent_lse = jnp.zeros((rows, HD), jnp.float32)
    for g, (mixed, top) in enumerate(results):
        total = mixed[:, HD:]
        mixed = mixed[:, :HD] / total
        lse = top + jnp.log(total)
        for j in range(group):
            h = g * group + j
            lower = j * 2 * rows
            kept_ref[:, pl.ds(h * HD, HD)] = mixed[lower : lower + rows]
            sent_ref[:, pl.ds(h * HD, HD)] = mixed[lower + rows : lower + 2 * rows].astype(
                jnp.bfloat16
            )
            kept_lse = jnp.where(lane == h, lse[lower : lower + rows], kept_lse)
            sent_lse = jnp.where(
                remainder(lane, heads) == h, lse[lower + rows : lower + 2 * rows], sent_lse
            )
    kept_lse_ref[...] = kept_lse
    terms = jnp.zeros((rows, HD), jnp.float32)
    rest = sent_lse
    for n in range(3):
        term = rest.astype(jnp.bfloat16).astype(jnp.float32)
        terms = jnp.where(quotient(lane, heads) == n, term, terms)
        rest = rest - term
    sent_ref[:, pl.ds(heads * HD, HD)] = terms.astype(jnp.bfloat16)


def fetch_kernel(kept_lse_ref, w_out, kept_lse_out, w_out_ref, sems):
    copies = []
    tp = w_out_ref.shape[0]
    part = w_out_ref.shape[-1]
    me_tp = lax.axis_index("tp")
    for d in range(tp):
        place = pl.ds(pl.multiple_of((me_tp ^ d) * part, HD), part)
        copies.append(pltpu.make_async_copy(w_out.at[:, place], w_out_ref.at[d], sems.at[d]))
    for copy in copies:
        copy.start()
    kept_lse_out[...] = kept_lse_ref[...]
    for copy in copies:
        copy.wait()


def project_kernel(sizes, kept_ref, kept_lse_ref, got_ref, w_out_ref, *refs):
    steps, own, tp, heads, chunk = sizes
    outs = refs[:tp]
    (ctx_s,) = refs[tp:]
    part = outs[0].shape[-1]
    base = heads * HD
    lse_mine = kept_lse_ref[...]
    terms = got_ref[:, pl.ds(base, HD)].astype(jnp.float32)
    lse_got = terms + pltpu.roll(terms, HD - heads, 1) + pltpu.roll(terms, HD - 2 * heads, 1)
    top = jnp.maximum(lse_mine, lse_got)
    mine = jnp.exp(lse_mine - top)
    got = jnp.exp(lse_got - top)
    share = mine / (mine + got)
    for h in range(heads):
        cols = pl.ds(h * HD, HD)
        w = share[:, h : h + 1]
        ctx_s[:, cols] = (
            kept_ref[:, cols] * w + got_ref[:, cols].astype(jnp.float32) * (1.0 - w)
        ).astype(jnp.bfloat16)
    for d in list(range(1, tp)) + [0]:
        for lower in range(0, part, chunk):
            cols = pl.ds(lower, chunk)
            out = jnp.dot(ctx_s[...], w_out_ref[d, :, cols], preferred_element_type=jnp.float32)
            for s in range(steps):
                outs[d][s, :, cols] = out[s * own : (s + 1) * own].astype(outs[d].dtype)


def body(
    hidden_in,
    norm_gain,
    w_query,
    w_key,
    w_value,
    w_out,
    prompt_keys,
    prompt_values,
    gen_keys,
    gen_values,
    lengths,
    parents,
):
    steps, own, part = hidden_in.shape
    tp = lax.axis_size("tp")
    rows = steps * own
    width = w_query.shape[0]
    kv = w_key.shape[1] // HD
    group = w_query.shape[1] // w_key.shape[1]
    heads = kv * group
    history = gen_keys.shape[1]

    near_pieces = [across(hidden_in, 0, t) for t in range(1, tp)]
    far_pieces = [across(hidden_in, 1, t) for t in range(tp)]

    def in_hbm(x):
        return pltpu.with_memory_space_constraint(x, pltpu.HBM)

    vmem = pl.BlockSpec(memory_space=pltpu.VMEM)
    hbm = pl.BlockSpec(memory_space=pltpu.HBM)
    params = pltpu.CompilerParams(vmem_limit_bytes=16 * 2**20)
    f32, bf16 = jnp.float32, jnp.bfloat16
    blocks = prompt_keys.shape[1] // history
    cache = (blocks + own + HD // history, history, kv * HD)
    near = max(kv // 2, 1) * group * HD
    loaded = pl.pallas_call(
        functools.partial(load_kernel, (steps, own, tp, kv, group, history)),
        out_shape=(
            jax.ShapeDtypeStruct((1, width), f32),
            jax.ShapeDtypeStruct((rows, width), bf16),
            jax.ShapeDtypeStruct((rows, HD), f32),
            jax.ShapeDtypeStruct((width, near), bf16),
            jax.ShapeDtypeStruct(cache, bf16),
            jax.ShapeDtypeStruct(cache, bf16),
            jax.ShapeDtypeStruct((rows, HD), f32),
            jax.ShapeDtypeStruct((rows, HD), f32),
            jax.ShapeDtypeStruct((group * 2 * rows, cache[0] * history), f32),
        ),
        in_specs=[hbm] * 11 + [vmem] * (tp - 1),
        out_specs=(vmem,) * 9,
        scratch_shapes=[
            pltpu.SMEM(lengths.shape, jnp.int32),
            pltpu.SMEM(parents.shape, jnp.int32),
            pltpu.VMEM(hidden_in.shape, bf16),
            pltpu.VMEM((tp, rows, part), f32),
            pltpu.VMEM(w_key.shape, bf16),
            pltpu.VMEM(w_value.shape, bf16),
            pltpu.SemaphoreType.DMA((16,)),
        ],
        compiler_params=params,
        name="load",
    )(
        *(
            in_hbm(x)
            for x in (
                lengths,
                parents,
                norm_gain[None, :],
                hidden_in,
                w_query,
                w_key,
                w_value,
                prompt_keys.reshape(blocks, history, kv * HD),
                prompt_values.reshape(blocks, history, kv * HD),
                gen_keys,
                gen_values,
            )
        ),
        *near_pieces,
    )

    kept, kept_lse, sent = pl.pallas_call(
        functools.partial(attend_kernel, (steps, own, tp, kv, group)),
        out_shape=(
            jax.ShapeDtypeStruct((rows, heads * HD), f32),
            jax.ShapeDtypeStruct((rows, HD), f32),
            jax.ShapeDtypeStruct((rows, heads * HD + HD), bf16),
        ),
        in_specs=[vmem] * 9 + [hbm] + [vmem] * tp,
        out_specs=(vmem,) * 3,
        scratch_shapes=[
            pltpu.VMEM((tp, rows, part), f32),
            pltpu.VMEM((2 * rows, width), bf16),
            pltpu.VMEM((kv, width, group * HD), bf16),
            pltpu.SemaphoreType.DMA((kv,)),
        ],
        compiler_params=params,
        name="attend",
    )(*loaded, in_hbm(w_query), *far_pieces)

    got = permute_by(sent, "req", 1)
    kept_lse, w_out_near = pl.pallas_call(
        fetch_kernel,
        out_shape=(
            jax.ShapeDtypeStruct((rows, HD), f32),
            jax.ShapeDtypeStruct((tp, heads * HD, part), bf16),
        ),
        in_specs=[vmem, hbm],
        out_specs=(vmem, vmem),
        scratch_shapes=[pltpu.SemaphoreType.DMA((tp,))],
        compiler_params=params,
        name="fetch",
    )(kept_lse, in_hbm(w_out))

    out_types = [f32] + [bf16] * (tp - 1)
    sums = pl.pallas_call(
        functools.partial(project_kernel, (steps, own, tp, heads, math.gcd(part, 512))),
        out_shape=tuple(jax.ShapeDtypeStruct((steps, own, part), kind) for kind in out_types),
        in_specs=[vmem] * 4,
        out_specs=(vmem,) * tp,
        scratch_shapes=[pltpu.VMEM((rows, heads * HD), bf16)],
        compiler_params=params,
        name="project",
    )(kept, kept_lse, got, w_out_near)
    total = sums[0]
    for t in range(1, tp):
        total = total + across(sums[t], 0, t).astype(f32)
    return total.astype(bf16)


def solution(mesh):
    in_specs = (
        P(None, "req", "tp"),
        P(),
        P(None, "tp"),
        P(None, "tp"),
        P(None, "tp"),
        P("tp", None),
        P("req", None, "tp"),
        P("req", None, "tp"),
        P("req", None, "tp"),
        P("req", None, "tp"),
        P(),
        P(),
    )
    out_specs = P(None, "req", "tp")
    return jax.shard_map(body, mesh=mesh, in_specs=in_specs, out_specs=out_specs, check_vma=False)
```

```python
import functools
import math

import jax
import jax.numpy as jnp
from jax import lax
from jax.experimental import pallas as pl
from jax.experimental.pallas import tpu as pltpu
from jax.sharding import PartitionSpec as P

HD = 128
BEAMS = 8

norm_eps = 1e-05
masked_score = -1e30
rope_base = 500000.0


def quotient(x, size):
    return x >> (size.bit_length() - 1) if size & (size - 1) == 0 else x // size


def remainder(x, size):
    return x & (size - 1) if size & (size - 1) == 0 else x % size


def permute_by(value, axis, distance):
    pairs = [(source, source ^ distance) for source in range(lax.axis_size(axis))]
    return lax.ppermute(value, axis, pairs)


def across(value, beam_distance, tp_distance):
    req, tp = lax.axis_size("req"), lax.axis_size("tp")
    pairs = [
        (r * tp + t, (r ^ beam_distance) * tp + (t ^ tp_distance))
        for r in range(req)
        for t in range(tp)
    ]
    return lax.ppermute(value, ("req", "tp"), pairs)


def lay_out(pieces, gain, x_s, xn_ref, first):
    steps, own, part = pieces[0].shape
    rows = steps * own
    me_tp = lax.axis_index("tp")
    total = jnp.zeros((rows, HD), jnp.float32)
    for t, piece in enumerate(pieces):
        column = pl.multiple_of((me_tp ^ t) * part, HD)
        for s in range(steps):
            x_s[t, pl.ds(s * own, own), :] = piece[s].astype(jnp.float32)
        mine = x_s[t]
        xn_ref[pl.ds(first, rows), pl.ds(column, part)] = (
            mine * gain[:, pl.ds(column, part)]
        ).astype(jnp.bfloat16)
        mine = mine * mine
        for c in range(part // HD):
            total = total + mine[:, c * HD : (c + 1) * HD]
    mean = jnp.sum(total, axis=-1, keepdims=True) / (part * len(pieces))
    return lax.rsqrt(mean + norm_eps)


def rotate(x, cosine, sine):
    return (x * cosine + pltpu.roll(x, HD // 2, 1) * sine).astype(jnp.bfloat16)


def load_kernel(
    sizes,
    lengths,
    parents,
    gain,
    hidden,
    wq,
    wk,
    wv,
    pk,
    pv,
    gk,
    gv,
    *refs,
):
    steps, own, tp, kv, group, history, packed = sizes
    pieces = refs[: tp - 1]
    (
        gain_ref,
        xn_ref,
        scale_ref,
        wq_ref,
        keys_ref,
        values_ref,
        cosine_ref,
        sine_ref,
        bias_ref,
        lengths_s,
        parents_s,
        hidden_s,
        x_s,
        wk_s,
        wv_s,
        values_s,
        sems,
    ) = refs[tp - 1 :]
    rows = steps * own
    blocks = pk.shape[0]
    half_len = blocks * history
    device = lax.axis_index("req")
    request = device // 2
    parity = device % 2

    small = [
        (gain, gain_ref),
        (hidden, hidden_s),
        (lengths, lengths_s),
        (parents, parents_s),
    ]
    old = blocks + own
    large = [(pv, values_s.at[pl.ds(0, blocks)]), (gv, values_s.at[pl.ds(blocks, own)])]
    for source, target, parts in ((wk, wk_s, 2), (wv, wv_s, 2)):
        size = source.shape[0] // parts
        for n in range(parts):
            place = pl.ds(n * size, size)
            large.append((source.at[place], target.at[place]))
    large += [(pk, keys_ref.at[pl.ds(0, blocks)]), (gk, keys_ref.at[pl.ds(blocks, own)])]
    size = wq.shape[0] // 4
    for n in range(4):
        place = pl.ds(n * size, size)
        large.append((wq.at[place, pl.ds(0, wq_ref.shape[1])], wq_ref.at[place]))
    copies = [
        pltpu.make_async_copy(source, target, sems.at[n])
        for n, (source, target) in enumerate(small + large)
    ]
    for copy in copies:
        copy.start()
    large = copies[len(small) :]
    for copy in copies[: len(small)]:
        copy.wait()

    scale = lay_out((hidden_s, *pieces), gain_ref, x_s, xn_ref, 0)
    scale_ref[...] = jnp.broadcast_to(scale, scale_ref.shape)

    length = lengths_s[request]
    half_dim = HD // 2
    fall = -math.log(rope_base) / half_dim

    def angles(step, place):
        return (length + history + step).astype(jnp.float32) * jnp.exp(
            place.astype(jnp.float32) * fall
        )

    row = lax.broadcasted_iota(jnp.int32, (rows, HD), 0)
    lane = lax.broadcasted_iota(jnp.int32, (rows, HD), 1)
    angle = angles(quotient(row, own), remainder(lane, half_dim))
    key_cosine = jnp.cos(angle) * scale
    key_sine = jnp.sin(angle) * scale
    key_sine = jnp.where(lane < half_dim, -key_sine, key_sine)

    lanes = packed * group * 2 * rows
    place = lax.broadcasted_iota(jnp.int32, (half_dim, lanes), 0)
    lane = lax.broadcasted_iota(jnp.int32, (half_dim, lanes), 1)
    angle = angles(quotient(remainder(lane, rows), own), place)
    cosine_ref[...] = jnp.cos(angle)
    sine_ref[...] = jnp.sin(angle)

    def parent_of(s, beam):
        out = jnp.zeros_like(beam)
        for j in range(BEAMS):
            out = jnp.where(beam == j, parents_s[s, request * BEAMS + j], out)
        return out

    row = remainder(lax.broadcasted_iota(jnp.int32, (8, lanes), 1), 2 * rows)
    row_step = quotient(remainder(row, rows), own)
    row_parity = jnp.where(row < rows, parity, 1 - parity)
    beam = row_parity * own + remainder(row, own)
    ancestors = [None] * steps
    at = beam
    for s in reversed(range(steps)):
        if s < steps - 1:
            at = jnp.where(row_step > s, parent_of(s + 1, at), beam)
        ancestors[s] = jnp.where(row_step >= s, at, -1)
    origin = parent_of(0, at)

    place = parity * half_len + lax.broadcasted_iota(jnp.int32, (half_len, lanes), 0)
    bias_ref[pl.ds(0, half_len), :] = jnp.where(place < length, 0.0, masked_score)
    for n in range(own):
        seen = jnp.where(origin == parity * own + n, 0.0, masked_score)
        for c in range(0, history, 8):
            bias_ref[pl.ds(half_len + n * history + c, 8), :] = seen
    sublane = lax.broadcasted_iota(jnp.int32, (8, lanes), 0)
    for c in range(0, HD, 8):
        seen = jnp.full((8, lanes), masked_score, jnp.float32)
        for s in range(c // own, min((c + 8) // own, steps)):
            hit = (quotient(c + sublane, own) == s) & (
                ancestors[s] == parity * own + remainder(c + sublane, own)
            )
            seen = jnp.where(hit, 0.0, seen)
        bias_ref[pl.ds(old * history + c, 8), :] = seen

    for copy in large[:2]:
        copy.wait()
    values_ref[:, pl.ds(0, old * history)] = values_s[...].reshape(old * history, kv * HD).T
    keys_ref[pl.ds(old, HD // history)] = jnp.zeros(
        (HD // history, history, kv * HD), jnp.bfloat16
    )
    for copy in large[2:4]:
        copy.wait()
    fresh = jnp.dot(xn_ref[...], wk_s[...], preferred_element_type=jnp.float32)
    for g in range(kv):
        cols = pl.ds(g * HD, HD)
        keys_ref[old, pl.ds(0, rows), cols] = rotate(
            fresh[:, g * HD : (g + 1) * HD], key_cosine, key_sine
        )
    for copy in large[4:6]:
        copy.wait()
    fresh = jnp.dot(xn_ref[...], wv_s[...], preferred_element_type=jnp.float32) * scale
    fresh = jnp.concatenate(
        [fresh, jnp.zeros((HD - rows, kv * HD), jnp.float32)], axis=0
    ).astype(jnp.bfloat16)
    values_ref[:, pl.ds(old * history, HD)] = fresh.T
    for copy in large[6:]:
        copy.wait()


def attend_kernel(
    sizes,
    gain_ref,
    xn_ref,
    scale_ref,
    wq_ref,
    keys_ref,
    values_ref,
    cosine_ref,
    sine_ref,
    bias_ref,
    wq,
    *refs,
):
    steps, own, tp, kv, group, packed = sizes
    pieces = refs[:tp]
    kept_ref, kept_lse_ref, sent_ref, x_s, xn_s, wq_s, sems = refs[tp:]
    rows = steps * own
    packs = kv // packed
    keys_count = keys_ref.shape[0] * keys_ref.shape[1]
    near = wq_ref.shape[1]
    size = packed * group * HD
    copies = [
        pltpu.make_async_copy(
            wq.at[:, pl.ds(near + n * size, size)], wq_s.at[n], sems.at[n]
        )
        for n in range((wq.shape[1] - near) // size)
    ]
    for copy in copies:
        copy.start()

    xn_s[pl.ds(0, rows), :] = xn_ref[...]
    scale = lay_out(pieces, gain_ref, x_s, xn_s, rows)
    scale = jnp.concatenate([scale_ref[...], jnp.broadcast_to(scale, (rows, HD))], axis=0)
    scale = scale * HD**-0.5
    lanes = size // HD * 2 * rows
    lane = lax.broadcasted_iota(jnp.int32, (HD, lanes), 1)
    owner = quotient(lane, group * 2 * rows)

    def score(p):
        if p * size < near:
            w = wq_ref[:, pl.ds(p * size, size)]
        else:
            n = p - near // size
            copies[n].wait()
            w = wq_s[n]
        q = jnp.dot(xn_s[...], w, preferred_element_type=jnp.float32)
        q = jnp.concatenate(
            [q[:, j * HD : (j + 1) * HD] * scale for j in range(packed * group)], axis=0
        ).T
        cosine, sine = cosine_ref[...], sine_ref[...]
        first, second = q[: HD // 2], q[HD // 2 :]
        q = jnp.concatenate(
            [first * cosine - second * sine, second * cosine + first * sine], axis=0
        )
        q = jnp.concatenate([jnp.where(owner == i, q, 0.0) for i in range(packed)], axis=0)
        keys = keys_ref[:, :, pl.ds(p * packed * HD, packed * HD)]
        return (
            jnp.dot(
                keys.reshape(keys_count, packed * HD),
                q.astype(jnp.bfloat16),
                preferred_element_type=jnp.float32,
            )
            + bias_ref[...]
        )

    def mix(p, scores):
        top = jnp.max(scores, axis=0, keepdims=True)
        powers = jnp.exp(scores - top)
        total = jnp.sum(powers, axis=0, keepdims=True)
        mixed = jnp.dot(
            values_ref[pl.ds(p * packed * HD, packed * HD), :],
            powers.astype(jnp.bfloat16),
            preferred_element_type=jnp.float32,
        )
        out = mixed[:HD]
        for i in range(1, packed):
            out = jnp.where(owner == i, mixed[i * HD : (i + 1) * HD], out)
        out = (out * (1.0 / total)).T
        for j in range(packed * group):
            cols = pl.ds((p * packed * group + j) * HD, HD)
            lower = j * 2 * rows
            kept_ref[:, cols] = out[lower : lower + rows]
            sent_ref[:, cols] = out[lower + rows : lower + 2 * rows].astype(jnp.bfloat16)
        lse = top + jnp.log(total)
        if lanes < HD:
            lse = jnp.concatenate([lse, jnp.zeros((1, HD - lanes), jnp.float32)], axis=1)
        return lse

    results, scores = [], None
    for p in range(packs):
        after = score(p)
        if p > 0:
            results.append(mix(p - 1, scores))
        scores = after
    results.append(mix(packs - 1, scores))

    sublane = lax.broadcasted_iota(jnp.int32, (rows, HD), 0)
    kept_lse = jnp.zeros((rows, HD), jnp.float32)
    terms = jnp.zeros((rows, HD), jnp.float32)
    for p, lse in enumerate(results):
        kept_lse = jnp.where(sublane == p, lse, kept_lse)
        rest = lse
        for n in range(3):
            term = rest.astype(jnp.bfloat16).astype(jnp.float32)
            terms = jnp.where(sublane == n * packs + p, term, terms)
            rest = rest - term
    kept_lse_ref[...] = kept_lse
    sent_ref[:, pl.ds(kv * group * HD, HD)] = terms.astype(jnp.bfloat16)


def fetch_kernel(kept_lse_ref, w_out, kept_lse_out, w_out_ref, sems):
    copies = []
    tp = w_out_ref.shape[0]
    part = w_out_ref.shape[-1]
    me_tp = lax.axis_index("tp")
    for d in range(tp):
        place = pl.ds(pl.multiple_of((me_tp ^ d) * part, HD), part)
        copies.append(pltpu.make_async_copy(w_out.at[:, place], w_out_ref.at[d], sems.at[d]))
    for copy in copies:
        copy.start()
    kept_lse_out[...] = kept_lse_ref[...]
    for copy in copies:
        copy.wait()


def project_kernel(sizes, kept_ref, kept_lse_ref, got_ref, w_out_ref, *refs):
    steps, own, tp, heads, packs, chunk = sizes
    outs = refs[:tp]
    (ctx_s,) = refs[tp:]
    rows = steps * own
    part = outs[0].shape[-1]
    base = heads * HD
    terms = got_ref[:, pl.ds(base, HD)].astype(jnp.float32)
    lse_got = sum(terms[n * packs : (n + 1) * packs] for n in range(3))
    lse_got = pltpu.roll(jnp.concatenate([lse_got] * (8 // packs), axis=0), HD - rows, 1)
    lse_mine = kept_lse_ref[pl.ds(0, 8), :]
    top = jnp.maximum(lse_mine, lse_got)
    mine = jnp.exp(lse_mine - top)
    got = jnp.exp(lse_got - top)
    share = (mine / (mine + got)).T
    for h in range(heads):
        cols = pl.ds(h * HD, HD)
        p, j = divmod(h, heads // packs)
        w = share[j * 2 * rows : j * 2 * rows + rows, p : p + 1]
        ctx_s[:, cols] = (
            kept_ref[:, cols] * w + got_ref[:, cols].astype(jnp.float32) * (1.0 - w)
        ).astype(jnp.bfloat16)
    for d in list(range(1, tp)) + [0]:
        for lower in range(0, part, chunk):
            cols = pl.ds(lower, chunk)
            out = jnp.dot(ctx_s[...], w_out_ref[d, :, cols], preferred_element_type=jnp.float32)
            for s in range(steps):
                outs[d][s, :, cols] = out[s * own : (s + 1) * own].astype(outs[d].dtype)


def body(
    hidden_in,
    norm_gain,
    w_query,
    w_key,
    w_value,
    w_out,
    prompt_keys,
    prompt_values,
    gen_keys,
    gen_values,
    lengths,
    parents,
):
    steps, own, part = hidden_in.shape
    tp = lax.axis_size("tp")
    rows = steps * own
    width = w_query.shape[0]
    kv = w_key.shape[1] // HD
    group = w_query.shape[1] // w_key.shape[1]
    heads = kv * group
    history = gen_keys.shape[1]

    near_pieces = [across(hidden_in, 0, t) for t in range(1, tp)]
    far_pieces = [across(hidden_in, 1, t) for t in range(tp)]

    def in_hbm(x):
        return pltpu.with_memory_space_constraint(x, pltpu.HBM)

    vmem = pl.BlockSpec(memory_space=pltpu.VMEM)
    hbm = pl.BlockSpec(memory_space=pltpu.HBM)
    params = pltpu.CompilerParams(vmem_limit_bytes=16 * 2**20)
    f32, bf16 = jnp.float32, jnp.bfloat16
    blocks = prompt_keys.shape[1] // history
    cache = (blocks + own + HD // history, history, kv * HD)
    packed = 2 - kv % 2
    packs = kv // packed
    near = max(packs // 2, 1) * packed * group * HD
    lanes = packed * group * 2 * rows
    loaded = pl.pallas_call(
        functools.partial(load_kernel, (steps, own, tp, kv, group, history, packed)),
        out_shape=(
            jax.ShapeDtypeStruct((1, width), f32),
            jax.ShapeDtypeStruct((rows, width), bf16),
            jax.ShapeDtypeStruct((rows, HD), f32),
            jax.ShapeDtypeStruct((width, near), bf16),
            jax.ShapeDtypeStruct(cache, bf16),
            jax.ShapeDtypeStruct((kv * HD, cache[0] * history), bf16),
            jax.ShapeDtypeStruct((HD // 2, lanes), f32),
            jax.ShapeDtypeStruct((HD // 2, lanes), f32),
            jax.ShapeDtypeStruct((cache[0] * history, lanes), f32),
        ),
        in_specs=[hbm] * 11 + [vmem] * (tp - 1),
        out_specs=(vmem,) * 9,
        scratch_shapes=[
            pltpu.SMEM(lengths.shape, jnp.int32),
            pltpu.SMEM(parents.shape, jnp.int32),
            pltpu.VMEM(hidden_in.shape, bf16),
            pltpu.VMEM((tp, rows, part), f32),
            pltpu.VMEM(w_key.shape, bf16),
            pltpu.VMEM(w_value.shape, bf16),
            pltpu.VMEM((blocks + own, history, kv * HD), bf16),
            pltpu.SemaphoreType.DMA((16,)),
        ],
        compiler_params=params,
        name="load",
    )(
        *(
            in_hbm(x)
            for x in (
                lengths,
                parents,
                norm_gain[None, :],
                hidden_in,
                w_query,
                w_key,
                w_value,
                prompt_keys.reshape(blocks, history, kv * HD),
                prompt_values.reshape(blocks, history, kv * HD),
                gen_keys,
                gen_values,
            )
        ),
        *near_pieces,
    )

    kept, kept_lse, sent = pl.pallas_call(
        functools.partial(attend_kernel, (steps, own, tp, kv, group, packed)),
        out_shape=(
            jax.ShapeDtypeStruct((rows, heads * HD), f32),
            jax.ShapeDtypeStruct((rows, HD), f32),
            jax.ShapeDtypeStruct((rows, heads * HD + HD), bf16),
        ),
        in_specs=[vmem] * 9 + [hbm] + [vmem] * tp,
        out_specs=(vmem,) * 3,
        scratch_shapes=[
            pltpu.VMEM((tp, rows, part), f32),
            pltpu.VMEM((2 * rows, width), bf16),
            pltpu.VMEM((packs, width, packed * group * HD), bf16),
            pltpu.SemaphoreType.DMA((kv,)),
        ],
        compiler_params=params,
        name="attend",
    )(*loaded, in_hbm(w_query), *far_pieces)

    got = permute_by(sent, "req", 1)
    kept_lse, w_out_near = pl.pallas_call(
        fetch_kernel,
        out_shape=(
            jax.ShapeDtypeStruct((rows, HD), f32),
            jax.ShapeDtypeStruct((tp, heads * HD, part), bf16),
        ),
        in_specs=[vmem, hbm],
        out_specs=(vmem, vmem),
        scratch_shapes=[pltpu.SemaphoreType.DMA((tp,))],
        compiler_params=params,
        name="fetch",
    )(kept_lse, in_hbm(w_out))

    out_types = [f32] + [bf16] * (tp - 1)
    sums = pl.pallas_call(
        functools.partial(project_kernel, (steps, own, tp, heads, packs, math.gcd(part, 512))),
        out_shape=tuple(jax.ShapeDtypeStruct((steps, own, part), kind) for kind in out_types),
        in_specs=[vmem] * 4,
        out_specs=(vmem,) * tp,
        scratch_shapes=[pltpu.VMEM((rows, heads * HD), bf16)],
        compiler_params=params,
        name="project",
    )(kept, kept_lse, got, w_out_near)
    total = sums[0]
    for t in range(1, tp):
        total = total + across(sums[t], 0, t).astype(f32)
    return total.astype(bf16)


def solution(mesh):
    in_specs = (
        P(None, "req", "tp"),
        P(),
        P(None, "tp"),
        P(None, "tp"),
        P(None, "tp"),
        P("tp", None),
        P("req", None, "tp"),
        P("req", None, "tp"),
        P("req", None, "tp"),
        P("req", None, "tp"),
        P(),
        P(),
    )
    out_specs = P(None, "req", "tp")
    return jax.shard_map(body, mesh=mesh, in_specs=in_specs, out_specs=out_specs, check_vma=False)
```

```python
import functools
import math

import jax
import jax.numpy as jnp
from jax import lax
from jax.experimental import pallas as pl
from jax.experimental.pallas import tpu as pltpu
from jax.sharding import PartitionSpec as P

HD = 128
BEAMS = 8

norm_eps = 1e-05
masked_score = -1e30
rope_base = 500000.0


def quotient(x, size):
    return x >> (size.bit_length() - 1) if size & (size - 1) == 0 else x // size


def remainder(x, size):
    return x & (size - 1) if size & (size - 1) == 0 else x % size


def permute_by(value, axis, distance):
    pairs = [(source, source ^ distance) for source in range(lax.axis_size(axis))]
    return lax.ppermute(value, axis, pairs)


def across(value, beam_distance, tp_distance):
    req, tp = lax.axis_size("req"), lax.axis_size("tp")
    pairs = [
        (r * tp + t, (r ^ beam_distance) * tp + (t ^ tp_distance))
        for r in range(req)
        for t in range(tp)
    ]
    return lax.ppermute(value, ("req", "tp"), pairs)


def lay_out(pieces, gain, x_s, xn_ref, first):
    steps, own, part = pieces[0].shape
    rows = steps * own
    me_tp = lax.axis_index("tp")
    total = jnp.zeros((rows, HD), jnp.float32)
    for t, piece in enumerate(pieces):
        column = pl.multiple_of((me_tp ^ t) * part, HD)
        for s in range(steps):
            x_s[t, pl.ds(s * own, own), :] = piece[s].astype(jnp.float32)
        mine = x_s[t]
        xn_ref[pl.ds(first, rows), pl.ds(column, part)] = (
            mine * gain[:, pl.ds(column, part)]
        ).astype(jnp.bfloat16)
        mine = mine * mine
        for c in range(part // HD):
            total = total + mine[:, c * HD : (c + 1) * HD]
    mean = jnp.sum(total, axis=-1, keepdims=True) / (part * len(pieces))
    return lax.rsqrt(mean + norm_eps)


def rotate(x, cosine, sine):
    return (x * cosine + pltpu.roll(x, HD // 2, 1) * sine).astype(jnp.bfloat16)


def load_kernel(
    sizes,
    lengths,
    parents,
    gain,
    hidden,
    wq,
    wk,
    wv,
    pk,
    pv,
    gk,
    gv,
    *refs,
):
    steps, own, tp, kv, group, history, packed = sizes
    pieces = refs[: tp - 1]
    (
        gain_ref,
        xn_ref,
        scale_ref,
        wq_ref,
        keys_ref,
        values_ref,
        cosine_ref,
        sine_ref,
        bias_ref,
        lengths_s,
        parents_s,
        hidden_s,
        x_s,
        wk_s,
        wv_s,
        values_s,
        sems,
    ) = refs[tp - 1 :]
    rows = steps * own
    blocks = pk.shape[0]
    half_len = blocks * history
    device = lax.axis_index("req")
    request = device // 2
    parity = device % 2

    small = [
        (gain, gain_ref),
        (hidden, hidden_s),
        (lengths, lengths_s),
        (parents, parents_s),
    ]
    old = blocks + own
    large = [(pv, values_s.at[pl.ds(0, blocks)]), (gv, values_s.at[pl.ds(blocks, own)])]
    for source, target, parts in ((wk, wk_s, 2), (wv, wv_s, 2)):
        size = source.shape[0] // parts
        for n in range(parts):
            place = pl.ds(n * size, size)
            large.append((source.at[place], target.at[place]))
    large += [(pk, keys_ref.at[pl.ds(0, blocks)]), (gk, keys_ref.at[pl.ds(blocks, own)])]
    size = wq.shape[0] // 4
    for n in range(4):
        place = pl.ds(n * size, size)
        large.append((wq.at[place, pl.ds(0, wq_ref.shape[1])], wq_ref.at[place]))
    copies = [
        pltpu.make_async_copy(source, target, sems.at[n])
        for n, (source, target) in enumerate(small + large)
    ]
    for copy in copies:
        copy.start()
    large = copies[len(small) :]
    for copy in copies[: len(small)]:
        copy.wait()

    scale = lay_out((hidden_s, *pieces), gain_ref, x_s, xn_ref, 0)
    scale_ref[...] = jnp.broadcast_to(scale, scale_ref.shape)

    length = lengths_s[request]
    half_dim = HD // 2
    fall = -math.log(rope_base) / half_dim

    def angles(step, place):
        return (length + history + step).astype(jnp.float32) * jnp.exp(
            place.astype(jnp.float32) * fall
        )

    row = lax.broadcasted_iota(jnp.int32, (rows, HD), 0)
    lane = lax.broadcasted_iota(jnp.int32, (rows, HD), 1)
    angle = angles(quotient(row, own), remainder(lane, half_dim))
    key_cosine = jnp.cos(angle) * scale
    key_sine = jnp.sin(angle) * scale
    key_sine = jnp.where(lane < half_dim, -key_sine, key_sine)

    lanes = packed * group * 2 * rows
    place = lax.broadcasted_iota(jnp.int32, (half_dim, lanes), 0)
    lane = lax.broadcasted_iota(jnp.int32, (half_dim, lanes), 1)
    angle = angles(quotient(remainder(lane, rows), own), place)
    cosine_ref[...] = jnp.cos(angle)
    sine_ref[...] = jnp.sin(angle)

    def parent_of(s, beam):
        out = jnp.zeros_like(beam)
        for j in range(BEAMS):
            out = jnp.where(beam == j, parents_s[s, request * BEAMS + j], out)
        return out

    row = remainder(lax.broadcasted_iota(jnp.int32, (8, lanes), 1), 2 * rows)
    row_step = quotient(remainder(row, rows), own)
    row_parity = jnp.where(row < rows, parity, 1 - parity)
    beam = row_parity * own + remainder(row, own)
    ancestors = [None] * steps
    at = beam
    for s in reversed(range(steps)):
        if s < steps - 1:
            at = jnp.where(row_step > s, parent_of(s + 1, at), beam)
        ancestors[s] = jnp.where(row_step >= s, at, -1)
    origin = parent_of(0, at)

    place = parity * half_len + lax.broadcasted_iota(jnp.int32, (half_len, lanes), 0)
    bias_ref[pl.ds(0, half_len), :] = jnp.where(place < length, 0.0, masked_score)
    for n in range(own):
        seen = jnp.where(origin == parity * own + n, 0.0, masked_score)
        for c in range(0, history, 8):
            bias_ref[pl.ds(half_len + n * history + c, 8), :] = seen
    sublane = lax.broadcasted_iota(jnp.int32, (8, lanes), 0)
    for c in range(0, rows, 8):
        seen = jnp.full((8, lanes), masked_score, jnp.float32)
        for s in range(c // own, min((c + 8) // own, steps)):
            hit = (quotient(c + sublane, own) == s) & (
                ancestors[s] == parity * own + remainder(c + sublane, own)
            )
            seen = jnp.where(hit, 0.0, seen)
        bias_ref[pl.ds(old * history + c, 8), :] = seen

    for copy in large[:2]:
        copy.wait()
    values_ref[:, pl.ds(0, old * history)] = values_s[...].reshape(old * history, kv * HD).T
    keys_ref[pl.ds(old, HD // history)] = jnp.zeros(
        (HD // history, history, kv * HD), jnp.bfloat16
    )
    for copy in large[2:4]:
        copy.wait()
    fresh = jnp.dot(xn_ref[...], wk_s[...], preferred_element_type=jnp.float32)
    for g in range(kv):
        cols = pl.ds(g * HD, HD)
        keys_ref[old, pl.ds(0, rows), cols] = rotate(
            fresh[:, g * HD : (g + 1) * HD], key_cosine, key_sine
        )
    for copy in large[4:6]:
        copy.wait()
    fresh = jnp.dot(xn_ref[...], wv_s[...], preferred_element_type=jnp.float32) * scale
    fresh = jnp.concatenate(
        [fresh, jnp.zeros((HD - rows, kv * HD), jnp.float32)], axis=0
    ).astype(jnp.bfloat16)
    values_ref[:, pl.ds(old * history, HD)] = fresh.T
    for copy in large[6:]:
        copy.wait()


def attend_kernel(
    sizes,
    gain_ref,
    xn_ref,
    scale_ref,
    wq_ref,
    keys_ref,
    values_ref,
    cosine_ref,
    sine_ref,
    bias_ref,
    wq,
    *refs,
):
    steps, own, tp, kv, group, packed = sizes
    pieces = refs[:tp]
    kept_ref, kept_lse_ref, sent_ref, x_s, xn_s, wq_s, sems = refs[tp:]
    rows = steps * own
    packs = kv // packed
    keys_count = bias_ref.shape[0]
    keys_space = values_ref.shape[1]
    near = wq_ref.shape[1]
    size = packed * group * HD
    copies = [
        pltpu.make_async_copy(
            wq.at[:, pl.ds(near + n * size, size)], wq_s.at[n], sems.at[n]
        )
        for n in range((wq.shape[1] - near) // size)
    ]
    for copy in copies:
        copy.start()

    xn_s[pl.ds(0, rows), :] = xn_ref[...]
    scale = lay_out(pieces, gain_ref, x_s, xn_s, rows)
    scale = jnp.concatenate([scale_ref[...], jnp.broadcast_to(scale, (rows, HD))], axis=0)
    scale = scale * HD**-0.5
    lanes = size // HD * 2 * rows
    lane = lax.broadcasted_iota(jnp.int32, (HD, lanes), 1)
    owner = quotient(lane, group * 2 * rows)
    pad = jnp.zeros((keys_space - keys_count, lanes), jnp.bfloat16)

    def score(p):
        if p * size < near:
            w = wq_ref[:, pl.ds(p * size, size)]
        else:
            n = p - near // size
            copies[n].wait()
            w = wq_s[n]
        q = jnp.dot(xn_s[...], w, preferred_element_type=jnp.float32)
        q = jnp.concatenate(
            [q[:, j * HD : (j + 1) * HD] * scale for j in range(packed * group)], axis=0
        ).T
        cosine, sine = cosine_ref[...], sine_ref[...]
        first, second = q[: HD // 2], q[HD // 2 :]
        q = jnp.concatenate(
            [first * cosine - second * sine, second * cosine + first * sine], axis=0
        )
        q = jnp.concatenate([jnp.where(owner == i, q, 0.0) for i in range(packed)], axis=0)
        keys = keys_ref[:, :, pl.ds(p * packed * HD, packed * HD)]
        return (
            jnp.dot(
                keys.reshape(keys_space, packed * HD)[:keys_count],
                q.astype(jnp.bfloat16),
                preferred_element_type=jnp.float32,
            )
            + bias_ref[...]
        )

    def mix(p, scores):
        top = jnp.max(scores, axis=0, keepdims=True)
        powers = jnp.exp(scores - top)
        total = jnp.sum(powers, axis=0, keepdims=True)
        mixed = jnp.dot(
            values_ref[pl.ds(p * packed * HD, packed * HD), :],
            jnp.concatenate([powers.astype(jnp.bfloat16), pad], axis=0),
            preferred_element_type=jnp.float32,
        )
        out = mixed[:HD]
        for i in range(1, packed):
            out = jnp.where(owner == i, mixed[i * HD : (i + 1) * HD], out)
        out = (out * (1.0 / total)).T
        for j in range(packed * group):
            cols = pl.ds((p * packed * group + j) * HD, HD)
            lower = j * 2 * rows
            kept_ref[:, cols] = out[lower : lower + rows]
            sent_ref[:, cols] = out[lower + rows : lower + 2 * rows].astype(jnp.bfloat16)
        lse = top + jnp.log(total)
        if lanes < HD:
            lse = jnp.concatenate([lse, jnp.zeros((1, HD - lanes), jnp.float32)], axis=1)
        return lse

    results = [mix(p, score(p)) for p in range(packs)]

    sublane = lax.broadcasted_iota(jnp.int32, (rows, HD), 0)
    kept_lse = jnp.zeros((rows, HD), jnp.float32)
    terms = jnp.zeros((rows, HD), jnp.float32)
    for p, lse in enumerate(results):
        kept_lse = jnp.where(sublane == p, lse, kept_lse)
        rest = lse
        for n in range(3):
            term = rest.astype(jnp.bfloat16).astype(jnp.float32)
            terms = jnp.where(sublane == n * packs + p, term, terms)
            rest = rest - term
    kept_lse_ref[...] = kept_lse
    sent_ref[:, pl.ds(kv * group * HD, HD)] = terms.astype(jnp.bfloat16)


def fetch_kernel(kept_lse_ref, w_out, kept_lse_out, w_out_ref, sems):
    copies = []
    tp = w_out_ref.shape[0]
    part = w_out_ref.shape[-1]
    me_tp = lax.axis_index("tp")
    for d in range(tp):
        place = pl.ds(pl.multiple_of((me_tp ^ d) * part, HD), part)
        copies.append(pltpu.make_async_copy(w_out.at[:, place], w_out_ref.at[d], sems.at[d]))
    for copy in copies:
        copy.start()
    kept_lse_out[...] = kept_lse_ref[...]
    for copy in copies:
        copy.wait()


def multiply_out(sizes, ctx, w_out_ref, d, out_ref):
    steps, own, chunk = sizes
    for lower in range(0, out_ref.shape[-1], chunk):
        cols = pl.ds(lower, chunk)
        out = jnp.dot(ctx, w_out_ref[d, :, cols], preferred_element_type=jnp.float32)
        for s in range(steps):
            out_ref[s, :, cols] = out[s * own : (s + 1) * own].astype(out_ref.dtype)


def project_own_kernel(sizes, ctx_ref, w_out_ref, out_ref):
    multiply_out(sizes, ctx_ref[...], w_out_ref, 0, out_ref)


def project_kernel(sizes, kept_ref, kept_lse_ref, got_ref, w_out_ref, *refs):
    steps, own, tp, heads, packs, chunk = sizes
    ctx_ref, outs = refs[0], refs[1:]
    rows = steps * own
    base = heads * HD
    terms = got_ref[:, pl.ds(base, HD)].astype(jnp.float32)
    lse_got = sum(terms[n * packs : (n + 1) * packs] for n in range(3))
    lse_got = pltpu.roll(jnp.concatenate([lse_got] * (8 // packs), axis=0), HD - rows, 1)
    lse_mine = kept_lse_ref[pl.ds(0, 8), :]
    top = jnp.maximum(lse_mine, lse_got)
    mine = jnp.exp(lse_mine - top)
    got = jnp.exp(lse_got - top)
    share = (mine / (mine + got)).T
    for h in range(heads):
        cols = pl.ds(h * HD, HD)
        p, j = divmod(h, heads // packs)
        w = share[j * 2 * rows : j * 2 * rows + rows, p : p + 1]
        ctx_ref[:, cols] = (
            kept_ref[:, cols] * w + got_ref[:, cols].astype(jnp.float32) * (1.0 - w)
        ).astype(jnp.bfloat16)
    for d in range(1, tp):
        multiply_out((steps, own, chunk), ctx_ref[...], w_out_ref, d, outs[d - 1])


def body(
    hidden_in,
    norm_gain,
    w_query,
    w_key,
    w_value,
    w_out,
    prompt_keys,
    prompt_values,
    gen_keys,
    gen_values,
    lengths,
    parents,
):
    steps, own, part = hidden_in.shape
    tp = lax.axis_size("tp")
    rows = steps * own
    width = w_query.shape[0]
    kv = w_key.shape[1] // HD
    group = w_query.shape[1] // w_key.shape[1]
    heads = kv * group
    history = gen_keys.shape[1]

    near_pieces = [across(hidden_in, 0, t) for t in range(1, tp)]
    far_pieces = [across(hidden_in, 1, t) for t in range(tp)]

    def in_hbm(x):
        return pltpu.with_memory_space_constraint(x, pltpu.HBM)

    vmem = pl.BlockSpec(memory_space=pltpu.VMEM)
    hbm = pl.BlockSpec(memory_space=pltpu.HBM)
    params = pltpu.CompilerParams(vmem_limit_bytes=16 * 2**20)
    f32, bf16 = jnp.float32, jnp.bfloat16
    blocks = prompt_keys.shape[1] // history
    cache = (blocks + own + HD // history, history, kv * HD)
    packed = 2 - kv % 2
    packs = kv // packed
    near = max(packs // 2, 1) * packed * group * HD
    lanes = packed * group * 2 * rows
    loaded = pl.pallas_call(
        functools.partial(load_kernel, (steps, own, tp, kv, group, history, packed)),
        out_shape=(
            jax.ShapeDtypeStruct((1, width), f32),
            jax.ShapeDtypeStruct((rows, width), bf16),
            jax.ShapeDtypeStruct((rows, HD), f32),
            jax.ShapeDtypeStruct((width, near), bf16),
            jax.ShapeDtypeStruct(cache, bf16),
            jax.ShapeDtypeStruct((kv * HD, cache[0] * history), bf16),
            jax.ShapeDtypeStruct((HD // 2, lanes), f32),
            jax.ShapeDtypeStruct((HD // 2, lanes), f32),
            jax.ShapeDtypeStruct(((blocks + own) * history + rows, lanes), f32),
        ),
        in_specs=[hbm] * 11 + [vmem] * (tp - 1),
        out_specs=(vmem,) * 9,
        scratch_shapes=[
            pltpu.SMEM(lengths.shape, jnp.int32),
            pltpu.SMEM(parents.shape, jnp.int32),
            pltpu.VMEM(hidden_in.shape, bf16),
            pltpu.VMEM((tp, rows, part), f32),
            pltpu.VMEM(w_key.shape, bf16),
            pltpu.VMEM(w_value.shape, bf16),
            pltpu.VMEM((blocks + own, history, kv * HD), bf16),
            pltpu.SemaphoreType.DMA((16,)),
        ],
        compiler_params=params,
        name="load",
    )(
        *(
            in_hbm(x)
            for x in (
                lengths,
                parents,
                norm_gain[None, :],
                hidden_in,
                w_query,
                w_key,
                w_value,
                prompt_keys.reshape(blocks, history, kv * HD),
                prompt_values.reshape(blocks, history, kv * HD),
                gen_keys,
                gen_values,
            )
        ),
        *near_pieces,
    )

    kept, kept_lse, sent = pl.pallas_call(
        functools.partial(attend_kernel, (steps, own, tp, kv, group, packed)),
        out_shape=(
            jax.ShapeDtypeStruct((rows, heads * HD), f32),
            jax.ShapeDtypeStruct((rows, HD), f32),
            jax.ShapeDtypeStruct((rows, heads * HD + HD), bf16),
        ),
        in_specs=[vmem] * 9 + [hbm] + [vmem] * tp,
        out_specs=(vmem,) * 3,
        scratch_shapes=[
            pltpu.VMEM((tp, rows, part), f32),
            pltpu.VMEM((2 * rows, width), bf16),
            pltpu.VMEM((packs, width, packed * group * HD), bf16),
            pltpu.SemaphoreType.DMA((kv,)),
        ],
        compiler_params=params,
        name="attend",
    )(*loaded, in_hbm(w_query), *far_pieces)

    got = permute_by(sent, "req", 1)
    kept_lse, w_out_near = pl.pallas_call(
        fetch_kernel,
        out_shape=(
            jax.ShapeDtypeStruct((rows, HD), f32),
            jax.ShapeDtypeStruct((tp, heads * HD, part), bf16),
        ),
        in_specs=[vmem, hbm],
        out_specs=(vmem, vmem),
        scratch_shapes=[pltpu.SemaphoreType.DMA((tp,))],
        compiler_params=params,
        name="fetch",
    )(kept_lse, in_hbm(w_out))

    chunk = math.gcd(part, 512)
    ctx, *sums = pl.pallas_call(
        functools.partial(project_kernel, (steps, own, tp, heads, packs, chunk)),
        out_shape=(
            jax.ShapeDtypeStruct((rows, heads * HD), bf16),
            *[jax.ShapeDtypeStruct((steps, own, part), bf16)] * (tp - 1),
        ),
        in_specs=[vmem] * 4,
        out_specs=(vmem,) * tp,
        compiler_params=params,
        name="project",
    )(kept, kept_lse, got, w_out_near)
    sums = [across(x, 0, t + 1) for t, x in enumerate(sums)]
    total = pl.pallas_call(
        functools.partial(project_own_kernel, (steps, own, chunk)),
        out_shape=jax.ShapeDtypeStruct((steps, own, part), f32),
        in_specs=[vmem] * 2,
        out_specs=vmem,
        compiler_params=params,
        name="project_own",
    )(ctx, w_out_near)
    for x in sums:
        total = total + x.astype(f32)
    return total.astype(bf16)


def solution(mesh):
    in_specs = (
        P(None, "req", "tp"),
        P(),
        P(None, "tp"),
        P(None, "tp"),
        P(None, "tp"),
        P("tp", None),
        P("req", None, "tp"),
        P("req", None, "tp"),
        P("req", None, "tp"),
        P("req", None, "tp"),
        P(),
        P(),
    )
    out_specs = P(None, "req", "tp")
    return jax.shard_map(body, mesh=mesh, in_specs=in_specs, out_specs=out_specs, check_vma=False)
```

```python
import functools
import math

import jax
import jax.numpy as jnp
from jax import lax
from jax.experimental import pallas as pl
from jax.experimental.pallas import tpu as pltpu
from jax.sharding import PartitionSpec as P

HD = 128
BEAMS = 8

norm_eps = 1e-05
masked_score = -1e30
rope_base = 500000.0


def quotient(x, size):
    return x >> (size.bit_length() - 1) if size & (size - 1) == 0 else x // size


def remainder(x, size):
    return x & (size - 1) if size & (size - 1) == 0 else x % size


def permute_by(value, axis, distance):
    pairs = [(source, source ^ distance) for source in range(lax.axis_size(axis))]
    return lax.ppermute(value, axis, pairs)


def across(value, beam_distance, tp_distance):
    req, tp = lax.axis_size("req"), lax.axis_size("tp")
    pairs = [
        (r * tp + t, (r ^ beam_distance) * tp + (t ^ tp_distance))
        for r in range(req)
        for t in range(tp)
    ]
    return lax.ppermute(value, ("req", "tp"), pairs)


def lay_out(pieces, gain, x_s, xn_ref, first):
    steps, own, part = pieces[0].shape
    rows = steps * own
    me_tp = lax.axis_index("tp")
    total = jnp.zeros((rows, HD), jnp.float32)
    for t, piece in enumerate(pieces):
        column = pl.multiple_of((me_tp ^ t) * part, HD)
        for s in range(steps):
            x_s[t, pl.ds(s * own, own), :] = piece[s].astype(jnp.float32)
        mine = x_s[t]
        xn_ref[pl.ds(first, rows), pl.ds(column, part)] = (
            mine * gain[:, pl.ds(column, part)]
        ).astype(jnp.bfloat16)
        mine = mine * mine
        for c in range(part // HD):
            total = total + mine[:, c * HD : (c + 1) * HD]
    mean = jnp.sum(total, axis=-1, keepdims=True) / (part * len(pieces))
    return lax.rsqrt(mean + norm_eps)


def rotate(x, cosine, sine):
    return (x * cosine + pltpu.roll(x, HD // 2, 1) * sine).astype(jnp.bfloat16)


def load_kernel(
    sizes,
    lengths,
    parents,
    gain,
    hidden,
    wk,
    wv,
    pk,
    pv,
    gk,
    gv,
    *refs,
):
    steps, own, tp, kv, group, history, packed = sizes
    pieces = refs[: tp - 1]
    (
        gain_ref,
        xn_ref,
        scale_ref,
        keys_ref,
        values_ref,
        cosine_ref,
        sine_ref,
        bias_ref,
        lengths_s,
        parents_s,
        hidden_s,
        x_s,
        wk_s,
        wv_s,
        values_s,
        sems,
    ) = refs[tp - 1 :]
    rows = steps * own
    blocks = pk.shape[0]
    half_len = blocks * history
    device = lax.axis_index("req")
    request = device // 2
    parity = device % 2

    small = [
        (gain, gain_ref),
        (hidden, hidden_s),
        (lengths, lengths_s),
        (parents, parents_s),
    ]
    old = blocks + own
    large = [(pv, values_s.at[pl.ds(0, blocks)]), (gv, values_s.at[pl.ds(blocks, own)])]
    for source, target, parts in ((wk, wk_s, 2), (wv, wv_s, 2)):
        size = source.shape[0] // parts
        for n in range(parts):
            place = pl.ds(n * size, size)
            large.append((source.at[place], target.at[place]))
    large += [(pk, keys_ref.at[pl.ds(0, blocks)]), (gk, keys_ref.at[pl.ds(blocks, own)])]
    copies = [
        pltpu.make_async_copy(source, target, sems.at[n])
        for n, (source, target) in enumerate(small + large)
    ]
    for copy in copies:
        copy.start()
    large = copies[len(small) :]
    for copy in copies[: len(small)]:
        copy.wait()

    scale = lay_out((hidden_s, *pieces), gain_ref, x_s, xn_ref, 0)
    scale_ref[...] = jnp.broadcast_to(scale, scale_ref.shape)

    length = lengths_s[request]
    half_dim = HD // 2
    fall = -math.log(rope_base) / half_dim

    def angles(step, place):
        return (length + history + step).astype(jnp.float32) * jnp.exp(
            place.astype(jnp.float32) * fall
        )

    row = lax.broadcasted_iota(jnp.int32, (rows, HD), 0)
    lane = lax.broadcasted_iota(jnp.int32, (rows, HD), 1)
    angle = angles(quotient(row, own), remainder(lane, half_dim))
    key_cosine = jnp.cos(angle) * scale
    key_sine = jnp.sin(angle) * scale
    key_sine = jnp.where(lane < half_dim, -key_sine, key_sine)

    lanes = packed * group * 2 * rows
    place = lax.broadcasted_iota(jnp.int32, (half_dim, lanes), 0)
    lane = lax.broadcasted_iota(jnp.int32, (half_dim, lanes), 1)
    angle = angles(quotient(remainder(lane, rows), own), place)
    cosine_ref[...] = jnp.cos(angle)
    sine_ref[...] = jnp.sin(angle)

    def parent_of(s, beam):
        out = jnp.zeros_like(beam)
        for j in range(BEAMS):
            out = jnp.where(beam == j, parents_s[s, request * BEAMS + j], out)
        return out

    row = remainder(lax.broadcasted_iota(jnp.int32, (8, lanes), 1), 2 * rows)
    row_step = quotient(remainder(row, rows), own)
    row_parity = jnp.where(row < rows, parity, 1 - parity)
    beam = row_parity * own + remainder(row, own)
    ancestors = [None] * steps
    at = beam
    for s in reversed(range(steps)):
        if s < steps - 1:
            at = jnp.where(row_step > s, parent_of(s + 1, at), beam)
        ancestors[s] = jnp.where(row_step >= s, at, -1)
    origin = parent_of(0, at)

    place = parity * half_len + lax.broadcasted_iota(jnp.int32, (half_len, lanes), 0)
    bias_ref[pl.ds(0, half_len), :] = jnp.where(place < length, 0.0, masked_score)
    for n in range(own):
        seen = jnp.where(origin == parity * own + n, 0.0, masked_score)
        for c in range(0, history, 8):
            bias_ref[pl.ds(half_len + n * history + c, 8), :] = seen
    sublane = lax.broadcasted_iota(jnp.int32, (8, lanes), 0)
    for c in range(0, rows, 8):
        seen = jnp.full((8, lanes), masked_score, jnp.float32)
        for s in range(c // own, min((c + 8) // own, steps)):
            hit = (quotient(c + sublane, own) == s) & (
                ancestors[s] == parity * own + remainder(c + sublane, own)
            )
            seen = jnp.where(hit, 0.0, seen)
        bias_ref[pl.ds(old * history + c, 8), :] = seen

    for copy in large[:2]:
        copy.wait()
    values_ref[:, pl.ds(0, old * history)] = values_s[...].reshape(old * history, kv * HD).T
    keys_ref[pl.ds(old, HD // history)] = jnp.zeros(
        (HD // history, history, kv * HD), jnp.bfloat16
    )
    for copy in large[2:4]:
        copy.wait()
    fresh = jnp.dot(xn_ref[...], wk_s[...], preferred_element_type=jnp.float32)
    for g in range(kv):
        cols = pl.ds(g * HD, HD)
        keys_ref[old, pl.ds(0, rows), cols] = rotate(
            fresh[:, g * HD : (g + 1) * HD], key_cosine, key_sine
        )
    for copy in large[4:6]:
        copy.wait()
    fresh = jnp.dot(xn_ref[...], wv_s[...], preferred_element_type=jnp.float32) * scale
    fresh = jnp.concatenate(
        [fresh, jnp.zeros((HD - rows, kv * HD), jnp.float32)], axis=0
    ).astype(jnp.bfloat16)
    values_ref[:, pl.ds(old * history, HD)] = fresh.T
    for copy in large[6:]:
        copy.wait()


def attend_kernel(
    sizes,
    gain_ref,
    xn_ref,
    scale_ref,
    keys_ref,
    values_ref,
    cosine_ref,
    sine_ref,
    bias_ref,
    wq_ref,
    *refs,
):
    steps, own, tp, kv, group, packed = sizes
    pieces = refs[:tp]
    kept_ref, kept_lse_ref, sent_ref, x_s, xn_s = refs[tp:]
    rows = steps * own
    packs = kv // packed
    keys_count = bias_ref.shape[0]
    keys_space = values_ref.shape[1]
    size = packed * group * HD

    xn_s[pl.ds(0, rows), :] = xn_ref[...]
    scale = lay_out(pieces, gain_ref, x_s, xn_s, rows)
    scale = jnp.concatenate([scale_ref[...], jnp.broadcast_to(scale, (rows, HD))], axis=0)
    scale = scale * HD**-0.5
    lanes = size // HD * 2 * rows
    lane = lax.broadcasted_iota(jnp.int32, (HD, lanes), 1)
    owner = quotient(lane, group * 2 * rows)
    pad = jnp.zeros((keys_space - keys_count, lanes), jnp.bfloat16)

    every = range(packs)
    queries = []
    for p in every:
        q = jnp.dot(
            xn_s[...], wq_ref[:, pl.ds(p * size, size)], preferred_element_type=jnp.float32
        )
        queries.append(
            jnp.concatenate(
                [q[:, j * HD : (j + 1) * HD] * scale for j in range(packed * group)], axis=0
            )
        )
    cosine, sine = cosine_ref[...], sine_ref[...]
    scores = []
    for p in every:
        q = queries[p].T
        first, second = q[: HD // 2], q[HD // 2 :]
        q = jnp.concatenate(
            [first * cosine - second * sine, second * cosine + first * sine], axis=0
        )
        q = jnp.concatenate([jnp.where(owner == i, q, 0.0) for i in range(packed)], axis=0)
        keys = keys_ref[:, :, pl.ds(p * packed * HD, packed * HD)]
        scores.append(
            jnp.dot(
                keys.reshape(keys_space, packed * HD)[:keys_count],
                q.astype(jnp.bfloat16),
                preferred_element_type=jnp.float32,
            )
            + bias_ref[...]
        )
    tops = [jnp.max(x, axis=0, keepdims=True) for x in scores]
    powers = [jnp.exp(x - top) for x, top in zip(scores, tops)]
    totals = [jnp.sum(x, axis=0, keepdims=True) for x in powers]
    mixed = [
        jnp.dot(
            values_ref[pl.ds(p * packed * HD, packed * HD), :],
            jnp.concatenate([powers[p].astype(jnp.bfloat16), pad], axis=0),
            preferred_element_type=jnp.float32,
        )
        for p in every
    ]
    results = []
    for p in every:
        out = mixed[p][:HD]
        for i in range(1, packed):
            out = jnp.where(owner == i, mixed[p][i * HD : (i + 1) * HD], out)
        out = (out * (1.0 / totals[p])).T
        for j in range(packed * group):
            cols = pl.ds((p * packed * group + j) * HD, HD)
            lower = j * 2 * rows
            kept_ref[:, cols] = out[lower : lower + rows]
            sent_ref[:, cols] = out[lower + rows : lower + 2 * rows].astype(jnp.bfloat16)
        lse = tops[p] + jnp.log(totals[p])
        if lanes < HD:
            lse = jnp.concatenate([lse, jnp.zeros((1, HD - lanes), jnp.float32)], axis=1)
        results.append(lse)

    sublane = lax.broadcasted_iota(jnp.int32, (rows, HD), 0)
    kept_lse = jnp.zeros((rows, HD), jnp.float32)
    terms = jnp.zeros((rows, HD), jnp.float32)
    for p, lse in enumerate(results):
        kept_lse = jnp.where(sublane == p, lse, kept_lse)
        rest = lse
        for n in range(3):
            term = rest.astype(jnp.bfloat16).astype(jnp.float32)
            terms = jnp.where(sublane == n * packs + p, term, terms)
            rest = rest - term
    kept_lse_ref[...] = kept_lse
    sent_ref[:, pl.ds(kv * group * HD, HD)] = terms.astype(jnp.bfloat16)


def fetch_kernel(kept_lse_ref, w_out, kept_lse_out, w_out_ref, sems):
    copies = []
    tp = w_out_ref.shape[0]
    part = w_out_ref.shape[-1]
    me_tp = lax.axis_index("tp")
    for d in range(tp):
        place = pl.ds(pl.multiple_of((me_tp ^ d) * part, HD), part)
        copies.append(pltpu.make_async_copy(w_out.at[:, place], w_out_ref.at[d], sems.at[d]))
    for copy in copies:
        copy.start()
    kept_lse_out[...] = kept_lse_ref[...]
    for copy in copies:
        copy.wait()


def multiply_out(sizes, ctx, w_out_ref, d, out_ref):
    steps, own, chunk = sizes
    for lower in range(0, out_ref.shape[-1], chunk):
        cols = pl.ds(lower, chunk)
        out = jnp.dot(ctx, w_out_ref[d, :, cols], preferred_element_type=jnp.float32)
        for s in range(steps):
            out_ref[s, :, cols] = out[s * own : (s + 1) * own].astype(out_ref.dtype)


def project_own_kernel(sizes, ctx_ref, w_out_ref, out_ref):
    multiply_out(sizes, ctx_ref[...], w_out_ref, 0, out_ref)


def project_kernel(sizes, kept_ref, kept_lse_ref, got_ref, w_out_ref, *refs):
    steps, own, tp, heads, packs, chunk = sizes
    ctx_ref, outs = refs[0], refs[1:]
    rows = steps * own
    base = heads * HD
    terms = got_ref[:, pl.ds(base, HD)].astype(jnp.float32)
    lse_got = sum(terms[n * packs : (n + 1) * packs] for n in range(3))
    lse_got = pltpu.roll(jnp.concatenate([lse_got] * (8 // packs), axis=0), HD - rows, 1)
    lse_mine = kept_lse_ref[pl.ds(0, 8), :]
    top = jnp.maximum(lse_mine, lse_got)
    mine = jnp.exp(lse_mine - top)
    got = jnp.exp(lse_got - top)
    share = (mine / (mine + got)).T
    for h in range(heads):
        cols = pl.ds(h * HD, HD)
        p, j = divmod(h, heads // packs)
        w = share[j * 2 * rows : j * 2 * rows + rows, p : p + 1]
        ctx_ref[:, cols] = (
            kept_ref[:, cols] * w + got_ref[:, cols].astype(jnp.float32) * (1.0 - w)
        ).astype(jnp.bfloat16)
    for d in range(1, tp):
        multiply_out((steps, own, chunk), ctx_ref[...], w_out_ref, d, outs[d - 1])


def body(
    hidden_in,
    norm_gain,
    w_query,
    w_key,
    w_value,
    w_out,
    prompt_keys,
    prompt_values,
    gen_keys,
    gen_values,
    lengths,
    parents,
):
    steps, own, part = hidden_in.shape
    tp = lax.axis_size("tp")
    rows = steps * own
    width = w_query.shape[0]
    kv = w_key.shape[1] // HD
    group = w_query.shape[1] // w_key.shape[1]
    heads = kv * group
    history = gen_keys.shape[1]

    near_pieces = [across(hidden_in, 0, t) for t in range(1, tp)]
    far_pieces = [across(hidden_in, 1, t) for t in range(tp)]

    def in_hbm(x):
        return pltpu.with_memory_space_constraint(x, pltpu.HBM)

    vmem = pl.BlockSpec(memory_space=pltpu.VMEM)
    hbm = pl.BlockSpec(memory_space=pltpu.HBM)
    params = pltpu.CompilerParams(vmem_limit_bytes=16 * 2**20)
    f32, bf16 = jnp.float32, jnp.bfloat16
    blocks = prompt_keys.shape[1] // history
    cache = (blocks + own + HD // history, history, kv * HD)
    packed = 2 - kv % 2
    packs = kv // packed
    lanes = packed * group * 2 * rows
    loaded = pl.pallas_call(
        functools.partial(load_kernel, (steps, own, tp, kv, group, history, packed)),
        out_shape=(
            jax.ShapeDtypeStruct((1, width), f32),
            jax.ShapeDtypeStruct((rows, width), bf16),
            jax.ShapeDtypeStruct((rows, HD), f32),
            jax.ShapeDtypeStruct(cache, bf16),
            jax.ShapeDtypeStruct((kv * HD, cache[0] * history), bf16),
            jax.ShapeDtypeStruct((HD // 2, lanes), f32),
            jax.ShapeDtypeStruct((HD // 2, lanes), f32),
            jax.ShapeDtypeStruct(((blocks + own) * history + rows, lanes), f32),
        ),
        in_specs=[hbm] * 10 + [vmem] * (tp - 1),
        out_specs=(vmem,) * 8,
        scratch_shapes=[
            pltpu.SMEM(lengths.shape, jnp.int32),
            pltpu.SMEM(parents.shape, jnp.int32),
            pltpu.VMEM(hidden_in.shape, bf16),
            pltpu.VMEM((tp, rows, part), f32),
            pltpu.VMEM(w_key.shape, bf16),
            pltpu.VMEM(w_value.shape, bf16),
            pltpu.VMEM((blocks + own, history, kv * HD), bf16),
            pltpu.SemaphoreType.DMA((16,)),
        ],
        compiler_params=params,
        name="load",
    )(
        *(
            in_hbm(x)
            for x in (
                lengths,
                parents,
                norm_gain[None, :],
                hidden_in,
                w_key,
                w_value,
                prompt_keys.reshape(blocks, history, kv * HD),
                prompt_values.reshape(blocks, history, kv * HD),
                gen_keys,
                gen_values,
            )
        ),
        *near_pieces,
    )

    kept, kept_lse, sent = pl.pallas_call(
        functools.partial(attend_kernel, (steps, own, tp, kv, group, packed)),
        out_shape=(
            jax.ShapeDtypeStruct((rows, heads * HD), f32),
            jax.ShapeDtypeStruct((rows, HD), f32),
            jax.ShapeDtypeStruct((rows, heads * HD + HD), bf16),
        ),
        in_specs=[vmem] * 9 + [vmem] * tp,
        out_specs=(vmem,) * 3,
        scratch_shapes=[
            pltpu.VMEM((tp, rows, part), f32),
            pltpu.VMEM((2 * rows, width), bf16),
        ],
        compiler_params=params,
        name="attend",
    )(*loaded, pltpu.with_memory_space_constraint(w_query, pltpu.VMEM), *far_pieces)

    got = permute_by(sent, "req", 1)
    kept_lse, w_out_near = pl.pallas_call(
        fetch_kernel,
        out_shape=(
            jax.ShapeDtypeStruct((rows, HD), f32),
            jax.ShapeDtypeStruct((tp, heads * HD, part), bf16),
        ),
        in_specs=[vmem, hbm],
        out_specs=(vmem, vmem),
        scratch_shapes=[pltpu.SemaphoreType.DMA((tp,))],
        compiler_params=params,
        name="fetch",
    )(kept_lse, in_hbm(w_out))

    chunk = math.gcd(part, 512)
    ctx, *sums = pl.pallas_call(
        functools.partial(project_kernel, (steps, own, tp, heads, packs, chunk)),
        out_shape=(
            jax.ShapeDtypeStruct((rows, heads * HD), bf16),
            *[jax.ShapeDtypeStruct((steps, own, part), bf16)] * (tp - 1),
        ),
        in_specs=[vmem] * 4,
        out_specs=(vmem,) * tp,
        compiler_params=params,
        name="project",
    )(kept, kept_lse, got, w_out_near)
    sums = [across(x, 0, t + 1) for t, x in enumerate(sums)]
    total = pl.pallas_call(
        functools.partial(project_own_kernel, (steps, own, chunk)),
        out_shape=jax.ShapeDtypeStruct((steps, own, part), f32),
        in_specs=[vmem] * 2,
        out_specs=vmem,
        compiler_params=params,
        name="project_own",
    )(ctx, w_out_near)
    for x in sums:
        total = total + x.astype(f32)
    return total.astype(bf16)


def solution(mesh):
    in_specs = (
        P(None, "req", "tp"),
        P(),
        P(None, "tp"),
        P(None, "tp"),
        P(None, "tp"),
        P("tp", None),
        P("req", None, "tp"),
        P("req", None, "tp"),
        P("req", None, "tp"),
        P("req", None, "tp"),
        P(),
        P(),
    )
    out_specs = P(None, "req", "tp")
    return jax.shard_map(body, mesh=mesh, in_specs=in_specs, out_specs=out_specs, check_vma=False)
```

```python
import functools
import math

import jax
import jax.numpy as jnp
from jax import lax
from jax.experimental import pallas as pl
from jax.experimental.pallas import tpu as pltpu
from jax.sharding import PartitionSpec as P

HD = 128
BEAMS = 8

norm_eps = 1e-05
masked_score = -1e30
rope_base = 500000.0


def quotient(x, size):
    return x >> (size.bit_length() - 1) if size & (size - 1) == 0 else x // size


def remainder(x, size):
    return x & (size - 1) if size & (size - 1) == 0 else x % size


def permute_by(value, axis, distance):
    pairs = [(source, source ^ distance) for source in range(lax.axis_size(axis))]
    return lax.ppermute(value, axis, pairs)


def across(value, beam_distance, tp_distance):
    req, tp = lax.axis_size("req"), lax.axis_size("tp")
    pairs = [
        (r * tp + t, (r ^ beam_distance) * tp + (t ^ tp_distance))
        for r in range(req)
        for t in range(tp)
    ]
    return lax.ppermute(value, ("req", "tp"), pairs)


def lay_out(pieces, gain, x_s, xn_ref, first):
    steps, own, part = pieces[0].shape
    rows = steps * own
    me_tp = lax.axis_index("tp")
    total = jnp.zeros((rows, HD), jnp.float32)
    for t, piece in enumerate(pieces):
        column = pl.multiple_of((me_tp ^ t) * part, HD)
        for s in range(steps):
            x_s[t, pl.ds(s * own, own), :] = piece[s].astype(jnp.float32)
        mine = x_s[t]
        xn_ref[pl.ds(first, rows), pl.ds(column, part)] = (
            mine * gain[:, pl.ds(column, part)]
        ).astype(jnp.bfloat16)
        mine = mine * mine
        for c in range(part // HD):
            total = total + mine[:, c * HD : (c + 1) * HD]
    mean = jnp.sum(total, axis=-1, keepdims=True) / (part * len(pieces))
    return lax.rsqrt(mean + norm_eps)


def rotate(x, cosine, sine):
    return (x * cosine + pltpu.roll(x, HD // 2, 1) * sine).astype(jnp.bfloat16)


def load_kernel(
    sizes,
    lengths,
    parents,
    gain,
    hidden,
    wk,
    wv,
    pv,
    gv,
    *refs,
):
    steps, own, tp, kv, group, history, packed = sizes
    pieces = refs[: tp - 1]
    (
        gain_ref,
        xn_ref,
        scale_ref,
        new_keys_ref,
        values_ref,
        cosine_ref,
        sine_ref,
        bias_ref,
        lengths_s,
        parents_s,
        hidden_s,
        x_s,
        wk_s,
        wv_s,
        values_s,
        sems,
    ) = refs[tp - 1 :]
    rows = steps * own
    quarters = 4
    blocks = pv.shape[0]
    half_len = blocks * history
    device = lax.axis_index("req")
    request = device // 2
    parity = device % 2

    small = [
        (gain, gain_ref),
        (hidden, hidden_s),
        (lengths, lengths_s),
        (parents, parents_s),
    ]
    old = blocks + own
    large = [(pv, values_s.at[pl.ds(0, blocks)]), (gv, values_s.at[pl.ds(blocks, own)])]
    for source, target in ((wk, wk_s), (wv, wv_s)):
        size = source.shape[0] // quarters
        for n in range(quarters):
            place = pl.ds(n * size, size)
            large.append((source.at[place], target.at[place]))
    copies = [
        pltpu.make_async_copy(source, target, sems.at[n])
        for n, (source, target) in enumerate(small + large)
    ]
    for copy in copies:
        copy.start()
    large = copies[len(small) :]
    for copy in copies[: len(small)]:
        copy.wait()

    scale = lay_out((hidden_s, *pieces), gain_ref, x_s, xn_ref, 0)
    scale_ref[...] = jnp.broadcast_to(scale, scale_ref.shape)

    length = lengths_s[request]
    half_dim = HD // 2
    fall = -math.log(rope_base) / half_dim

    def angles(step, place):
        return (length + history + step).astype(jnp.float32) * jnp.exp(
            place.astype(jnp.float32) * fall
        )

    row = lax.broadcasted_iota(jnp.int32, (rows, HD), 0)
    lane = lax.broadcasted_iota(jnp.int32, (rows, HD), 1)
    angle = angles(quotient(row, own), remainder(lane, half_dim))
    key_cosine = jnp.cos(angle) * scale
    key_sine = jnp.sin(angle) * scale
    key_sine = jnp.where(lane < half_dim, -key_sine, key_sine)

    lanes = packed * group * 2 * rows
    place = lax.broadcasted_iota(jnp.int32, (half_dim, lanes), 0)
    lane = lax.broadcasted_iota(jnp.int32, (half_dim, lanes), 1)
    angle = angles(quotient(remainder(lane, rows), own), place)
    cosine_ref[...] = jnp.cos(angle)
    sine_ref[...] = jnp.sin(angle)

    def parent_of(s, beam):
        out = jnp.zeros_like(beam)
        for j in range(BEAMS):
            out = jnp.where(beam == j, parents_s[s, request * BEAMS + j], out)
        return out

    lane = lax.broadcasted_iota(jnp.int32, (8, lanes), 1)
    row_step = quotient(remainder(lane, rows), own)
    row_parity = jnp.where(lane < lanes // 2, parity, 1 - parity)
    beam = row_parity * own + remainder(lane, own)
    ancestors = [None] * steps
    at = beam
    for s in reversed(range(steps)):
        if s < steps - 1:
            at = jnp.where(row_step > s, parent_of(s + 1, at), beam)
        ancestors[s] = jnp.where(row_step >= s, at, -1)
    origin = parent_of(0, at)

    place = parity * half_len + lax.broadcasted_iota(jnp.int32, (half_len, lanes), 0)
    bias_ref[pl.ds(0, half_len), :] = jnp.where(place < length, 0.0, masked_score)
    for n in range(own):
        seen = jnp.where(origin == parity * own + n, 0.0, masked_score)
        for c in range(0, history, 8):
            bias_ref[pl.ds(half_len + n * history + c, 8), :] = seen
    sublane = lax.broadcasted_iota(jnp.int32, (8, lanes), 0)
    for c in range(0, rows, 8):
        seen = jnp.full((8, lanes), masked_score, jnp.float32)
        for s in range(c // own, min((c + 8) // own, steps)):
            hit = (quotient(c + sublane, own) == s) & (
                ancestors[s] == parity * own + remainder(c + sublane, own)
            )
            seen = jnp.where(hit, 0.0, seen)
        bias_ref[pl.ds(old * history + c, 8), :] = seen

    for copy in large[:2]:
        copy.wait()
    values_ref[:, pl.ds(0, old * history)] = values_s[...].reshape(old * history, kv * HD).T

    def project(w_s, copies):
        size = w_s.shape[0] // quarters
        out = jnp.zeros((rows, kv * HD), jnp.float32)
        for n, copy in enumerate(copies):
            place = pl.ds(n * size, size)
            copy.wait()
            out += jnp.dot(xn_ref[:, place], w_s[place], preferred_element_type=jnp.float32)
        return out

    fresh = project(wk_s, large[2 : 2 + quarters])
    for g in range(kv):
        cols = pl.ds(g * HD, HD)
        new_keys_ref[:, cols] = rotate(fresh[:, g * HD : (g + 1) * HD], key_cosine, key_sine)
    fresh = project(wv_s, large[2 + quarters :]) * scale
    fresh = jnp.concatenate(
        [fresh, jnp.zeros((HD - rows, kv * HD), jnp.float32)], axis=0
    ).astype(jnp.bfloat16)
    values_ref[:, pl.ds(old * history, HD)] = fresh.T


def attend_kernel(
    sizes,
    gain_ref,
    xn_ref,
    scale_ref,
    new_keys_ref,
    values_ref,
    cosine_ref,
    sine_ref,
    bias_ref,
    wq_ref,
    pk_ref,
    gk_ref,
    *refs,
):
    steps, own, tp, kv, group, packed = sizes
    pieces = refs[:tp]
    kept_ref, kept_lse_ref, sent_ref, x_s, xn_s = refs[tp:]
    rows = steps * own
    part = pieces[0].shape[-1]
    packs = kv // packed
    each = packed * group
    size = each * HD
    lanes = each * 2 * rows
    keys_count = bias_ref.shape[0]
    keys_space = values_ref.shape[1]
    lane = lax.broadcasted_iota(jnp.int32, (HD, lanes), 1)
    owner = quotient(remainder(lane, lanes // 2), group * rows)
    pad = jnp.zeros((keys_space - keys_count, lanes), jnp.bfloat16)

    xn_s[pl.ds(0, rows), :] = xn_ref[...]
    scale = lay_out(pieces, gain_ref, x_s, xn_s, rows)
    me_tp = lax.axis_index("tp")
    product = jnp.zeros((2 * rows, kv * group * HD), jnp.float32)
    for t in range(tp):
        place = pl.ds(pl.multiple_of((me_tp ^ t) * part, HD), part)
        product += jnp.dot(xn_s[:, place], wq_ref[place, :], preferred_element_type=jnp.float32)
    scale = jnp.concatenate([scale_ref[...], jnp.broadcast_to(scale, (rows, HD))], axis=0)
    scale = scale * HD**-0.5
    product = [product[:, h * HD : (h + 1) * HD] * scale for h in range(kv * group)]

    every = range(packs)
    cosine, sine = cosine_ref[...], sine_ref[...]
    scores = []
    for p in every:
        q = product[p * each : (p + 1) * each]
        q = jnp.concatenate([x[:rows] for x in q] + [x[rows:] for x in q], axis=0).T
        first, second = q[: HD // 2], q[HD // 2 :]
        q = jnp.concatenate(
            [first * cosine - second * sine, second * cosine + first * sine], axis=0
        )
        q = jnp.concatenate([jnp.where(owner == i, q, 0.0) for i in range(packed)], axis=0)
        cols = pl.ds(p * packed * HD, packed * HD)
        keys = jnp.concatenate(
            [
                pk_ref[0, :, cols],
                gk_ref[:, :, cols].reshape(-1, packed * HD),
                new_keys_ref[:, cols],
            ],
            axis=0,
        )
        scores.append(
            jnp.dot(keys, q.astype(jnp.bfloat16), preferred_element_type=jnp.float32)
            + bias_ref[...]
        )
    tops = [jnp.max(x, axis=0, keepdims=True) for x in scores]
    powers = [jnp.exp(x - top) for x, top in zip(scores, tops)]
    totals = [jnp.sum(x, axis=0, keepdims=True) for x in powers]
    mixed = [
        jnp.dot(
            values_ref[pl.ds(p * packed * HD, packed * HD), :],
            jnp.concatenate([powers[p].astype(jnp.bfloat16), pad], axis=0),
            preferred_element_type=jnp.float32,
        )
        for p in every
    ]
    results, logs = [], []
    for p in every:
        out = mixed[p][:HD]
        for i in range(1, packed):
            out = jnp.where(owner == i, mixed[p][i * HD : (i + 1) * HD], out)
        results.append(out * (1.0 / totals[p]))
        logs.append(jnp.broadcast_to(tops[p] + jnp.log(totals[p]), (8, lanes)))

    def sort(parts):
        half = lanes // 2
        if packs == 1:
            return parts[0][:, :half], parts[0][:, half:]
        low = lax.broadcasted_iota(jnp.int32, parts[0].shape, 1) < half
        first, second = parts
        return (
            jnp.where(low, first, pltpu.roll(second, half, 1)),
            jnp.where(low, pltpu.roll(first, half, 1), second),
        )

    kept_ref[...], sent = sort(results)
    kept_lse_ref[...], rest = sort(logs)
    sent_ref[pl.ds(0, HD), :] = sent.astype(jnp.bfloat16)
    rest = jnp.concatenate([rest] * (rows // 8), axis=0)
    sublane = lax.broadcasted_iota(jnp.int32, rest.shape, 0)
    terms = jnp.zeros(rest.shape, jnp.float32)
    for n in range(3):
        term = rest.astype(jnp.bfloat16).astype(jnp.float32)
        terms = jnp.where(sublane == n, term, terms)
        rest = rest - term
    sent_ref[pl.ds(HD, rows), :] = terms.astype(jnp.bfloat16)


def fetch_kernel(kept_lse_ref, w_out, kept_lse_out, w_out_ref, sems):
    copies = []
    tp = w_out_ref.shape[0]
    part = w_out_ref.shape[-1]
    me_tp = lax.axis_index("tp")
    for d in range(tp):
        place = pl.ds(pl.multiple_of((me_tp ^ d) * part, HD), part)
        copies.append(pltpu.make_async_copy(w_out.at[:, place], w_out_ref.at[d], sems.at[d]))
    for copy in copies:
        copy.start()
    kept_lse_out[...] = kept_lse_ref[...]
    for copy in copies:
        copy.wait()


def multiply_out(sizes, ctx, w_out_ref, d, out_ref):
    steps, own, chunk = sizes
    for lower in range(0, out_ref.shape[-1], chunk):
        cols = pl.ds(lower, chunk)
        out = jnp.dot(ctx, w_out_ref[d, :, cols], preferred_element_type=jnp.float32)
        for s in range(steps):
            out_ref[s, :, cols] = out[s * own : (s + 1) * own].astype(out_ref.dtype)


def project_kernel(sizes, kept_ref, kept_lse_ref, got_ref, w_out_ref, ctx_ref, *outs):
    steps, own, tp, heads, chunk = sizes
    rows = steps * own
    terms = got_ref[pl.ds(HD, rows), :].astype(jnp.float32)
    lse_got = terms[0:1] + terms[1:2] + terms[2:3]
    lse_mine = kept_lse_ref[pl.ds(0, 1), :]
    top = jnp.maximum(lse_mine, lse_got)
    mine = jnp.exp(lse_mine - top)
    got = jnp.exp(lse_got - top)
    share = mine / (mine + got)
    ctx = kept_ref[...] * share + got_ref[pl.ds(0, HD), :].astype(jnp.float32) * (1.0 - share)
    ctx = ctx.T.astype(jnp.bfloat16)
    ctx = jnp.concatenate([ctx[h * rows : (h + 1) * rows] for h in range(heads)], axis=1)
    ctx_ref[...] = ctx
    for d in range(1, tp):
        multiply_out((steps, own, chunk), ctx, w_out_ref, d, outs[d - 1])


def project_own_kernel(sizes, ctx_ref, w_out_ref, out_ref):
    multiply_out(sizes, ctx_ref[...], w_out_ref, 0, out_ref)


def body(
    hidden_in,
    norm_gain,
    w_query,
    w_key,
    w_value,
    w_out,
    prompt_keys,
    prompt_values,
    gen_keys,
    gen_values,
    lengths,
    parents,
):
    steps, own, part = hidden_in.shape
    tp = lax.axis_size("tp")
    rows = steps * own
    width = w_query.shape[0]
    kv = w_key.shape[1] // HD
    group = w_query.shape[1] // w_key.shape[1]
    heads = kv * group
    history = gen_keys.shape[1]

    near_pieces = [across(hidden_in, 0, t) for t in range(1, tp)]
    far_pieces = [across(hidden_in, 1, t) for t in range(tp)]

    def in_hbm(x):
        return pltpu.with_memory_space_constraint(x, pltpu.HBM)

    def in_vmem(x):
        return pltpu.with_memory_space_constraint(x, pltpu.VMEM)

    vmem = pl.BlockSpec(memory_space=pltpu.VMEM)
    hbm = pl.BlockSpec(memory_space=pltpu.HBM)
    params = pltpu.CompilerParams(vmem_limit_bytes=16 * 2**20)
    f32, bf16 = jnp.float32, jnp.bfloat16
    blocks = prompt_keys.shape[1] // history
    old = (blocks + own) * history
    packed = 2 - kv % 2
    packs = kv // packed
    lanes = packed * group * 2 * rows
    loaded = pl.pallas_call(
        functools.partial(load_kernel, (steps, own, tp, kv, group, history, packed)),
        out_shape=(
            jax.ShapeDtypeStruct((1, width), f32),
            jax.ShapeDtypeStruct((rows, width), bf16),
            jax.ShapeDtypeStruct((rows, HD), f32),
            jax.ShapeDtypeStruct((rows, kv * HD), bf16),
            jax.ShapeDtypeStruct((kv * HD, old + HD), bf16),
            jax.ShapeDtypeStruct((HD // 2, lanes), f32),
            jax.ShapeDtypeStruct((HD // 2, lanes), f32),
            jax.ShapeDtypeStruct((old + rows, lanes), f32),
        ),
        in_specs=[hbm] * 8 + [vmem] * (tp - 1),
        out_specs=(vmem,) * 8,
        scratch_shapes=[
            pltpu.SMEM(lengths.shape, jnp.int32),
            pltpu.SMEM(parents.shape, jnp.int32),
            pltpu.VMEM(hidden_in.shape, bf16),
            pltpu.VMEM((tp, rows, part), f32),
            pltpu.VMEM(w_key.shape, bf16),
            pltpu.VMEM(w_value.shape, bf16),
            pltpu.VMEM((blocks + own, history, kv * HD), bf16),
            pltpu.SemaphoreType.DMA((16,)),
        ],
        compiler_params=params,
        name="load",
    )(
        *(
            in_hbm(x)
            for x in (
                lengths,
                parents,
                norm_gain[None, :],
                hidden_in,
                w_key,
                w_value,
                prompt_values.reshape(blocks, history, kv * HD),
                gen_values,
            )
        ),
        *near_pieces,
    )

    kept, kept_lse, sent = pl.pallas_call(
        functools.partial(attend_kernel, (steps, own, tp, kv, group, packed)),
        out_shape=(
            jax.ShapeDtypeStruct((HD, heads * rows), f32),
            jax.ShapeDtypeStruct((8, heads * rows), f32),
            jax.ShapeDtypeStruct((HD + rows, heads * rows), bf16),
        ),
        in_specs=[vmem] * (11 + tp),
        out_specs=(vmem,) * 3,
        scratch_shapes=[
            pltpu.VMEM((tp, rows, part), f32),
            pltpu.VMEM((2 * rows, width), bf16),
        ],
        compiler_params=params,
        name="attend",
    )(*loaded, in_vmem(w_query), in_vmem(prompt_keys), in_vmem(gen_keys), *far_pieces)

    got = permute_by(sent, "req", 1)
    kept_lse, w_out_near = pl.pallas_call(
        fetch_kernel,
        out_shape=(
            jax.ShapeDtypeStruct((8, heads * rows), f32),
            jax.ShapeDtypeStruct((tp, heads * HD, part), bf16),
        ),
        in_specs=[vmem, hbm],
        out_specs=(vmem, vmem),
        scratch_shapes=[pltpu.SemaphoreType.DMA((tp,))],
        compiler_params=params,
        name="fetch",
    )(kept_lse, in_hbm(w_out))

    chunk = math.gcd(part, 512)
    ctx, *sums = pl.pallas_call(
        functools.partial(project_kernel, (steps, own, tp, heads, chunk)),
        out_shape=(
            jax.ShapeDtypeStruct((rows, heads * HD), bf16),
            *[jax.ShapeDtypeStruct((steps, own, part), bf16)] * (tp - 1),
        ),
        in_specs=[vmem] * 4,
        out_specs=(vmem,) * tp,
        compiler_params=params,
        name="project",
    )(kept, kept_lse, got, w_out_near)
    sums = [across(x, 0, t + 1) for t, x in enumerate(sums)]
    total = pl.pallas_call(
        functools.partial(project_own_kernel, (steps, own, chunk)),
        out_shape=jax.ShapeDtypeStruct((steps, own, part), f32),
        in_specs=[vmem] * 2,
        out_specs=vmem,
        compiler_params=params,
        name="project_own",
    )(ctx, w_out_near)
    for x in sums:
        total = total + x.astype(f32)
    return total.astype(bf16)


def solution(mesh):
    in_specs = (
        P(None, "req", "tp"),
        P(),
        P(None, "tp"),
        P(None, "tp"),
        P(None, "tp"),
        P("tp", None),
        P("req", None, "tp"),
        P("req", None, "tp"),
        P("req", None, "tp"),
        P("req", None, "tp"),
        P(),
        P(),
    )
    out_specs = P(None, "req", "tp")
    return jax.shard_map(body, mesh=mesh, in_specs=in_specs, out_specs=out_specs, check_vma=False)
```

```python
import functools
import math

import jax
import jax.numpy as jnp
from jax import lax
from jax.experimental import pallas as pl
from jax.experimental.pallas import tpu as pltpu
from jax.sharding import PartitionSpec as P

HD = 128
BEAMS = 8

norm_eps = 1e-05
masked_score = -1e30
rope_base = 500000.0


def quotient(x, size):
    return x >> (size.bit_length() - 1) if size & (size - 1) == 0 else x // size


def remainder(x, size):
    return x & (size - 1) if size & (size - 1) == 0 else x % size


def permute_by(value, axis, distance):
    pairs = [(source, source ^ distance) for source in range(lax.axis_size(axis))]
    return lax.ppermute(value, axis, pairs)


def across(value, beam_distance, tp_distance):
    req, tp = lax.axis_size("req"), lax.axis_size("tp")
    pairs = [
        (r * tp + t, (r ^ beam_distance) * tp + (t ^ tp_distance))
        for r in range(req)
        for t in range(tp)
    ]
    return lax.ppermute(value, ("req", "tp"), pairs)


def lay_out(pieces, gain, x_s, xn_ref, first):
    steps, own, part = pieces[0].shape
    rows = steps * own
    me_tp = lax.axis_index("tp")
    total = jnp.zeros((rows, HD), jnp.float32)
    for t, piece in enumerate(pieces):
        column = pl.multiple_of((me_tp ^ t) * part, HD)
        for s in range(steps):
            x_s[t, pl.ds(s * own, own), :] = piece[s].astype(jnp.float32)
        mine = x_s[t]
        xn_ref[pl.ds(first, rows), pl.ds(column, part)] = (
            mine * gain[:, pl.ds(column, part)]
        ).astype(jnp.bfloat16)
        mine = mine * mine
        for c in range(part // HD):
            total = total + mine[:, c * HD : (c + 1) * HD]
    mean = jnp.sum(total, axis=-1, keepdims=True) / (part * len(pieces))
    return lax.rsqrt(mean + norm_eps)


def rotate(x, cosine, sine):
    return (x * cosine + pltpu.roll(x, HD // 2, 1) * sine).astype(jnp.bfloat16)


def load_kernel(
    sizes,
    lengths,
    parents,
    gain,
    hidden,
    wk,
    wv,
    pv,
    gv,
    *refs,
):
    steps, own, tp, kv, group, history, packed = sizes
    pieces = refs[: tp - 1]
    (
        gain_ref,
        xn_ref,
        scale_ref,
        new_keys_ref,
        values_ref,
        cosine_ref,
        sine_ref,
        bias_ref,
        lengths_s,
        parents_s,
        hidden_s,
        x_s,
        wk_s,
        wv_s,
        values_s,
        sems,
    ) = refs[tp - 1 :]
    rows = steps * own
    chunks = 6
    blocks = pv.shape[0]
    half_len = blocks * history
    free = half_len // 2
    device = lax.axis_index("req")
    request = device // 2
    parity = device % 2

    small = [
        (gain, gain_ref),
        (hidden, hidden_s),
        (lengths, lengths_s),
        (parents, parents_s),
    ]
    old = blocks + own
    large = [(pv, values_s.at[pl.ds(0, blocks)]), (gv, values_s.at[pl.ds(blocks, own)])]
    for source, target in ((wv, wv_s), (wk, wk_s)):
        size = source.shape[0] // chunks
        for n in range(chunks):
            place = pl.ds(n * size, size)
            large.append((source.at[place], target.at[place]))
    copies = [
        pltpu.make_async_copy(source, target, sems.at[n])
        for n, (source, target) in enumerate(small + large)
    ]
    for copy in copies:
        copy.start()
    large = copies[len(small) :]
    for copy in copies[: len(small)]:
        copy.wait()

    scale = lay_out((hidden_s, *pieces), gain_ref, x_s, xn_ref, 0)
    scale_ref[...] = jnp.broadcast_to(scale, scale_ref.shape)

    length = lengths_s[request]
    half_dim = HD // 2
    fall = -math.log(rope_base) / half_dim

    def angles(step, place):
        return (length + history + step).astype(jnp.float32) * jnp.exp(
            place.astype(jnp.float32) * fall
        )

    row = lax.broadcasted_iota(jnp.int32, (rows, HD), 0)
    lane = lax.broadcasted_iota(jnp.int32, (rows, HD), 1)
    angle = angles(quotient(row, own), remainder(lane, half_dim))
    key_cosine = jnp.cos(angle) * scale
    key_sine = jnp.sin(angle) * scale
    key_sine = jnp.where(lane < half_dim, -key_sine, key_sine)

    lanes = packed * group * 2 * rows
    place = lax.broadcasted_iota(jnp.int32, (half_dim, lanes), 0)
    lane = lax.broadcasted_iota(jnp.int32, (half_dim, lanes), 1)
    angle = angles(quotient(remainder(lane, rows), own), place)
    cosine_ref[...] = jnp.cos(angle)
    sine_ref[...] = jnp.sin(angle)

    def parent_of(s, beam):
        out = jnp.zeros_like(beam)
        for j in range(BEAMS):
            out = jnp.where(beam == j, parents_s[s, request * BEAMS + j], out)
        return out

    lane = lax.broadcasted_iota(jnp.int32, (8, lanes), 1)
    row_step = quotient(remainder(lane, rows), own)
    row_parity = jnp.where(lane < lanes // 2, parity, 1 - parity)
    beam = row_parity * own + remainder(lane, own)
    ancestors = [None] * steps
    at = beam
    for s in reversed(range(steps)):
        if s < steps - 1:
            at = jnp.where(row_step > s, parent_of(s + 1, at), beam)
        ancestors[s] = jnp.where(row_step >= s, at, -1)
    origin = parent_of(0, at)

    place = lax.broadcasted_iota(jnp.int32, (half_len - free, lanes), 0)
    place = parity * half_len + free + place
    bias_ref[pl.ds(0, half_len - free), :] = jnp.where(place < length, 0.0, masked_score)
    for n in range(own):
        seen = jnp.where(origin == parity * own + n, 0.0, masked_score)
        for c in range(0, history, 8):
            bias_ref[pl.ds(half_len - free + n * history + c, 8), :] = seen
    sublane = lax.broadcasted_iota(jnp.int32, (8, lanes), 0)
    for c in range(0, rows, 8):
        seen = jnp.full((8, lanes), masked_score, jnp.float32)
        for s in range(c // own, min((c + 8) // own, steps)):
            hit = (quotient(c + sublane, own) == s) & (
                ancestors[s] == parity * own + remainder(c + sublane, own)
            )
            seen = jnp.where(hit, 0.0, seen)
        bias_ref[pl.ds(old * history - free + c, 8), :] = seen

    for copy in large[:2]:
        copy.wait()
    values_ref[:, pl.ds(0, old * history)] = values_s[...].reshape(old * history, kv * HD).T

    def project(w_s, copies):
        size = w_s.shape[0] // chunks
        out = jnp.zeros((rows, kv * HD), jnp.float32)
        for n, copy in enumerate(copies):
            place = pl.ds(n * size, size)
            copy.wait()
            out += jnp.dot(xn_ref[:, place], w_s[place], preferred_element_type=jnp.float32)
        return out

    fresh = project(wv_s, large[2 : 2 + chunks]) * scale
    fresh = jnp.concatenate(
        [fresh, jnp.zeros((HD - rows, kv * HD), jnp.float32)], axis=0
    ).astype(jnp.bfloat16)
    values_ref[:, pl.ds(old * history, HD)] = fresh.T
    fresh = project(wk_s, large[2 + chunks :])
    for g in range(kv):
        cols = pl.ds(g * HD, HD)
        new_keys_ref[:, cols] = rotate(fresh[:, g * HD : (g + 1) * HD], key_cosine, key_sine)


def attend_kernel(
    sizes,
    gain_ref,
    xn_ref,
    scale_ref,
    new_keys_ref,
    values_ref,
    cosine_ref,
    sine_ref,
    bias_ref,
    wq_ref,
    pk_ref,
    gk_ref,
    w_out,
    *refs,
):
    steps, own, tp, kv, group, packed = sizes
    pieces = refs[:tp][::-1]
    kept_ref, kept_lse_ref, sent_ref, w_out_ref, x_s, xn_s, sems = refs[tp:]
    rows = steps * own
    part = pieces[0].shape[-1]
    packs = kv // packed
    each = packed * group
    size = each * HD
    lanes = each * 2 * rows
    keys_space = values_ref.shape[1]
    keys_count = keys_space - HD + rows
    free = keys_count - bias_ref.shape[0]
    lane = lax.broadcasted_iota(jnp.int32, (HD, lanes), 1)
    owner = quotient(remainder(lane, lanes // 2), group * rows)
    pad = jnp.zeros((keys_space - keys_count, lanes), jnp.bfloat16)

    me_tp = lax.axis_index("tp")
    copies = []
    for d in range(1, tp):
        place = pl.ds(pl.multiple_of((me_tp ^ d) * part, HD), part)
        copies.append(
            pltpu.make_async_copy(w_out.at[:, place], w_out_ref.at[d - 1], sems.at[d - 1])
        )
    for copy in copies:
        copy.start()

    xn_s[pl.ds(0, rows), :] = xn_ref[...]
    scale = lay_out(pieces, gain_ref, x_s, xn_s, rows)
    product = jnp.zeros((2 * rows, kv * group * HD), jnp.float32)
    for t in range(tp):
        place = pl.ds(pl.multiple_of((me_tp ^ t) * part, HD), part)
        product += jnp.dot(xn_s[:, place], wq_ref[place, :], preferred_element_type=jnp.float32)
    scale = jnp.concatenate([scale_ref[...], jnp.broadcast_to(scale, (rows, HD))], axis=0)
    scale = scale * HD**-0.5
    product = [product[:, h * HD : (h + 1) * HD] * scale for h in range(kv * group)]

    every = range(packs)
    cosine, sine = cosine_ref[...], sine_ref[...]
    scores = []
    for p in every:
        q = product[p * each : (p + 1) * each]
        q = jnp.concatenate([x[:rows] for x in q] + [x[rows:] for x in q], axis=0).T
        first, second = q[: HD // 2], q[HD // 2 :]
        q = jnp.concatenate(
            [first * cosine - second * sine, second * cosine + first * sine], axis=0
        )
        q = jnp.concatenate([jnp.where(owner == i, q, 0.0) for i in range(packed)], axis=0)
        cols = pl.ds(p * packed * HD, packed * HD)
        keys = jnp.concatenate(
            [
                pk_ref[0, :, cols],
                gk_ref[:, :, cols].reshape(-1, packed * HD),
                new_keys_ref[:, cols],
            ],
            axis=0,
        )
        score = jnp.dot(keys, q.astype(jnp.bfloat16), preferred_element_type=jnp.float32)
        scores.append(jnp.concatenate([score[:free], score[free:] + bias_ref[...]], axis=0))
    tops = [jnp.max(x, axis=0, keepdims=True) for x in scores]
    powers = [jnp.exp(x - top) for x, top in zip(scores, tops)]
    totals = [jnp.sum(x, axis=0, keepdims=True) for x in powers]
    mixed = [
        jnp.dot(
            values_ref[pl.ds(p * packed * HD, packed * HD), :],
            jnp.concatenate([powers[p].astype(jnp.bfloat16), pad], axis=0),
            preferred_element_type=jnp.float32,
        )
        for p in every
    ]
    results, logs = [], []
    for p in every:
        out = mixed[p][:HD]
        for i in range(1, packed):
            out = jnp.where(owner == i, mixed[p][i * HD : (i + 1) * HD], out)
        results.append(out * (1.0 / totals[p]))
        logs.append(jnp.broadcast_to(tops[p] + jnp.log(totals[p]), (8, lanes)))

    def sort(parts):
        half = lanes // 2
        if packs == 1:
            return parts[0][:, :half], parts[0][:, half:]
        low = lax.broadcasted_iota(jnp.int32, parts[0].shape, 1) < half
        first, second = parts
        return (
            jnp.where(low, first, pltpu.roll(second, half, 1)),
            jnp.where(low, pltpu.roll(first, half, 1), second),
        )

    kept_ref[...], sent = sort(results)
    kept_lse_ref[...], rest = sort(logs)
    sent_ref[pl.ds(0, HD), :] = sent.astype(jnp.bfloat16)
    rest = jnp.concatenate([rest] * (rows // 8), axis=0)
    sublane = lax.broadcasted_iota(jnp.int32, rest.shape, 0)
    terms = jnp.zeros(rest.shape, jnp.float32)
    for n in range(3):
        term = rest.astype(jnp.bfloat16).astype(jnp.float32)
        terms = jnp.where(sublane == n, term, terms)
        rest = rest - term
    sent_ref[pl.ds(HD, rows), :] = terms.astype(jnp.bfloat16)
    for copy in copies:
        copy.wait()


def fetch_kernel(kept_lse_ref, w_out, kept_lse_out, w_out_ref, sem):
    part = w_out_ref.shape[-1]
    place = pl.ds(pl.multiple_of(lax.axis_index("tp") * part, HD), part)
    copy = pltpu.make_async_copy(w_out.at[:, place], w_out_ref.at[0], sem.at[0])
    copy.start()
    kept_lse_out[...] = kept_lse_ref[...]
    copy.wait()


def multiply_out(sizes, ctx, w_out_ref, out_ref):
    steps, own, chunk = sizes
    for lower in range(0, out_ref.shape[-1], chunk):
        cols = pl.ds(lower, chunk)
        out = jnp.dot(ctx, w_out_ref[:, cols], preferred_element_type=jnp.float32)
        for s in range(steps):
            out_ref[s, :, cols] = out[s * own : (s + 1) * own].astype(out_ref.dtype)


def project_kernel(sizes, kept_ref, kept_lse_ref, got_ref, w_out_ref, ctx_ref, *outs):
    steps, own, tp, heads, chunk = sizes
    rows = steps * own
    terms = got_ref[pl.ds(HD, rows), :].astype(jnp.float32)
    lse_got = terms[0:1] + terms[1:2] + terms[2:3]
    lse_mine = kept_lse_ref[pl.ds(0, 1), :]
    top = jnp.maximum(lse_mine, lse_got)
    mine = jnp.exp(lse_mine - top)
    got = jnp.exp(lse_got - top)
    share = mine / (mine + got)
    ctx = kept_ref[...] * share + got_ref[pl.ds(0, HD), :].astype(jnp.float32) * (1.0 - share)
    ctx = ctx.T.astype(jnp.bfloat16)
    ctx = jnp.concatenate([ctx[h * rows : (h + 1) * rows] for h in range(heads)], axis=1)
    ctx_ref[...] = ctx
    for d in range(1, tp):
        multiply_out((steps, own, chunk), ctx, w_out_ref.at[d - 1], outs[d - 1])


def project_own_kernel(sizes, ctx_ref, w_out_ref, out_ref):
    multiply_out(sizes, ctx_ref[...], w_out_ref.at[0], out_ref)


def body(
    hidden_in,
    norm_gain,
    w_query,
    w_key,
    w_value,
    w_out,
    prompt_keys,
    prompt_values,
    gen_keys,
    gen_values,
    lengths,
    parents,
):
    steps, own, part = hidden_in.shape
    tp = lax.axis_size("tp")
    rows = steps * own
    width = w_query.shape[0]
    kv = w_key.shape[1] // HD
    group = w_query.shape[1] // w_key.shape[1]
    heads = kv * group
    history = gen_keys.shape[1]

    near_pieces = [across(hidden_in, 0, t) for t in range(1, tp)]
    far_pieces = [across(hidden_in, 1, t) for t in range(tp)]

    def in_hbm(x):
        return pltpu.with_memory_space_constraint(x, pltpu.HBM)

    def in_vmem(x):
        return pltpu.with_memory_space_constraint(x, pltpu.VMEM)

    vmem = pl.BlockSpec(memory_space=pltpu.VMEM)
    hbm = pl.BlockSpec(memory_space=pltpu.HBM)
    params = pltpu.CompilerParams(vmem_limit_bytes=16 * 2**20)
    f32, bf16 = jnp.float32, jnp.bfloat16
    blocks = prompt_keys.shape[1] // history
    old = (blocks + own) * history
    packed = 2 - kv % 2
    packs = kv // packed
    lanes = packed * group * 2 * rows
    loaded = pl.pallas_call(
        functools.partial(load_kernel, (steps, own, tp, kv, group, history, packed)),
        out_shape=(
            jax.ShapeDtypeStruct((1, width), f32),
            jax.ShapeDtypeStruct((rows, width), bf16),
            jax.ShapeDtypeStruct((rows, HD), f32),
            jax.ShapeDtypeStruct((rows, kv * HD), bf16),
            jax.ShapeDtypeStruct((kv * HD, old + HD), bf16),
            jax.ShapeDtypeStruct((HD // 2, lanes), f32),
            jax.ShapeDtypeStruct((HD // 2, lanes), f32),
            jax.ShapeDtypeStruct((old + rows - prompt_keys.shape[1] // 2, lanes), f32),
        ),
        in_specs=[hbm] * 8 + [vmem] * (tp - 1),
        out_specs=(vmem,) * 8,
        scratch_shapes=[
            pltpu.SMEM(lengths.shape, jnp.int32),
            pltpu.SMEM(parents.shape, jnp.int32),
            pltpu.VMEM(hidden_in.shape, bf16),
            pltpu.VMEM((tp, rows, part), f32),
            pltpu.VMEM(w_key.shape, bf16),
            pltpu.VMEM(w_value.shape, bf16),
            pltpu.VMEM((blocks + own, history, kv * HD), bf16),
            pltpu.SemaphoreType.DMA((18,)),
        ],
        compiler_params=params,
        name="load",
    )(
        *(
            in_hbm(x)
            for x in (
                lengths,
                parents,
                norm_gain[None, :],
                hidden_in,
                w_key,
                w_value,
                prompt_values.reshape(blocks, history, kv * HD),
                gen_values,
            )
        ),
        *near_pieces,
    )

    kept, kept_lse, sent, w_out_far = pl.pallas_call(
        functools.partial(attend_kernel, (steps, own, tp, kv, group, packed)),
        out_shape=(
            jax.ShapeDtypeStruct((HD, heads * rows), f32),
            jax.ShapeDtypeStruct((8, heads * rows), f32),
            jax.ShapeDtypeStruct((HD + rows, heads * rows), bf16),
            jax.ShapeDtypeStruct((tp - 1, heads * HD, part), bf16),
        ),
        in_specs=[vmem] * 11 + [hbm] + [vmem] * tp,
        out_specs=(vmem,) * 4,
        scratch_shapes=[
            pltpu.VMEM((tp, rows, part), f32),
            pltpu.VMEM((2 * rows, width), bf16),
            pltpu.SemaphoreType.DMA((tp - 1,)),
        ],
        compiler_params=params,
        name="attend",
    )(*loaded, in_vmem(w_query), in_vmem(prompt_keys), in_vmem(gen_keys), in_hbm(w_out), *far_pieces[::-1])

    got = permute_by(sent, "req", 1)
    kept_lse, w_out_near = pl.pallas_call(
        fetch_kernel,
        out_shape=(
            jax.ShapeDtypeStruct((8, heads * rows), f32),
            jax.ShapeDtypeStruct((tp, heads * HD, part), bf16),
        ),
        in_specs=[vmem, hbm],
        out_specs=(vmem, vmem),
        scratch_shapes=[pltpu.SemaphoreType.DMA((1,))],
        compiler_params=params,
        name="fetch",
    )(kept_lse, in_hbm(w_out))

    chunk = math.gcd(part, 512)
    ctx, *sums = pl.pallas_call(
        functools.partial(project_kernel, (steps, own, tp, heads, chunk)),
        out_shape=(
            jax.ShapeDtypeStruct((rows, heads * HD), bf16),
            *[jax.ShapeDtypeStruct((steps, own, part), bf16)] * (tp - 1),
        ),
        in_specs=[vmem] * 4,
        out_specs=(vmem,) * tp,
        compiler_params=params,
        name="project",
    )(kept, kept_lse, got, w_out_far)
    sums = [across(x, 0, t + 1) for t, x in enumerate(sums)]
    total = pl.pallas_call(
        functools.partial(project_own_kernel, (steps, own, chunk)),
        out_shape=jax.ShapeDtypeStruct((steps, own, part), f32),
        in_specs=[vmem] * 2,
        out_specs=vmem,
        compiler_params=params,
        name="project_own",
    )(ctx, w_out_near)
    for x in sums:
        total = total + x.astype(f32)
    return total.astype(bf16)


def solution(mesh):
    in_specs = (
        P(None, "req", "tp"),
        P(),
        P(None, "tp"),
        P(None, "tp"),
        P(None, "tp"),
        P("tp", None),
        P("req", None, "tp"),
        P("req", None, "tp"),
        P("req", None, "tp"),
        P("req", None, "tp"),
        P(),
        P(),
    )
    out_specs = P(None, "req", "tp")
    return jax.shard_map(body, mesh=mesh, in_specs=in_specs, out_specs=out_specs, check_vma=False)
```

```python
import functools
import math

import jax
import jax.numpy as jnp
from jax import lax
from jax.experimental import pallas as pl
from jax.experimental.pallas import tpu as pltpu
from jax.sharding import PartitionSpec as P

HD = 128
BEAMS = 8

norm_eps = 1e-05
masked_score = -1e30
rope_base = 500000.0


def quotient(x, size):
    return x >> (size.bit_length() - 1) if size & (size - 1) == 0 else x // size


def remainder(x, size):
    return x & (size - 1) if size & (size - 1) == 0 else x % size


def permute_by(value, axis, distance):
    pairs = [(source, source ^ distance) for source in range(lax.axis_size(axis))]
    return lax.ppermute(value, axis, pairs)


def across(value, beam_distance, tp_distance):
    req, tp = lax.axis_size("req"), lax.axis_size("tp")
    pairs = [
        (r * tp + t, (r ^ beam_distance) * tp + (t ^ tp_distance))
        for r in range(req)
        for t in range(tp)
    ]
    return lax.ppermute(value, ("req", "tp"), pairs)


def lay_out(pieces, gain, x_s, xn_ref, first):
    steps, own, part = pieces[0].shape
    rows = steps * own
    me_tp = lax.axis_index("tp")
    total = jnp.zeros((rows, HD), jnp.float32)
    for t, piece in enumerate(pieces):
        column = pl.multiple_of((me_tp ^ t) * part, HD)
        for s in range(steps):
            x_s[t, pl.ds(s * own, own), :] = piece[s].astype(jnp.float32)
        mine = x_s[t]
        xn_ref[pl.ds(first, rows), pl.ds(column, part)] = (
            mine * gain[:, pl.ds(column, part)]
        ).astype(jnp.bfloat16)
        mine = mine * mine
        for c in range(part // HD):
            total = total + mine[:, c * HD : (c + 1) * HD]
    mean = jnp.sum(total, axis=-1, keepdims=True) / (part * len(pieces))
    return lax.rsqrt(mean + norm_eps)


def rotate(x, cosine, sine):
    return (x * cosine + pltpu.roll(x, HD // 2, 1) * sine).astype(jnp.bfloat16)


def load_kernel(
    sizes,
    lengths,
    parents,
    gain,
    hidden,
    wk,
    wv,
    pv,
    gv,
    *refs,
):
    steps, own, tp, kv, group, history, packed = sizes
    pieces = refs[: tp - 1]
    (
        gain_ref,
        xn_ref,
        scale_ref,
        new_keys_ref,
        values_ref,
        cosine_ref,
        sine_ref,
        bias_ref,
        lengths_s,
        parents_s,
        hidden_s,
        x_s,
        wk_s,
        wv_s,
        values_s,
        sems,
    ) = refs[tp - 1 :]
    rows = steps * own
    chunks = 6
    blocks = pv.shape[0]
    half_len = blocks * history
    free = half_len // 2
    device = lax.axis_index("req")
    request = device // 2
    parity = device % 2

    small = [
        (gain, gain_ref),
        (hidden, hidden_s),
        (lengths, lengths_s),
        (parents, parents_s),
    ]
    old = blocks + own
    large = [(pv, values_s.at[pl.ds(0, blocks)]), (gv, values_s.at[pl.ds(blocks, own)])]
    for source, target in ((wv, wv_s), (wk, wk_s)):
        size = source.shape[0] // chunks
        for n in range(chunks):
            place = pl.ds(n * size, size)
            large.append((source.at[place], target.at[place]))
    copies = [
        pltpu.make_async_copy(source, target, sems.at[n])
        for n, (source, target) in enumerate(small + large)
    ]
    for copy in copies:
        copy.start()
    large = copies[len(small) :]
    for copy in copies[: len(small)]:
        copy.wait()

    scale = lay_out((hidden_s, *pieces), gain_ref, x_s, xn_ref, 0)
    scale_ref[...] = jnp.broadcast_to(scale, scale_ref.shape)

    length = lengths_s[request]
    half_dim = HD // 2
    fall = -math.log(rope_base) / half_dim

    def angles(step, place):
        return (length + history + step).astype(jnp.float32) * jnp.exp(
            place.astype(jnp.float32) * fall
        )

    row = lax.broadcasted_iota(jnp.int32, (rows, HD), 0)
    lane = lax.broadcasted_iota(jnp.int32, (rows, HD), 1)
    angle = angles(quotient(row, own), remainder(lane, half_dim))
    key_cosine = jnp.cos(angle) * scale
    key_sine = jnp.sin(angle) * scale
    key_sine = jnp.where(lane < half_dim, -key_sine, key_sine)

    lanes = packed * group * 2 * rows
    place = lax.broadcasted_iota(jnp.int32, (half_dim, lanes), 0)
    lane = lax.broadcasted_iota(jnp.int32, (half_dim, lanes), 1)
    angle = angles(quotient(remainder(lane, rows), own), place)
    cosine_ref[...] = jnp.cos(angle)
    sine_ref[...] = jnp.sin(angle)

    def parent_of(s, beam):
        out = jnp.zeros_like(beam)
        for j in range(BEAMS):
            out = jnp.where(beam == j, parents_s[s, request * BEAMS + j], out)
        return out

    lane = lax.broadcasted_iota(jnp.int32, (8, lanes), 1)
    row_step = quotient(remainder(lane, rows), own)
    row_parity = jnp.where(lane < lanes // 2, parity, 1 - parity)
    beam = row_parity * own + remainder(lane, own)
    ancestors = [None] * steps
    at = beam
    for s in reversed(range(steps)):
        if s < steps - 1:
            at = jnp.where(row_step > s, parent_of(s + 1, at), beam)
        ancestors[s] = jnp.where(row_step >= s, at, -1)
    origin = parent_of(0, at)

    place = lax.broadcasted_iota(jnp.int32, (half_len - free, lanes), 0)
    place = parity * half_len + free + place
    bias_ref[pl.ds(0, half_len - free), :] = jnp.where(place < length, 0.0, masked_score)
    for n in range(own):
        seen = jnp.where(origin == parity * own + n, 0.0, masked_score)
        for c in range(0, history, 8):
            bias_ref[pl.ds(half_len - free + n * history + c, 8), :] = seen
    sublane = lax.broadcasted_iota(jnp.int32, (8, lanes), 0)
    for c in range(0, rows, 8):
        seen = jnp.full((8, lanes), masked_score, jnp.float32)
        for s in range(c // own, min((c + 8) // own, steps)):
            hit = (quotient(c + sublane, own) == s) & (
                ancestors[s] == parity * own + remainder(c + sublane, own)
            )
            seen = jnp.where(hit, 0.0, seen)
        bias_ref[pl.ds(old * history - free + c, 8), :] = seen

    for copy in large[:2]:
        copy.wait()
    values_ref[:, pl.ds(0, old * history)] = values_s[...].reshape(old * history, kv * HD).T

    def project(w_s, copies):
        size = w_s.shape[0] // chunks
        out = jnp.zeros((rows, kv * HD), jnp.float32)
        for n, copy in enumerate(copies):
            place = pl.ds(n * size, size)
            copy.wait()
            out += jnp.dot(xn_ref[:, place], w_s[place], preferred_element_type=jnp.float32)
        return out

    fresh = project(wv_s, large[2 : 2 + chunks]) * scale
    fresh = jnp.concatenate(
        [fresh, jnp.zeros((HD - rows, kv * HD), jnp.float32)], axis=0
    ).astype(jnp.bfloat16)
    values_ref[:, pl.ds(old * history, HD)] = fresh.T
    fresh = project(wk_s, large[2 + chunks :])
    for g in range(kv):
        cols = pl.ds(g * HD, HD)
        new_keys_ref[:, cols] = rotate(fresh[:, g * HD : (g + 1) * HD], key_cosine, key_sine)


def attend_kernel(
    sizes,
    gain_ref,
    xn_ref,
    scale_ref,
    new_keys_ref,
    values_ref,
    cosine_ref,
    sine_ref,
    bias_ref,
    wq_ref,
    pk_ref,
    gk_ref,
    *refs,
):
    steps, own, tp, kv, group, packed = sizes
    pieces = refs[:tp][::-1]
    kept_ref, kept_lse_ref, sent_ref, x_s, xn_s = refs[tp:]
    rows = steps * own
    part = pieces[0].shape[-1]
    packs = kv // packed
    each = packed * group
    size = each * HD
    lanes = each * 2 * rows
    keys_space = values_ref.shape[1]
    keys_count = keys_space - HD + rows
    free = keys_count - bias_ref.shape[0]
    lane = lax.broadcasted_iota(jnp.int32, (HD, lanes), 1)
    owner = quotient(remainder(lane, lanes // 2), group * rows)
    pad = jnp.zeros((keys_space - keys_count, lanes), jnp.bfloat16)

    xn_s[pl.ds(0, rows), :] = xn_ref[...]
    scale = lay_out(pieces, gain_ref, x_s, xn_s, rows)
    me_tp = lax.axis_index("tp")
    product = jnp.zeros((2 * rows, kv * group * HD), jnp.float32)
    for t in range(tp):
        place = pl.ds(pl.multiple_of((me_tp ^ t) * part, HD), part)
        product += jnp.dot(xn_s[:, place], wq_ref[place, :], preferred_element_type=jnp.float32)
    scale = jnp.concatenate([scale_ref[...], jnp.broadcast_to(scale, (rows, HD))], axis=0)
    scale = scale * HD**-0.5
    product = [product[:, h * HD : (h + 1) * HD] * scale for h in range(kv * group)]

    every = range(packs)
    cosine, sine = cosine_ref[...], sine_ref[...]
    scores = []
    for p in every:
        q = product[p * each : (p + 1) * each]
        q = jnp.concatenate([x[:rows] for x in q] + [x[rows:] for x in q], axis=0).T
        first, second = q[: HD // 2], q[HD // 2 :]
        q = jnp.concatenate(
            [first * cosine - second * sine, second * cosine + first * sine], axis=0
        )
        q = jnp.concatenate([jnp.where(owner == i, q, 0.0) for i in range(packed)], axis=0)
        cols = pl.ds(p * packed * HD, packed * HD)
        keys = jnp.concatenate(
            [
                pk_ref[0, :, cols],
                gk_ref[:, :, cols].reshape(-1, packed * HD),
                new_keys_ref[:, cols],
            ],
            axis=0,
        )
        score = jnp.dot(keys, q.astype(jnp.bfloat16), preferred_element_type=jnp.float32)
        scores.append(jnp.concatenate([score[:free], score[free:] + bias_ref[...]], axis=0))
    tops = [jnp.max(x, axis=0, keepdims=True) for x in scores]
    powers = [jnp.exp(x - top) for x, top in zip(scores, tops)]
    totals = [jnp.sum(x, axis=0, keepdims=True) for x in powers]
    mixed = [
        jnp.dot(
            values_ref[pl.ds(p * packed * HD, packed * HD), :],
            jnp.concatenate([powers[p].astype(jnp.bfloat16), pad], axis=0),
            preferred_element_type=jnp.float32,
        )
        for p in every
    ]
    results, logs = [], []
    for p in every:
        out = mixed[p][:HD]
        for i in range(1, packed):
            out = jnp.where(owner == i, mixed[p][i * HD : (i + 1) * HD], out)
        results.append(out * (1.0 / totals[p]))
        logs.append(jnp.broadcast_to(tops[p] + jnp.log(totals[p]), (8, lanes)))

    def sort(parts):
        half = lanes // 2
        if packs == 1:
            return parts[0][:, :half], parts[0][:, half:]
        low = lax.broadcasted_iota(jnp.int32, parts[0].shape, 1) < half
        first, second = parts
        return (
            jnp.where(low, first, pltpu.roll(second, half, 1)),
            jnp.where(low, pltpu.roll(first, half, 1), second),
        )

    kept_ref[...], sent = sort(results)
    kept_lse_ref[...], rest = sort(logs)
    sent_ref[pl.ds(0, HD), :] = sent.astype(jnp.bfloat16)
    rest = jnp.concatenate([rest] * (rows // 8), axis=0)
    sublane = lax.broadcasted_iota(jnp.int32, rest.shape, 0)
    terms = jnp.zeros(rest.shape, jnp.float32)
    for n in range(3):
        term = rest.astype(jnp.bfloat16).astype(jnp.float32)
        terms = jnp.where(sublane == n, term, terms)
        rest = rest - term
    sent_ref[pl.ds(HD, rows), :] = terms.astype(jnp.bfloat16)


def fetch_kernel(kept_lse_ref, w_out, kept_lse_out, w_out_ref, sems):
    tp, depth, part = w_out_ref.shape
    me_tp = lax.axis_index("tp")
    copies = []
    for d in range(1, tp):
        cols = pl.ds(pl.multiple_of((me_tp ^ d) * part, HD), part)
        for n in range(2):
            rows = pl.ds(n * (depth // 2), depth // 2)
            copies.append(
                pltpu.make_async_copy(
                    w_out.at[rows, cols], w_out_ref.at[d - 1, rows], sems.at[2 * d - 2 + n]
                )
            )
    for copy in copies:
        copy.start()
    kept_lse_out[...] = kept_lse_ref[...]
    for copy in copies:
        copy.wait()


def multiply_out(sizes, ctx, w_out_ref, first, out_ref):
    steps, own, chunk = sizes
    for lower in range(0, out_ref.shape[-1], chunk):
        place = pl.ds(pl.multiple_of(first + lower, HD), chunk)
        out = jnp.dot(ctx, w_out_ref[:, place], preferred_element_type=jnp.float32)
        for s in range(steps):
            out_ref[s, :, pl.ds(lower, chunk)] = out[s * own : (s + 1) * own].astype(out_ref.dtype)


def project_kernel(sizes, kept_ref, kept_lse_ref, got_ref, w_out_ref, ctx_ref, *outs):
    steps, own, tp, heads, chunk = sizes
    rows = steps * own
    terms = got_ref[pl.ds(HD, rows), :].astype(jnp.float32)
    lse_got = terms[0:1] + terms[1:2] + terms[2:3]
    lse_mine = kept_lse_ref[pl.ds(0, 1), :]
    top = jnp.maximum(lse_mine, lse_got)
    mine = jnp.exp(lse_mine - top)
    got = jnp.exp(lse_got - top)
    share = mine / (mine + got)
    ctx = kept_ref[...] * share + got_ref[pl.ds(0, HD), :].astype(jnp.float32) * (1.0 - share)
    ctx = ctx.T.astype(jnp.bfloat16)
    ctx = jnp.concatenate([ctx[h * rows : (h + 1) * rows] for h in range(heads)], axis=1)
    ctx_ref[...] = ctx
    for d in range(1, tp):
        multiply_out((steps, own, chunk), ctx, w_out_ref.at[d - 1], 0, outs[d - 1])


def project_own_kernel(sizes, ctx_ref, w_out_ref, out_ref):
    first = lax.axis_index("tp") * out_ref.shape[-1]
    multiply_out(sizes, ctx_ref[...], w_out_ref, first, out_ref)


def body(
    hidden_in,
    norm_gain,
    w_query,
    w_key,
    w_value,
    w_out,
    prompt_keys,
    prompt_values,
    gen_keys,
    gen_values,
    lengths,
    parents,
):
    steps, own, part = hidden_in.shape
    tp = lax.axis_size("tp")
    rows = steps * own
    width = w_query.shape[0]
    kv = w_key.shape[1] // HD
    group = w_query.shape[1] // w_key.shape[1]
    heads = kv * group
    history = gen_keys.shape[1]

    near_pieces = [across(hidden_in, 0, t) for t in range(1, tp)]
    far_pieces = [across(hidden_in, 1, t) for t in range(tp)]

    def in_hbm(x):
        return pltpu.with_memory_space_constraint(x, pltpu.HBM)

    def in_vmem(x):
        return pltpu.with_memory_space_constraint(x, pltpu.VMEM)

    vmem = pl.BlockSpec(memory_space=pltpu.VMEM)
    hbm = pl.BlockSpec(memory_space=pltpu.HBM)
    params = pltpu.CompilerParams(vmem_limit_bytes=16 * 2**20)
    f32, bf16 = jnp.float32, jnp.bfloat16
    blocks = prompt_keys.shape[1] // history
    old = (blocks + own) * history
    packed = 2 - kv % 2
    packs = kv // packed
    lanes = packed * group * 2 * rows
    loaded = pl.pallas_call(
        functools.partial(load_kernel, (steps, own, tp, kv, group, history, packed)),
        out_shape=(
            jax.ShapeDtypeStruct((1, width), f32),
            jax.ShapeDtypeStruct((rows, width), bf16),
            jax.ShapeDtypeStruct((rows, HD), f32),
            jax.ShapeDtypeStruct((rows, kv * HD), bf16),
            jax.ShapeDtypeStruct((kv * HD, old + HD), bf16),
            jax.ShapeDtypeStruct((HD // 2, lanes), f32),
            jax.ShapeDtypeStruct((HD // 2, lanes), f32),
            jax.ShapeDtypeStruct((old + rows - prompt_keys.shape[1] // 2, lanes), f32),
        ),
        in_specs=[hbm] * 8 + [vmem] * (tp - 1),
        out_specs=(vmem,) * 8,
        scratch_shapes=[
            pltpu.SMEM(lengths.shape, jnp.int32),
            pltpu.SMEM(parents.shape, jnp.int32),
            pltpu.VMEM(hidden_in.shape, bf16),
            pltpu.VMEM((tp, rows, part), f32),
            pltpu.VMEM(w_key.shape, bf16),
            pltpu.VMEM(w_value.shape, bf16),
            pltpu.VMEM((blocks + own, history, kv * HD), bf16),
            pltpu.SemaphoreType.DMA((18,)),
        ],
        compiler_params=params,
        name="load",
    )(
        *(
            in_hbm(x)
            for x in (
                lengths,
                parents,
                norm_gain[None, :],
                hidden_in,
                w_key,
                w_value,
                prompt_values.reshape(blocks, history, kv * HD),
                gen_values,
            )
        ),
        *near_pieces,
    )

    kept, kept_lse, sent = pl.pallas_call(
        functools.partial(attend_kernel, (steps, own, tp, kv, group, packed)),
        out_shape=(
            jax.ShapeDtypeStruct((HD, heads * rows), f32),
            jax.ShapeDtypeStruct((8, heads * rows), f32),
            jax.ShapeDtypeStruct((HD + rows, heads * rows), bf16),
        ),
        in_specs=[vmem] * (11 + tp),
        out_specs=(vmem,) * 3,
        scratch_shapes=[
            pltpu.VMEM((tp, rows, part), f32),
            pltpu.VMEM((2 * rows, width), bf16),
        ],
        compiler_params=params,
        name="attend",
    )(*loaded, in_vmem(w_query), in_vmem(prompt_keys), in_vmem(gen_keys), *far_pieces[::-1])

    got = permute_by(sent, "req", 1)
    kept_lse, w_out_far = pl.pallas_call(
        fetch_kernel,
        out_shape=(
            jax.ShapeDtypeStruct((8, heads * rows), f32),
            jax.ShapeDtypeStruct((tp, heads * HD, part), bf16),
        ),
        in_specs=[vmem, hbm],
        out_specs=(vmem, vmem),
        scratch_shapes=[pltpu.SemaphoreType.DMA((2 * tp - 2,))],
        compiler_params=params,
        name="fetch",
    )(kept_lse, in_hbm(w_out))

    chunk = math.gcd(part, 512)
    ctx, *sums = pl.pallas_call(
        functools.partial(project_kernel, (steps, own, tp, heads, chunk)),
        out_shape=(
            jax.ShapeDtypeStruct((rows, heads * HD), bf16),
            *[jax.ShapeDtypeStruct((steps, own, part), bf16)] * (tp - 1),
        ),
        in_specs=[vmem] * 4,
        out_specs=(vmem,) * tp,
        compiler_params=params,
        name="project",
    )(kept, kept_lse, got, w_out_far)
    sums = [across(x, 0, t + 1) for t, x in enumerate(sums)]
    total = pl.pallas_call(
        functools.partial(project_own_kernel, (steps, own, chunk)),
        out_shape=jax.ShapeDtypeStruct((steps, own, part), f32),
        in_specs=[vmem] * 2,
        out_specs=vmem,
        compiler_params=params,
        name="project_own",
    )(ctx, in_vmem(w_out))
    for x in sums:
        total = total + x.astype(f32)
    return total.astype(bf16)


def solution(mesh):
    in_specs = (
        P(None, "req", "tp"),
        P(),
        P(None, "tp"),
        P(None, "tp"),
        P(None, "tp"),
        P("tp", None),
        P("req", None, "tp"),
        P("req", None, "tp"),
        P("req", None, "tp"),
        P("req", None, "tp"),
        P(),
        P(),
    )
    out_specs = P(None, "req", "tp")
    return jax.shard_map(body, mesh=mesh, in_specs=in_specs, out_specs=out_specs, check_vma=False)
```

```python
import functools
import math

import jax
import jax.numpy as jnp
from jax import lax
from jax.experimental import pallas as pl
from jax.experimental.pallas import tpu as pltpu
from jax.sharding import PartitionSpec as P

HD = 128
BEAMS = 8

norm_eps = 1e-05
masked_score = -1e30
rope_base = 500000.0


def quotient(x, size):
    return x >> (size.bit_length() - 1) if size & (size - 1) == 0 else x // size


def remainder(x, size):
    return x & (size - 1) if size & (size - 1) == 0 else x % size


def permute_by(value, axis, distance):
    pairs = [(source, source ^ distance) for source in range(lax.axis_size(axis))]
    return lax.ppermute(value, axis, pairs)


def across(value, beam_distance, tp_distance):
    req, tp = lax.axis_size("req"), lax.axis_size("tp")
    pairs = [
        (r * tp + t, (r ^ beam_distance) * tp + (t ^ tp_distance))
        for r in range(req)
        for t in range(tp)
    ]
    return lax.ppermute(value, ("req", "tp"), pairs)


def lay_out(pieces, gain, x_s, xn_ref, first):
    steps, own, part = pieces[0].shape
    rows = steps * own
    me_tp = lax.axis_index("tp")
    total = jnp.zeros((rows, HD), jnp.float32)
    for t, piece in enumerate(pieces):
        column = pl.multiple_of((me_tp ^ t) * part, HD)
        for s in range(steps):
            x_s[t, pl.ds(s * own, own), :] = piece[s].astype(jnp.float32)
        mine = x_s[t]
        xn_ref[pl.ds(first, rows), pl.ds(column, part)] = (
            mine * gain[:, pl.ds(column, part)]
        ).astype(jnp.bfloat16)
        mine = mine * mine
        for c in range(part // HD):
            total = total + mine[:, c * HD : (c + 1) * HD]
    mean = jnp.sum(total, axis=-1, keepdims=True) / (part * len(pieces))
    return lax.rsqrt(mean + norm_eps)


def rotate(x, cosine, sine):
    return (x * cosine + pltpu.roll(x, HD // 2, 1) * sine).astype(jnp.bfloat16)


def prepare_kernel(sizes, lengths, parents, gain, hidden, *refs):
    steps, own, tp, group, history, half_len, packed = sizes
    pieces = refs[: tp - 1]
    (
        gain_ref,
        xn_ref,
        scale_ref,
        key_cosine_ref,
        key_sine_ref,
        cosine_ref,
        sine_ref,
        bias_ref,
        lengths_s,
        parents_s,
        hidden_s,
        x_s,
        sems,
    ) = refs[tp - 1 :]
    rows = steps * own
    free = half_len // 2
    device = lax.axis_index("req")
    request = device // 2
    parity = device % 2

    copies = [
        pltpu.make_async_copy(source, target, sems.at[n])
        for n, (source, target) in enumerate(
            ((gain, gain_ref), (hidden, hidden_s), (lengths, lengths_s), (parents, parents_s))
        )
    ]
    for copy in copies:
        copy.start()
    for copy in copies:
        copy.wait()

    scale = lay_out((hidden_s, *pieces), gain_ref, x_s, xn_ref, 0)
    scale_ref[...] = jnp.broadcast_to(scale, scale_ref.shape)

    length = lengths_s[request]
    half_dim = HD // 2
    fall = -math.log(rope_base) / half_dim

    def angles(step, place):
        return (length + history + step).astype(jnp.float32) * jnp.exp(
            place.astype(jnp.float32) * fall
        )

    row = lax.broadcasted_iota(jnp.int32, (rows, HD), 0)
    lane = lax.broadcasted_iota(jnp.int32, (rows, HD), 1)
    angle = angles(quotient(row, own), remainder(lane, half_dim))
    key_cosine_ref[...] = jnp.cos(angle) * scale
    key_sine = jnp.sin(angle) * scale
    key_sine_ref[...] = jnp.where(lane < half_dim, -key_sine, key_sine)

    lanes = packed * group * 2 * rows
    place = lax.broadcasted_iota(jnp.int32, (half_dim, lanes), 0)
    lane = lax.broadcasted_iota(jnp.int32, (half_dim, lanes), 1)
    angle = angles(quotient(remainder(lane, rows), own), place)
    cosine_ref[...] = jnp.cos(angle)
    sine_ref[...] = jnp.sin(angle)

    def parent_of(s, beam):
        out = jnp.zeros_like(beam)
        for j in range(BEAMS):
            out = jnp.where(beam == j, parents_s[s, request * BEAMS + j], out)
        return out

    lane = lax.broadcasted_iota(jnp.int32, (8, lanes), 1)
    row_step = quotient(remainder(lane, rows), own)
    row_parity = jnp.where(lane < lanes // 2, parity, 1 - parity)
    beam = row_parity * own + remainder(lane, own)
    ancestors = [None] * steps
    at = beam
    for s in reversed(range(steps)):
        if s < steps - 1:
            at = jnp.where(row_step > s, parent_of(s + 1, at), beam)
        ancestors[s] = jnp.where(row_step >= s, at, -1)
    origin = parent_of(0, at)

    place = lax.broadcasted_iota(jnp.int32, (half_len - free, lanes), 0)
    place = parity * half_len + free + place
    bias_ref[pl.ds(0, half_len - free), :] = jnp.where(place < length, 0.0, masked_score)
    for n in range(own):
        seen = jnp.where(origin == parity * own + n, 0.0, masked_score)
        for c in range(0, history, 8):
            bias_ref[pl.ds(half_len - free + n * history + c, 8), :] = seen
    sublane = lax.broadcasted_iota(jnp.int32, (8, lanes), 0)
    for c in range(0, rows, 8):
        seen = jnp.full((8, lanes), masked_score, jnp.float32)
        for s in range(c // own, min((c + 8) // own, steps)):
            hit = (quotient(c + sublane, own) == s) & (
                ancestors[s] == parity * own + remainder(c + sublane, own)
            )
            seen = jnp.where(hit, 0.0, seen)
        bias_ref[pl.ds(half_len + own * history - free + c, 8), :] = seen


def fresh_kernel(
    xn_ref,
    scale_ref,
    key_cosine_ref,
    key_sine_ref,
    wk_ref,
    wv_ref,
    pv_ref,
    gv_ref,
    new_keys_ref,
    values_ref,
):
    rows = xn_ref.shape[0]
    half_len, width = pv_ref.shape[1:]
    old = values_ref.shape[1] - HD
    xn = xn_ref[...]
    keys = jnp.dot(xn, wk_ref[...], preferred_element_type=jnp.float32)
    values = jnp.dot(xn, wv_ref[...], preferred_element_type=jnp.float32)
    values_ref[:, pl.ds(0, half_len)] = pv_ref[0].T
    values_ref[:, pl.ds(half_len, old - half_len)] = gv_ref[...].reshape(-1, width).T
    for g in range(width // HD):
        cols = pl.ds(g * HD, HD)
        new_keys_ref[:, cols] = rotate(
            keys[:, g * HD : (g + 1) * HD], key_cosine_ref[...], key_sine_ref[...]
        )
    scale = scale_ref[...]
    values = [values[:, g * HD : (g + 1) * HD] * scale for g in range(width // HD)]
    values = jnp.concatenate(
        [jnp.concatenate(values, axis=1), jnp.zeros((HD - rows, width), jnp.float32)], axis=0
    )
    values_ref[:, pl.ds(old, HD)] = values.astype(jnp.bfloat16).T


def attend_kernel(
    sizes,
    gain_ref,
    xn_ref,
    scale_ref,
    new_keys_ref,
    values_ref,
    cosine_ref,
    sine_ref,
    bias_ref,
    wq_ref,
    pk_ref,
    gk_ref,
    *refs,
):
    steps, own, tp, kv, group, packed = sizes
    pieces = refs[:tp][::-1]
    kept_ref, kept_lse_ref, sent_ref, x_s, xn_s = refs[tp:]
    rows = steps * own
    part = pieces[0].shape[-1]
    packs = kv // packed
    each = packed * group
    size = each * HD
    lanes = each * 2 * rows
    keys_space = values_ref.shape[1]
    keys_count = keys_space - HD + rows
    free = keys_count - bias_ref.shape[0]
    lane = lax.broadcasted_iota(jnp.int32, (HD, lanes), 1)
    owner = quotient(remainder(lane, lanes // 2), group * rows)
    pad = jnp.zeros((keys_space - keys_count, lanes), jnp.bfloat16)

    xn_s[pl.ds(0, rows), :] = xn_ref[...]
    scale = lay_out(pieces, gain_ref, x_s, xn_s, rows)
    product = [
        jnp.dot(xn_s[...], wq_ref[:, pl.ds(p * size, size)], preferred_element_type=jnp.float32)
        for p in range(packs)
    ]
    scale = jnp.concatenate([scale_ref[...], jnp.broadcast_to(scale, (rows, HD))], axis=0)
    scale = scale * HD**-0.5
    product = [x[:, h * HD : (h + 1) * HD] * scale for x in product for h in range(each)]

    every = range(packs)
    cosine, sine = cosine_ref[...], sine_ref[...]
    scores = []
    for p in every:
        q = product[p * each : (p + 1) * each]
        q = jnp.concatenate([x[:rows] for x in q] + [x[rows:] for x in q], axis=0).T
        first, second = q[: HD // 2], q[HD // 2 :]
        q = jnp.concatenate(
            [first * cosine - second * sine, second * cosine + first * sine], axis=0
        )
        q = jnp.concatenate([jnp.where(owner == i, q, 0.0) for i in range(packed)], axis=0)
        cols = pl.ds(p * packed * HD, packed * HD)
        keys = jnp.concatenate(
            [
                pk_ref[0, :, cols],
                gk_ref[:, :, cols].reshape(-1, packed * HD),
                new_keys_ref[:, cols],
            ],
            axis=0,
        )
        score = jnp.dot(keys, q.astype(jnp.bfloat16), preferred_element_type=jnp.float32)
        scores.append(jnp.concatenate([score[:free], score[free:] + bias_ref[...]], axis=0))
    tops = [jnp.max(x, axis=0, keepdims=True) for x in scores]
    powers = [jnp.exp(x - top) for x, top in zip(scores, tops)]
    totals = [jnp.sum(x, axis=0, keepdims=True) for x in powers]
    mixed = [
        jnp.dot(
            values_ref[pl.ds(p * packed * HD, packed * HD), :],
            jnp.concatenate([powers[p].astype(jnp.bfloat16), pad], axis=0),
            preferred_element_type=jnp.float32,
        )
        for p in every
    ]
    results, logs = [], []
    for p in every:
        out = mixed[p][:HD]
        for i in range(1, packed):
            out = jnp.where(owner == i, mixed[p][i * HD : (i + 1) * HD], out)
        results.append(out * (1.0 / totals[p]))
        logs.append(jnp.broadcast_to(tops[p] + jnp.log(totals[p]), (8, lanes)))

    def sort(parts):
        half = lanes // 2
        if packs == 1:
            return parts[0][:, :half], parts[0][:, half:]
        low = lax.broadcasted_iota(jnp.int32, parts[0].shape, 1) < half
        first, second = parts
        return (
            jnp.where(low, first, pltpu.roll(second, half, 1)),
            jnp.where(low, pltpu.roll(first, half, 1), second),
        )

    kept_ref[...], sent = sort(results)
    kept_lse_ref[...], rest = sort(logs)
    sent_ref[pl.ds(0, HD), :] = sent.astype(jnp.bfloat16)
    rest = jnp.concatenate([rest] * (rows // 8), axis=0)
    sublane = lax.broadcasted_iota(jnp.int32, rest.shape, 0)
    terms = jnp.zeros(rest.shape, jnp.float32)
    for n in range(3):
        term = rest.astype(jnp.bfloat16).astype(jnp.float32)
        terms = jnp.where(sublane == n, term, terms)
        rest = rest - term
    sent_ref[pl.ds(HD, rows), :] = terms.astype(jnp.bfloat16)


def fetch_kernel(kept_lse_ref, w_out, kept_lse_out, w_out_ref, sems):
    tp, depth, part = w_out_ref.shape
    me_tp = lax.axis_index("tp")
    copies = []
    for d in range(1, tp):
        cols = pl.ds(pl.multiple_of((me_tp ^ d) * part, HD), part)
        for n in range(2):
            rows = pl.ds(n * (depth // 2), depth // 2)
            copies.append(
                pltpu.make_async_copy(
                    w_out.at[rows, cols], w_out_ref.at[d - 1, rows], sems.at[2 * d - 2 + n]
                )
            )
    for copy in copies:
        copy.start()
    kept_lse_out[...] = kept_lse_ref[...]
    for copy in copies:
        copy.wait()


def multiply_out(sizes, ctx, w_out_ref, first, out_ref):
    steps, own, chunk = sizes
    for lower in range(0, out_ref.shape[-1], chunk):
        place = pl.ds(pl.multiple_of(first + lower, HD), chunk)
        out = jnp.dot(ctx, w_out_ref[:, place], preferred_element_type=jnp.float32)
        for s in range(steps):
            out_ref[s, :, pl.ds(lower, chunk)] = out[s * own : (s + 1) * own].astype(out_ref.dtype)


def project_kernel(sizes, kept_ref, kept_lse_ref, got_ref, w_out_ref, ctx_ref, *outs):
    steps, own, tp, heads, chunk = sizes
    rows = steps * own
    terms = got_ref[pl.ds(HD, rows), :].astype(jnp.float32)
    lse_got = terms[0:1] + terms[1:2] + terms[2:3]
    lse_mine = kept_lse_ref[pl.ds(0, 1), :]
    top = jnp.maximum(lse_mine, lse_got)
    mine = jnp.exp(lse_mine - top)
    got = jnp.exp(lse_got - top)
    share = mine / (mine + got)
    ctx = kept_ref[...] * share + got_ref[pl.ds(0, HD), :].astype(jnp.float32) * (1.0 - share)
    ctx = ctx.T.astype(jnp.bfloat16)
    ctx = jnp.concatenate([ctx[h * rows : (h + 1) * rows] for h in range(heads)], axis=1)
    ctx_ref[...] = ctx
    for d in range(1, tp):
        multiply_out((steps, own, chunk), ctx, w_out_ref.at[d - 1], 0, outs[d - 1])


def project_own_kernel(sizes, ctx_ref, w_out_ref, out_ref):
    first = lax.axis_index("tp") * out_ref.shape[-1]
    multiply_out(sizes, ctx_ref[...], w_out_ref, first, out_ref)


def body(
    hidden_in,
    norm_gain,
    w_query,
    w_key,
    w_value,
    w_out,
    prompt_keys,
    prompt_values,
    gen_keys,
    gen_values,
    lengths,
    parents,
):
    steps, own, part = hidden_in.shape
    tp = lax.axis_size("tp")
    rows = steps * own
    width = w_query.shape[0]
    kv = w_key.shape[1] // HD
    group = w_query.shape[1] // w_key.shape[1]
    heads = kv * group
    history = gen_keys.shape[1]

    near_pieces = [across(hidden_in, 0, t) for t in range(1, tp)]
    far_pieces = [across(hidden_in, 1, t) for t in range(tp)]

    def in_hbm(x):
        return pltpu.with_memory_space_constraint(x, pltpu.HBM)

    def in_vmem(x):
        return pltpu.with_memory_space_constraint(x, pltpu.VMEM)

    vmem = pl.BlockSpec(memory_space=pltpu.VMEM)
    hbm = pl.BlockSpec(memory_space=pltpu.HBM)
    params = pltpu.CompilerParams(vmem_limit_bytes=16 * 2**20)
    f32, bf16 = jnp.float32, jnp.bfloat16
    half_len = prompt_keys.shape[1]
    old = half_len + own * history
    packed = 2 - kv % 2
    lanes = packed * group * 2 * rows
    gain, xn, scale, key_cosine, key_sine, cosine, sine, bias = pl.pallas_call(
        functools.partial(prepare_kernel, (steps, own, tp, group, history, half_len, packed)),
        out_shape=(
            jax.ShapeDtypeStruct((1, width), f32),
            jax.ShapeDtypeStruct((rows, width), bf16),
            jax.ShapeDtypeStruct((rows, HD), f32),
            jax.ShapeDtypeStruct((rows, HD), f32),
            jax.ShapeDtypeStruct((rows, HD), f32),
            jax.ShapeDtypeStruct((HD // 2, lanes), f32),
            jax.ShapeDtypeStruct((HD // 2, lanes), f32),
            jax.ShapeDtypeStruct((old + rows - half_len // 2, lanes), f32),
        ),
        in_specs=[hbm] * 4 + [vmem] * (tp - 1),
        out_specs=(vmem,) * 8,
        scratch_shapes=[
            pltpu.SMEM(lengths.shape, jnp.int32),
            pltpu.SMEM(parents.shape, jnp.int32),
            pltpu.VMEM(hidden_in.shape, bf16),
            pltpu.VMEM((tp, rows, part), f32),
            pltpu.SemaphoreType.DMA((4,)),
        ],
        compiler_params=params,
        cost_estimate=pl.CostEstimate(
            flops=2000 * 10**6, bytes_accessed=2**20, transcendentals=0
        ),
        name="prepare",
    )(*(in_hbm(x) for x in (lengths, parents, norm_gain[None, :], hidden_in)), *near_pieces)

    new_keys, values = pl.pallas_call(
        fresh_kernel,
        out_shape=(
            jax.ShapeDtypeStruct((rows, kv * HD), bf16),
            jax.ShapeDtypeStruct((kv * HD, old + HD), bf16),
        ),
        in_specs=[vmem] * 8,
        out_specs=(vmem,) * 2,
        compiler_params=params,
        name="fresh",
    )(
        xn,
        scale,
        key_cosine,
        key_sine,
        *(in_vmem(x) for x in (w_key, w_value, prompt_values, gen_values)),
    )

    kept, kept_lse, sent = pl.pallas_call(
        functools.partial(attend_kernel, (steps, own, tp, kv, group, packed)),
        out_shape=(
            jax.ShapeDtypeStruct((HD, heads * rows), f32),
            jax.ShapeDtypeStruct((8, heads * rows), f32),
            jax.ShapeDtypeStruct((HD + rows, heads * rows), bf16),
        ),
        in_specs=[vmem] * (11 + tp),
        out_specs=(vmem,) * 3,
        scratch_shapes=[
            pltpu.VMEM((tp, rows, part), f32),
            pltpu.VMEM((2 * rows, width), bf16),
        ],
        compiler_params=params,
        name="attend",
    )(gain, xn, scale, new_keys, values, cosine, sine, bias, in_vmem(w_query), in_vmem(prompt_keys), in_vmem(gen_keys), *far_pieces[::-1])

    got = permute_by(sent, "req", 1)
    kept_lse, w_out_far = pl.pallas_call(
        fetch_kernel,
        out_shape=(
            jax.ShapeDtypeStruct((8, heads * rows), f32),
            jax.ShapeDtypeStruct((tp, heads * HD, part), bf16),
        ),
        in_specs=[vmem, hbm],
        out_specs=(vmem, vmem),
        scratch_shapes=[pltpu.SemaphoreType.DMA((2 * tp - 2,))],
        compiler_params=params,
        name="fetch",
    )(kept_lse, in_hbm(w_out))

    chunk = math.gcd(part, 512)
    ctx, *sums = pl.pallas_call(
        functools.partial(project_kernel, (steps, own, tp, heads, chunk)),
        out_shape=(
            jax.ShapeDtypeStruct((rows, heads * HD), bf16),
            *[jax.ShapeDtypeStruct((steps, own, part), bf16)] * (tp - 1),
        ),
        in_specs=[vmem] * 4,
        out_specs=(vmem,) * tp,
        compiler_params=params,
        name="project",
    )(kept, kept_lse, got, w_out_far)
    sums = [across(x, 0, t + 1) for t, x in enumerate(sums)]
    total = pl.pallas_call(
        functools.partial(project_own_kernel, (steps, own, chunk)),
        out_shape=jax.ShapeDtypeStruct((steps, own, part), f32),
        in_specs=[vmem] * 2,
        out_specs=vmem,
        compiler_params=params,
        name="project_own",
    )(ctx, in_vmem(w_out))
    for x in sums:
        total = total + x.astype(f32)
    return total.astype(bf16)


def solution(mesh):
    in_specs = (
        P(None, "req", "tp"),
        P(),
        P(None, "tp"),
        P(None, "tp"),
        P(None, "tp"),
        P("tp", None),
        P("req", None, "tp"),
        P("req", None, "tp"),
        P("req", None, "tp"),
        P("req", None, "tp"),
        P(),
        P(),
    )
    out_specs = P(None, "req", "tp")
    return jax.shard_map(body, mesh=mesh, in_specs=in_specs, out_specs=out_specs, check_vma=False)
```

```python
import functools
import math

import jax
import jax.numpy as jnp
from jax import lax
from jax.experimental import pallas as pl
from jax.experimental.pallas import tpu as pltpu
from jax.sharding import PartitionSpec as P

HD = 128
BEAMS = 8

norm_eps = 1e-05
masked_score = -1e30
rope_base = 500000.0


def quotient(x, size):
    return x >> (size.bit_length() - 1) if size & (size - 1) == 0 else x // size


def remainder(x, size):
    return x & (size - 1) if size & (size - 1) == 0 else x % size


def permute_by(value, axis, distance):
    pairs = [(source, source ^ distance) for source in range(lax.axis_size(axis))]
    return lax.ppermute(value, axis, pairs)


def across(value, beam_distance, tp_distance):
    req, tp = lax.axis_size("req"), lax.axis_size("tp")
    pairs = [
        (r * tp + t, (r ^ beam_distance) * tp + (t ^ tp_distance))
        for r in range(req)
        for t in range(tp)
    ]
    return lax.ppermute(value, ("req", "tp"), pairs)


def lay_out(pieces, gain, x_s, xn_ref, first):
    steps, own, part = pieces[0].shape
    rows = steps * own
    me_tp = lax.axis_index("tp")
    total = jnp.zeros((rows, HD), jnp.float32)
    for t, piece in enumerate(pieces):
        column = pl.multiple_of((me_tp ^ t) * part, HD)
        for s in range(steps):
            x_s[t, pl.ds(s * own, own), :] = piece[s].astype(jnp.float32)
        mine = x_s[t]
        xn_ref[pl.ds(first, rows), pl.ds(column, part)] = (
            mine * gain[:, pl.ds(column, part)]
        ).astype(jnp.bfloat16)
        mine = mine * mine
        for c in range(part // HD):
            total = total + mine[:, c * HD : (c + 1) * HD]
    mean = jnp.sum(total, axis=-1, keepdims=True) / (part * len(pieces))
    return lax.rsqrt(mean + norm_eps)


def rotate(x, cosine, sine):
    return (x * cosine + pltpu.roll(x, HD // 2, 1) * sine).astype(jnp.bfloat16)


def prepare_kernel(sizes, lengths, parents, gain, hidden, *refs):
    steps, own, tp, group, history, half_len, packed = sizes
    pieces = refs[: tp - 1]
    (
        gain_ref,
        xn_ref,
        scale_ref,
        key_cosine_ref,
        key_sine_ref,
        cosine_ref,
        sine_ref,
        bias_ref,
        lengths_s,
        parents_s,
        hidden_s,
        x_s,
        sems,
    ) = refs[tp - 1 :]
    rows = steps * own
    free = half_len // 2
    device = lax.axis_index("req")
    request = device // 2
    parity = device % 2

    copies = [
        pltpu.make_async_copy(source, target, sems.at[n])
        for n, (source, target) in enumerate(
            ((gain, gain_ref), (hidden, hidden_s), (lengths, lengths_s), (parents, parents_s))
        )
    ]
    for copy in copies:
        copy.start()
    for copy in copies:
        copy.wait()

    scale = lay_out((hidden_s, *pieces), gain_ref, x_s, xn_ref, 0)
    scale_ref[...] = jnp.broadcast_to(scale, scale_ref.shape)

    length = lengths_s[request]
    half_dim = HD // 2
    fall = -math.log(rope_base) / half_dim

    def angles(step, place):
        return (length + history + step).astype(jnp.float32) * jnp.exp(
            place.astype(jnp.float32) * fall
        )

    row = lax.broadcasted_iota(jnp.int32, (rows, HD), 0)
    lane = lax.broadcasted_iota(jnp.int32, (rows, HD), 1)
    angle = angles(quotient(row, own), remainder(lane, half_dim))
    key_cosine_ref[...] = jnp.cos(angle) * scale
    key_sine = jnp.sin(angle) * scale
    key_sine_ref[...] = jnp.where(lane < half_dim, -key_sine, key_sine)

    lanes = packed * group * 2 * rows
    place = lax.broadcasted_iota(jnp.int32, (half_dim, lanes), 0)
    lane = lax.broadcasted_iota(jnp.int32, (half_dim, lanes), 1)
    angle = angles(quotient(remainder(lane, rows), own), place)
    cosine_ref[...] = jnp.cos(angle)
    sine_ref[...] = jnp.sin(angle)

    def parent_of(s, beam):
        out = jnp.zeros_like(beam)
        for j in range(BEAMS):
            out = jnp.where(beam == j, parents_s[s, request * BEAMS + j], out)
        return out

    lane = lax.broadcasted_iota(jnp.int32, (8, lanes), 1)
    row_step = quotient(remainder(lane, rows), own)
    row_parity = jnp.where(lane < lanes // 2, parity, 1 - parity)
    beam = row_parity * own + remainder(lane, own)
    ancestors = [None] * steps
    at = beam
    for s in reversed(range(steps)):
        if s < steps - 1:
            at = jnp.where(row_step > s, parent_of(s + 1, at), beam)
        ancestors[s] = jnp.where(row_step >= s, at, -1)
    origin = parent_of(0, at)

    place = lax.broadcasted_iota(jnp.int32, (half_len - free, lanes), 0)
    place = parity * half_len + free + place
    bias_ref[pl.ds(0, half_len - free), :] = jnp.where(place < length, 0.0, masked_score)
    for n in range(own):
        seen = jnp.where(origin == parity * own + n, 0.0, masked_score)
        for c in range(0, history, 8):
            bias_ref[pl.ds(half_len - free + n * history + c, 8), :] = seen
    sublane = lax.broadcasted_iota(jnp.int32, (8, lanes), 0)
    for c in range(0, rows, 8):
        seen = jnp.full((8, lanes), masked_score, jnp.float32)
        for s in range(c // own, min((c + 8) // own, steps)):
            hit = (quotient(c + sublane, own) == s) & (
                ancestors[s] == parity * own + remainder(c + sublane, own)
            )
            seen = jnp.where(hit, 0.0, seen)
        bias_ref[pl.ds(half_len + own * history - free + c, 8), :] = seen


def fresh_kernel(
    xn_ref,
    scale_ref,
    key_cosine_ref,
    key_sine_ref,
    wk_ref,
    wv_ref,
    pv_ref,
    gv_ref,
    new_keys_ref,
    values_ref,
):
    rows = xn_ref.shape[0]
    half_len, width = pv_ref.shape[1:]
    old = values_ref.shape[1] - HD
    xn = xn_ref[...]
    keys = jnp.dot(xn, wk_ref[...], preferred_element_type=jnp.float32)
    values = jnp.dot(xn, wv_ref[...], preferred_element_type=jnp.float32)
    values_ref[:, pl.ds(0, half_len)] = pv_ref[0].T
    values_ref[:, pl.ds(half_len, old - half_len)] = gv_ref[...].reshape(-1, width).T
    for g in range(width // HD):
        cols = pl.ds(g * HD, HD)
        new_keys_ref[:, cols] = rotate(
            keys[:, g * HD : (g + 1) * HD], key_cosine_ref[...], key_sine_ref[...]
        )
    scale = scale_ref[...]
    values = [values[:, g * HD : (g + 1) * HD] * scale for g in range(width // HD)]
    values = jnp.concatenate(
        [jnp.concatenate(values, axis=1), jnp.zeros((HD - rows, width), jnp.float32)], axis=0
    )
    values_ref[:, pl.ds(old, HD)] = values.astype(jnp.bfloat16).T


def attend_kernel(
    sizes,
    gain_ref,
    xn_ref,
    scale_ref,
    new_keys_ref,
    values_ref,
    cosine_ref,
    sine_ref,
    bias_ref,
    wq_ref,
    pk_ref,
    gk_ref,
    *refs,
):
    steps, own, tp, kv, group, packed = sizes
    pieces = refs[:tp][::-1]
    kept_ref, kept_lse_ref, sent_ref, x_s, xn_s = refs[tp:]
    rows = steps * own
    part = pieces[0].shape[-1]
    packs = kv // packed
    each = packed * group
    size = each * HD
    lanes = each * 2 * rows
    keys_space = values_ref.shape[1]
    keys_count = keys_space - HD + rows
    free = keys_count - bias_ref.shape[0]
    lane = lax.broadcasted_iota(jnp.int32, (HD, lanes), 1)
    owner = quotient(remainder(lane, lanes // 2), group * rows)
    pad = jnp.zeros((keys_space - keys_count, lanes), jnp.bfloat16)

    xn_s[pl.ds(0, rows), :] = xn_ref[...]
    scale = lay_out(pieces, gain_ref, x_s, xn_s, rows)
    product = [
        jnp.dot(xn_s[...], wq_ref[:, pl.ds(p * size, size)], preferred_element_type=jnp.float32)
        for p in range(packs)
    ]
    scale = jnp.concatenate([scale_ref[...], jnp.broadcast_to(scale, (rows, HD))], axis=0)
    scale = scale * HD**-0.5
    product = [x[:, h * HD : (h + 1) * HD] * scale for x in product for h in range(each)]

    every = range(packs)
    cosine, sine = cosine_ref[...], sine_ref[...]
    scores = []
    for p in every:
        q = product[p * each : (p + 1) * each]
        q = jnp.concatenate([x[:rows] for x in q] + [x[rows:] for x in q], axis=0).T
        first, second = q[: HD // 2], q[HD // 2 :]
        q = jnp.concatenate(
            [first * cosine - second * sine, second * cosine + first * sine], axis=0
        )
        q = jnp.concatenate([jnp.where(owner == i, q, 0.0) for i in range(packed)], axis=0)
        cols = pl.ds(p * packed * HD, packed * HD)
        keys = jnp.concatenate(
            [
                pk_ref[0, :, cols],
                gk_ref[:, :, cols].reshape(-1, packed * HD),
                new_keys_ref[:, cols],
            ],
            axis=0,
        )
        score = jnp.dot(keys, q.astype(jnp.bfloat16), preferred_element_type=jnp.float32)
        scores.append(jnp.concatenate([score[:free], score[free:] + bias_ref[...]], axis=0))
    tops = [jnp.max(x, axis=0, keepdims=True) for x in scores]
    powers = [jnp.exp(x - top) for x, top in zip(scores, tops)]
    totals = [jnp.sum(x, axis=0, keepdims=True) for x in powers]
    mixed = [
        jnp.dot(
            values_ref[pl.ds(p * packed * HD, packed * HD), :],
            jnp.concatenate([powers[p].astype(jnp.bfloat16), pad], axis=0),
            preferred_element_type=jnp.float32,
        )
        for p in every
    ]
    results, logs = [], []
    for p in every:
        out = mixed[p][:HD]
        for i in range(1, packed):
            out = jnp.where(owner == i, mixed[p][i * HD : (i + 1) * HD], out)
        results.append(out * (1.0 / totals[p]))
        logs.append(jnp.broadcast_to(tops[p] + jnp.log(totals[p]), (8, lanes)))

    def sort(parts):
        half = lanes // 2
        if packs == 1:
            return parts[0][:, :half], parts[0][:, half:]
        low = lax.broadcasted_iota(jnp.int32, parts[0].shape, 1) < half
        first, second = parts
        return (
            jnp.where(low, first, pltpu.roll(second, half, 1)),
            jnp.where(low, pltpu.roll(first, half, 1), second),
        )

    kept_ref[...], sent = sort(results)
    kept_lse_ref[...], rest = sort(logs)
    sent_ref[pl.ds(0, HD), :] = sent.astype(jnp.bfloat16)
    rest = jnp.concatenate([rest] * (rows // 8), axis=0)
    sublane = lax.broadcasted_iota(jnp.int32, rest.shape, 0)
    terms = jnp.zeros(rest.shape, jnp.float32)
    for n in range(3):
        term = rest.astype(jnp.bfloat16).astype(jnp.float32)
        terms = jnp.where(sublane == n, term, terms)
        rest = rest - term
    sent_ref[pl.ds(HD, rows), :] = terms.astype(jnp.bfloat16)


def fetch_kernel(kept_lse_ref, w_out, kept_lse_out, w_out_ref, sems):
    tp, depth, part = w_out_ref.shape
    me_tp = lax.axis_index("tp")
    copies = []
    for d in range(1, tp):
        cols = pl.ds(pl.multiple_of((me_tp ^ d) * part, HD), part)
        for n in range(2):
            rows = pl.ds(n * (depth // 2), depth // 2)
            copies.append(
                pltpu.make_async_copy(
                    w_out.at[rows, cols], w_out_ref.at[d - 1, rows], sems.at[2 * d - 2 + n]
                )
            )
    for copy in copies:
        copy.start()
    kept_lse_out[...] = kept_lse_ref[...]
    for copy in copies:
        copy.wait()


def multiply_out(sizes, ctx, w_out_ref, first, out_ref):
    steps, own, chunk = sizes
    for lower in range(0, out_ref.shape[-1], chunk):
        place = pl.ds(pl.multiple_of(first + lower, HD), chunk)
        out = jnp.dot(ctx, w_out_ref[:, place], preferred_element_type=jnp.float32)
        for s in range(steps):
            out_ref[s, :, pl.ds(lower, chunk)] = out[s * own : (s + 1) * own].astype(out_ref.dtype)


def project_kernel(sizes, kept_ref, kept_lse_ref, got_ref, w_out_ref, ctx_ref, *outs):
    steps, own, tp, heads, chunk = sizes
    rows = steps * own
    terms = got_ref[pl.ds(HD, rows), :].astype(jnp.float32)
    lse_got = terms[0:1] + terms[1:2] + terms[2:3]
    lse_mine = kept_lse_ref[pl.ds(0, 1), :]
    top = jnp.maximum(lse_mine, lse_got)
    mine = jnp.exp(lse_mine - top)
    got = jnp.exp(lse_got - top)
    share = mine / (mine + got)
    ctx = kept_ref[...] * share + got_ref[pl.ds(0, HD), :].astype(jnp.float32) * (1.0 - share)
    ctx = ctx.T.astype(jnp.bfloat16)
    ctx = jnp.concatenate([ctx[h * rows : (h + 1) * rows] for h in range(heads)], axis=1)
    ctx_ref[...] = ctx
    for d in range(1, tp):
        multiply_out((steps, own, chunk), ctx, w_out_ref.at[d - 1], 0, outs[d - 1])


def project_own_kernel(sizes, ctx_ref, w_out_ref, out_ref):
    first = lax.axis_index("tp") * out_ref.shape[-1]
    multiply_out(sizes, ctx_ref[...], w_out_ref, first, out_ref)


def body(
    hidden_in,
    norm_gain,
    w_query,
    w_key,
    w_value,
    w_out,
    prompt_keys,
    prompt_values,
    gen_keys,
    gen_values,
    lengths,
    parents,
):
    steps, own, part = hidden_in.shape
    tp = lax.axis_size("tp")
    rows = steps * own
    width = w_query.shape[0]
    kv = w_key.shape[1] // HD
    group = w_query.shape[1] // w_key.shape[1]
    heads = kv * group
    history = gen_keys.shape[1]

    near_pieces = [across(hidden_in, 0, t) for t in range(1, tp)]
    far = across(hidden_in, 1, 0)

    def in_hbm(x):
        return pltpu.with_memory_space_constraint(x, pltpu.HBM)

    def in_vmem(x):
        return pltpu.with_memory_space_constraint(x, pltpu.VMEM)

    vmem = pl.BlockSpec(memory_space=pltpu.VMEM)
    hbm = pl.BlockSpec(memory_space=pltpu.HBM)
    params = pltpu.CompilerParams(vmem_limit_bytes=16 * 2**20)
    f32, bf16 = jnp.float32, jnp.bfloat16
    half_len = prompt_keys.shape[1]
    old = half_len + own * history
    packed = 2 - kv % 2
    lanes = packed * group * 2 * rows
    gain, xn, scale, key_cosine, key_sine, cosine, sine, bias = pl.pallas_call(
        functools.partial(prepare_kernel, (steps, own, tp, group, history, half_len, packed)),
        out_shape=(
            jax.ShapeDtypeStruct((1, width), f32),
            jax.ShapeDtypeStruct((rows, width), bf16),
            jax.ShapeDtypeStruct((rows, HD), f32),
            jax.ShapeDtypeStruct((rows, HD), f32),
            jax.ShapeDtypeStruct((rows, HD), f32),
            jax.ShapeDtypeStruct((HD // 2, lanes), f32),
            jax.ShapeDtypeStruct((HD // 2, lanes), f32),
            jax.ShapeDtypeStruct((old + rows - half_len // 2, lanes), f32),
        ),
        in_specs=[hbm] * 4 + [vmem] * (tp - 1),
        out_specs=(vmem,) * 8,
        scratch_shapes=[
            pltpu.SMEM(lengths.shape, jnp.int32),
            pltpu.SMEM(parents.shape, jnp.int32),
            pltpu.VMEM(hidden_in.shape, bf16),
            pltpu.VMEM((tp, rows, part), f32),
            pltpu.SemaphoreType.DMA((4,)),
        ],
        compiler_params=params,
        cost_estimate=pl.CostEstimate(
            flops=2000 * 10**6, bytes_accessed=2**20, transcendentals=0
        ),
        name="prepare",
    )(*(in_hbm(x) for x in (lengths, parents, norm_gain[None, :], hidden_in)), *near_pieces)

    far, xn = lax.optimization_barrier((far, xn))
    far_pieces = [far] + [across(far, 0, t) for t in range(1, tp)]
    new_keys, values = pl.pallas_call(
        fresh_kernel,
        out_shape=(
            jax.ShapeDtypeStruct((rows, kv * HD), bf16),
            jax.ShapeDtypeStruct((kv * HD, old + HD), bf16),
        ),
        in_specs=[vmem] * 8,
        out_specs=(vmem,) * 2,
        compiler_params=params,
        name="fresh",
    )(
        xn,
        scale,
        key_cosine,
        key_sine,
        *(in_vmem(x) for x in (w_key, w_value, prompt_values, gen_values)),
    )

    kept, kept_lse, sent = pl.pallas_call(
        functools.partial(attend_kernel, (steps, own, tp, kv, group, packed)),
        out_shape=(
            jax.ShapeDtypeStruct((HD, heads * rows), f32),
            jax.ShapeDtypeStruct((8, heads * rows), f32),
            jax.ShapeDtypeStruct((HD + rows, heads * rows), bf16),
        ),
        in_specs=[vmem] * (11 + tp),
        out_specs=(vmem,) * 3,
        scratch_shapes=[
            pltpu.VMEM((tp, rows, part), f32),
            pltpu.VMEM((2 * rows, width), bf16),
        ],
        compiler_params=params,
        name="attend",
    )(gain, xn, scale, new_keys, values, cosine, sine, bias, in_vmem(w_query), in_vmem(prompt_keys), in_vmem(gen_keys), *far_pieces[::-1])

    got = permute_by(sent, "req", 1)
    kept_lse, w_out_far = pl.pallas_call(
        fetch_kernel,
        out_shape=(
            jax.ShapeDtypeStruct((8, heads * rows), f32),
            jax.ShapeDtypeStruct((tp, heads * HD, part), bf16),
        ),
        in_specs=[vmem, hbm],
        out_specs=(vmem, vmem),
        scratch_shapes=[pltpu.SemaphoreType.DMA((2 * tp - 2,))],
        compiler_params=params,
        name="fetch",
    )(kept_lse, in_hbm(w_out))

    chunk = math.gcd(part, 512)
    ctx, *sums = pl.pallas_call(
        functools.partial(project_kernel, (steps, own, tp, heads, chunk)),
        out_shape=(
            jax.ShapeDtypeStruct((rows, heads * HD), bf16),
            *[jax.ShapeDtypeStruct((steps, own, part), bf16)] * (tp - 1),
        ),
        in_specs=[vmem] * 4,
        out_specs=(vmem,) * tp,
        compiler_params=params,
        name="project",
    )(kept, kept_lse, got, w_out_far)
    sums = [across(x, 0, t + 1) for t, x in enumerate(sums)]
    total = pl.pallas_call(
        functools.partial(project_own_kernel, (steps, own, chunk)),
        out_shape=jax.ShapeDtypeStruct((steps, own, part), f32),
        in_specs=[vmem] * 2,
        out_specs=vmem,
        compiler_params=params,
        name="project_own",
    )(ctx, in_vmem(w_out))
    for x in sums:
        total = total + x.astype(f32)
    return total.astype(bf16)


def solution(mesh):
    in_specs = (
        P(None, "req", "tp"),
        P(),
        P(None, "tp"),
        P(None, "tp"),
        P(None, "tp"),
        P("tp", None),
        P("req", None, "tp"),
        P("req", None, "tp"),
        P("req", None, "tp"),
        P("req", None, "tp"),
        P(),
        P(),
    )
    out_specs = P(None, "req", "tp")
    return jax.shard_map(body, mesh=mesh, in_specs=in_specs, out_specs=out_specs, check_vma=False)
```

```python
import functools
import math

import jax
import jax.numpy as jnp
from jax import lax
from jax.experimental import pallas as pl
from jax.experimental.pallas import tpu as pltpu
from jax.sharding import PartitionSpec as P

HD = 128
BEAMS = 8

norm_eps = 1e-05
masked_score = -1e30
rope_base = 500000.0


def quotient(x, size):
    return x >> (size.bit_length() - 1) if size & (size - 1) == 0 else x // size


def remainder(x, size):
    return x & (size - 1) if size & (size - 1) == 0 else x % size


def permute_by(value, axis, distance):
    pairs = [(source, source ^ distance) for source in range(lax.axis_size(axis))]
    return lax.ppermute(value, axis, pairs)


def across(value, beam_distance, tp_distance):
    req, tp = lax.axis_size("req"), lax.axis_size("tp")
    pairs = [
        (r * tp + t, (r ^ beam_distance) * tp + (t ^ tp_distance))
        for r in range(req)
        for t in range(tp)
    ]
    return lax.ppermute(value, ("req", "tp"), pairs)


def lay_out(piece, place, gain, x_s, xn_ref, first):
    steps, own, part = piece.shape
    rows = steps * own
    for s in range(steps):
        x_s[pl.ds(s * own, own), :] = piece[s].astype(jnp.float32)
    mine = x_s[...]
    xn_ref[pl.ds(first, rows), place] = (mine * gain).astype(jnp.bfloat16)
    mine = mine * mine
    return sum(mine[:, c * HD : (c + 1) * HD] for c in range(part // HD))


def norm_scale(squares, width):
    return lax.rsqrt(jnp.sum(squares, axis=-1, keepdims=True) / width + norm_eps)


def block_of(distance, part):
    return pl.ds(pl.multiple_of((lax.axis_index("tp") ^ distance) * part, HD), part)


def rotate(x, cosine, sine):
    return (x * cosine + pltpu.roll(x, HD // 2, 1) * sine).astype(jnp.bfloat16)


def prepare_kernel(sizes, lengths, parents, gain, hidden, *refs):
    steps, own, tp, group, history, half_len, packed = sizes
    pieces = refs[: tp - 1]
    (
        gain_ref,
        xn_ref,
        scale_ref,
        key_cosine_ref,
        key_sine_ref,
        cosine_ref,
        sine_ref,
        bias_ref,
        lengths_s,
        parents_s,
        hidden_s,
        x_s,
        sems,
    ) = refs[tp - 1 :]
    rows = steps * own
    free = half_len // 2
    device = lax.axis_index("req")
    request = device // 2
    parity = device % 2

    copies = [
        pltpu.make_async_copy(source, target, sems.at[n])
        for n, (source, target) in enumerate(
            ((gain, gain_ref), (hidden, hidden_s), (lengths, lengths_s), (parents, parents_s))
        )
    ]
    for copy in copies:
        copy.start()
    for copy in copies:
        copy.wait()

    squares = []
    for t, piece in enumerate((hidden_s, *pieces)):
        place = block_of(t, piece.shape[-1])
        squares.append(lay_out(piece, place, gain_ref[:, place], x_s.at[t], xn_ref, 0))
    scale = norm_scale(sum(squares), xn_ref.shape[1])
    scale_ref[...] = jnp.broadcast_to(scale, scale_ref.shape)

    length = lengths_s[request]
    half_dim = HD // 2
    fall = -math.log(rope_base) / half_dim

    def angles(step, place):
        return (length + history + step).astype(jnp.float32) * jnp.exp(
            place.astype(jnp.float32) * fall
        )

    row = lax.broadcasted_iota(jnp.int32, (rows, HD), 0)
    lane = lax.broadcasted_iota(jnp.int32, (rows, HD), 1)
    angle = angles(quotient(row, own), remainder(lane, half_dim))
    key_cosine_ref[...] = jnp.cos(angle) * scale
    key_sine = jnp.sin(angle) * scale
    key_sine_ref[...] = jnp.where(lane < half_dim, -key_sine, key_sine)

    lanes = packed * group * 2 * rows
    place = lax.broadcasted_iota(jnp.int32, (half_dim, lanes), 0)
    lane = lax.broadcasted_iota(jnp.int32, (half_dim, lanes), 1)
    angle = angles(quotient(remainder(lane, rows), own), place)
    cosine_ref[...] = jnp.cos(angle)
    sine_ref[...] = jnp.sin(angle)

    def parent_of(s, beam):
        out = jnp.zeros_like(beam)
        for j in range(BEAMS):
            out = jnp.where(beam == j, parents_s[s, request * BEAMS + j], out)
        return out

    lane = lax.broadcasted_iota(jnp.int32, (8, lanes), 1)
    row_step = quotient(remainder(lane, rows), own)
    row_parity = jnp.where(lane < lanes // 2, parity, 1 - parity)
    beam = row_parity * own + remainder(lane, own)
    ancestors = [None] * steps
    at = beam
    for s in reversed(range(steps)):
        if s < steps - 1:
            at = jnp.where(row_step > s, parent_of(s + 1, at), beam)
        ancestors[s] = jnp.where(row_step >= s, at, -1)
    origin = parent_of(0, at)

    place = lax.broadcasted_iota(jnp.int32, (half_len - free, lanes), 0)
    place = parity * half_len + free + place
    bias_ref[pl.ds(0, half_len - free), :] = jnp.where(place < length, 0.0, masked_score)
    for n in range(own):
        seen = jnp.where(origin == parity * own + n, 0.0, masked_score)
        for c in range(0, history, 8):
            bias_ref[pl.ds(half_len - free + n * history + c, 8), :] = seen
    sublane = lax.broadcasted_iota(jnp.int32, (8, lanes), 0)
    for c in range(0, rows, 8):
        seen = jnp.full((8, lanes), masked_score, jnp.float32)
        for s in range(c // own, min((c + 8) // own, steps)):
            hit = (quotient(c + sublane, own) == s) & (
                ancestors[s] == parity * own + remainder(c + sublane, own)
            )
            seen = jnp.where(hit, 0.0, seen)
        bias_ref[pl.ds(half_len + own * history - free + c, 8), :] = seen


def fresh_kernel(
    xn_ref,
    scale_ref,
    key_cosine_ref,
    key_sine_ref,
    wk_ref,
    wv_ref,
    pv_ref,
    gv_ref,
    new_keys_ref,
    values_ref,
):
    rows = xn_ref.shape[0]
    half_len, width = pv_ref.shape[1:]
    old = values_ref.shape[1] - HD
    xn = xn_ref[...]
    keys = jnp.dot(xn, wk_ref[...], preferred_element_type=jnp.float32)
    values = jnp.dot(xn, wv_ref[...], preferred_element_type=jnp.float32)
    values_ref[:, pl.ds(0, half_len)] = pv_ref[0].T
    values_ref[:, pl.ds(half_len, old - half_len)] = gv_ref[...].reshape(-1, width).T
    for g in range(width // HD):
        cols = pl.ds(g * HD, HD)
        new_keys_ref[:, cols] = rotate(
            keys[:, g * HD : (g + 1) * HD], key_cosine_ref[...], key_sine_ref[...]
        )
    scale = scale_ref[...]
    values = [values[:, g * HD : (g + 1) * HD] * scale for g in range(width // HD)]
    values = jnp.concatenate(
        [jnp.concatenate(values, axis=1), jnp.zeros((HD - rows, width), jnp.float32)], axis=0
    )
    values_ref[:, pl.ds(old, HD)] = values.astype(jnp.bfloat16).T


def query_kernel(gain_ref, xn_ref, wq_ref, piece, product_ref, squares_ref, x_s, xn_s):
    rows = xn_ref.shape[0]
    place = block_of(0, piece.shape[-1])
    xn_s[pl.ds(0, rows), :] = xn_ref[:, place]
    squares_ref[...] = lay_out(piece, slice(None), gain_ref[:, place], x_s, xn_s, rows)
    product_ref[...] = jnp.dot(xn_s[...], wq_ref[place, :], preferred_element_type=jnp.float32)


def attend_kernel(
    sizes,
    gain_ref,
    xn_ref,
    scale_ref,
    new_keys_ref,
    values_ref,
    cosine_ref,
    sine_ref,
    bias_ref,
    wq_ref,
    pk_ref,
    gk_ref,
    product_ref,
    squares_ref,
    *refs,
):
    steps, own, tp, kv, group, packed = sizes
    pieces = refs[: tp - 1]
    kept_ref, kept_lse_ref, sent_ref, x_s, xn_s = refs[tp - 1 :]
    rows = steps * own
    part = pieces[0].shape[-1]
    packs = kv // packed
    each = packed * group
    size = each * HD
    lanes = each * 2 * rows
    keys_space = values_ref.shape[1]
    keys_count = keys_space - HD + rows
    free = keys_count - bias_ref.shape[0]
    lane = lax.broadcasted_iota(jnp.int32, (HD, lanes), 1)
    owner = quotient(remainder(lane, lanes // 2), group * rows)
    pad = jnp.zeros((keys_space - keys_count, lanes), jnp.bfloat16)

    squares = squares_ref[...]
    product = product_ref[...]
    for n, piece in enumerate(pieces):
        place = block_of(n + 1, part)
        xn_s[n, pl.ds(0, rows), :] = xn_ref[:, place]
        squares += lay_out(piece, slice(None), gain_ref[:, place], x_s.at[n], xn_s.at[n], rows)
        product += jnp.dot(xn_s[n], wq_ref[place, :], preferred_element_type=jnp.float32)
    scale = norm_scale(squares, xn_ref.shape[1])
    scale = jnp.concatenate([scale_ref[...], jnp.broadcast_to(scale, (rows, HD))], axis=0)
    scale = scale * HD**-0.5
    product = [product[:, h * HD : (h + 1) * HD] * scale for h in range(kv * group)]

    every = range(packs)
    cosine, sine = cosine_ref[...], sine_ref[...]
    scores = []
    for p in every:
        q = product[p * each : (p + 1) * each]
        q = jnp.concatenate([x[:rows] for x in q] + [x[rows:] for x in q], axis=0).T
        first, second = q[: HD // 2], q[HD // 2 :]
        q = jnp.concatenate(
            [first * cosine - second * sine, second * cosine + first * sine], axis=0
        )
        q = jnp.concatenate([jnp.where(owner == i, q, 0.0) for i in range(packed)], axis=0)
        cols = pl.ds(p * packed * HD, packed * HD)
        keys = jnp.concatenate(
            [
                pk_ref[0, :, cols],
                gk_ref[:, :, cols].reshape(-1, packed * HD),
                new_keys_ref[:, cols],
            ],
            axis=0,
        )
        score = jnp.dot(keys, q.astype(jnp.bfloat16), preferred_element_type=jnp.float32)
        scores.append(jnp.concatenate([score[:free], score[free:] + bias_ref[...]], axis=0))
    tops = [jnp.max(x, axis=0, keepdims=True) for x in scores]
    powers = [jnp.exp(x - top) for x, top in zip(scores, tops)]
    totals = [jnp.sum(x, axis=0, keepdims=True) for x in powers]
    mixed = [
        jnp.dot(
            values_ref[pl.ds(p * packed * HD, packed * HD), :],
            jnp.concatenate([powers[p].astype(jnp.bfloat16), pad], axis=0),
            preferred_element_type=jnp.float32,
        )
        for p in every
    ]
    results, logs = [], []
    for p in every:
        out = mixed[p][:HD]
        for i in range(1, packed):
            out = jnp.where(owner == i, mixed[p][i * HD : (i + 1) * HD], out)
        results.append(out * (1.0 / totals[p]))
        logs.append(jnp.broadcast_to(tops[p] + jnp.log(totals[p]), (8, lanes)))

    def sort(parts):
        half = lanes // 2
        if packs == 1:
            return parts[0][:, :half], parts[0][:, half:]
        low = lax.broadcasted_iota(jnp.int32, parts[0].shape, 1) < half
        first, second = parts
        return (
            jnp.where(low, first, pltpu.roll(second, half, 1)),
            jnp.where(low, pltpu.roll(first, half, 1), second),
        )

    kept_ref[...], sent = sort(results)
    kept_lse_ref[...], rest = sort(logs)
    sent_ref[pl.ds(0, HD), :] = sent.astype(jnp.bfloat16)
    rest = jnp.concatenate([rest] * (rows // 8), axis=0)
    sublane = lax.broadcasted_iota(jnp.int32, rest.shape, 0)
    terms = jnp.zeros(rest.shape, jnp.float32)
    for n in range(3):
        term = rest.astype(jnp.bfloat16).astype(jnp.float32)
        terms = jnp.where(sublane == n, term, terms)
        rest = rest - term
    sent_ref[pl.ds(HD, rows), :] = terms.astype(jnp.bfloat16)


def fetch_kernel(kept_lse_ref, w_out, kept_lse_out, w_out_ref, sems):
    tp, depth, part = w_out_ref.shape
    me_tp = lax.axis_index("tp")
    copies = []
    for d in range(1, tp):
        cols = pl.ds(pl.multiple_of((me_tp ^ d) * part, HD), part)
        for n in range(2):
            rows = pl.ds(n * (depth // 2), depth // 2)
            copies.append(
                pltpu.make_async_copy(
                    w_out.at[rows, cols], w_out_ref.at[d - 1, rows], sems.at[2 * d - 2 + n]
                )
            )
    for copy in copies:
        copy.start()
    kept_lse_out[...] = kept_lse_ref[...]
    for copy in copies:
        copy.wait()


def multiply_out(sizes, ctx, w_out_ref, first, out_ref):
    steps, own, chunk = sizes
    for lower in range(0, out_ref.shape[-1], chunk):
        place = pl.ds(pl.multiple_of(first + lower, HD), chunk)
        out = jnp.dot(ctx, w_out_ref[:, place], preferred_element_type=jnp.float32)
        for s in range(steps):
            out_ref[s, :, pl.ds(lower, chunk)] = out[s * own : (s + 1) * own].astype(out_ref.dtype)


def project_kernel(sizes, kept_ref, kept_lse_ref, got_ref, w_out_ref, ctx_ref, *outs):
    steps, own, tp, heads, chunk = sizes
    rows = steps * own
    terms = got_ref[pl.ds(HD, rows), :].astype(jnp.float32)
    lse_got = terms[0:1] + terms[1:2] + terms[2:3]
    lse_mine = kept_lse_ref[pl.ds(0, 1), :]
    top = jnp.maximum(lse_mine, lse_got)
    mine = jnp.exp(lse_mine - top)
    got = jnp.exp(lse_got - top)
    share = mine / (mine + got)
    ctx = kept_ref[...] * share + got_ref[pl.ds(0, HD), :].astype(jnp.float32) * (1.0 - share)
    ctx = ctx.T.astype(jnp.bfloat16)
    ctx = jnp.concatenate([ctx[h * rows : (h + 1) * rows] for h in range(heads)], axis=1)
    ctx_ref[...] = ctx
    for d in range(1, tp):
        multiply_out((steps, own, chunk), ctx, w_out_ref.at[d - 1], 0, outs[d - 1])


def project_own_kernel(sizes, ctx_ref, w_out_ref, out_ref):
    first = lax.axis_index("tp") * out_ref.shape[-1]
    multiply_out(sizes, ctx_ref[...], w_out_ref, first, out_ref)


def body(
    hidden_in,
    norm_gain,
    w_query,
    w_key,
    w_value,
    w_out,
    prompt_keys,
    prompt_values,
    gen_keys,
    gen_values,
    lengths,
    parents,
):
    steps, own, part = hidden_in.shape
    tp = lax.axis_size("tp")
    rows = steps * own
    width = w_query.shape[0]
    kv = w_key.shape[1] // HD
    group = w_query.shape[1] // w_key.shape[1]
    heads = kv * group
    history = gen_keys.shape[1]

    near_pieces = [across(hidden_in, 0, t) for t in range(1, tp)]
    later = lax.optimization_barrier((hidden_in, near_pieces[0]))[0]
    far_pieces = [across(hidden_in, 1, 0)] + [across(later, 1, t) for t in range(1, tp)]

    def in_hbm(x):
        return pltpu.with_memory_space_constraint(x, pltpu.HBM)

    def in_vmem(x):
        return pltpu.with_memory_space_constraint(x, pltpu.VMEM)

    vmem = pl.BlockSpec(memory_space=pltpu.VMEM)
    hbm = pl.BlockSpec(memory_space=pltpu.HBM)
    params = pltpu.CompilerParams(vmem_limit_bytes=16 * 2**20)
    f32, bf16 = jnp.float32, jnp.bfloat16
    half_len = prompt_keys.shape[1]
    old = half_len + own * history
    packed = 2 - kv % 2
    lanes = packed * group * 2 * rows
    gain, xn, scale, key_cosine, key_sine, cosine, sine, bias = pl.pallas_call(
        functools.partial(prepare_kernel, (steps, own, tp, group, history, half_len, packed)),
        out_shape=(
            jax.ShapeDtypeStruct((1, width), f32),
            jax.ShapeDtypeStruct((rows, width), bf16),
            jax.ShapeDtypeStruct((rows, HD), f32),
            jax.ShapeDtypeStruct((rows, HD), f32),
            jax.ShapeDtypeStruct((rows, HD), f32),
            jax.ShapeDtypeStruct((HD // 2, lanes), f32),
            jax.ShapeDtypeStruct((HD // 2, lanes), f32),
            jax.ShapeDtypeStruct((old + rows - half_len // 2, lanes), f32),
        ),
        in_specs=[hbm] * 4 + [vmem] * (tp - 1),
        out_specs=(vmem,) * 8,
        scratch_shapes=[
            pltpu.SMEM(lengths.shape, jnp.int32),
            pltpu.SMEM(parents.shape, jnp.int32),
            pltpu.VMEM(hidden_in.shape, bf16),
            pltpu.VMEM((tp, rows, part), f32),
            pltpu.SemaphoreType.DMA((4,)),
        ],
        compiler_params=params,
        cost_estimate=pl.CostEstimate(
            flops=2000 * 10**6, bytes_accessed=2**20, transcendentals=0
        ),
        name="prepare",
    )(*(in_hbm(x) for x in (lengths, parents, norm_gain[None, :], hidden_in)), *near_pieces)

    new_keys, values = pl.pallas_call(
        fresh_kernel,
        out_shape=(
            jax.ShapeDtypeStruct((rows, kv * HD), bf16),
            jax.ShapeDtypeStruct((kv * HD, old + HD), bf16),
        ),
        in_specs=[vmem] * 8,
        out_specs=(vmem,) * 2,
        compiler_params=params,
        name="fresh",
    )(
        xn,
        scale,
        key_cosine,
        key_sine,
        *(in_vmem(x) for x in (w_key, w_value, prompt_values, gen_values)),
    )

    w_query = in_vmem(w_query)
    product, squares = pl.pallas_call(
        query_kernel,
        out_shape=(
            jax.ShapeDtypeStruct((2 * rows, heads * HD), f32),
            jax.ShapeDtypeStruct((rows, HD), f32),
        ),
        in_specs=[vmem] * 4,
        out_specs=(vmem,) * 2,
        scratch_shapes=[pltpu.VMEM((rows, part), f32), pltpu.VMEM((2 * rows, part), bf16)],
        compiler_params=params,
        name="query",
    )(gain, xn, w_query, far_pieces[0])

    kept, kept_lse, sent = pl.pallas_call(
        functools.partial(attend_kernel, (steps, own, tp, kv, group, packed)),
        out_shape=(
            jax.ShapeDtypeStruct((HD, heads * rows), f32),
            jax.ShapeDtypeStruct((8, heads * rows), f32),
            jax.ShapeDtypeStruct((HD + rows, heads * rows), bf16),
        ),
        in_specs=[vmem] * (12 + tp),
        out_specs=(vmem,) * 3,
        scratch_shapes=[
            pltpu.VMEM((tp - 1, rows, part), f32),
            pltpu.VMEM((tp - 1, 2 * rows, part), bf16),
        ],
        compiler_params=params,
        name="attend",
    )(gain, xn, scale, new_keys, values, cosine, sine, bias, w_query, in_vmem(prompt_keys), in_vmem(gen_keys), product, squares, *far_pieces[1:])

    got = permute_by(sent, "req", 1)
    kept_lse, w_out_far = pl.pallas_call(
        fetch_kernel,
        out_shape=(
            jax.ShapeDtypeStruct((8, heads * rows), f32),
            jax.ShapeDtypeStruct((tp, heads * HD, part), bf16),
        ),
        in_specs=[vmem, hbm],
        out_specs=(vmem, vmem),
        scratch_shapes=[pltpu.SemaphoreType.DMA((2 * tp - 2,))],
        compiler_params=params,
        name="fetch",
    )(kept_lse, in_hbm(w_out))

    chunk = math.gcd(part, 512)
    ctx, *sums = pl.pallas_call(
        functools.partial(project_kernel, (steps, own, tp, heads, chunk)),
        out_shape=(
            jax.ShapeDtypeStruct((rows, heads * HD), bf16),
            *[jax.ShapeDtypeStruct((steps, own, part), bf16)] * (tp - 1),
        ),
        in_specs=[vmem] * 4,
        out_specs=(vmem,) * tp,
        compiler_params=params,
        name="project",
    )(kept, kept_lse, got, w_out_far)
    sums = [across(x, 0, t + 1) for t, x in enumerate(sums)]
    total = pl.pallas_call(
        functools.partial(project_own_kernel, (steps, own, chunk)),
        out_shape=jax.ShapeDtypeStruct((steps, own, part), f32),
        in_specs=[vmem] * 2,
        out_specs=vmem,
        compiler_params=params,
        name="project_own",
    )(ctx, in_vmem(w_out))
    for x in sums:
        total = total + x.astype(f32)
    return total.astype(bf16)


def solution(mesh):
    in_specs = (
        P(None, "req", "tp"),
        P(),
        P(None, "tp"),
        P(None, "tp"),
        P(None, "tp"),
        P("tp", None),
        P("req", None, "tp"),
        P("req", None, "tp"),
        P("req", None, "tp"),
        P("req", None, "tp"),
        P(),
        P(),
    )
    out_specs = P(None, "req", "tp")
    return jax.shard_map(body, mesh=mesh, in_specs=in_specs, out_specs=out_specs, check_vma=False)
```

```python
import functools
import math

import jax
import jax.numpy as jnp
from jax import lax
from jax.experimental import pallas as pl
from jax.experimental.pallas import tpu as pltpu
from jax.sharding import PartitionSpec as P

HD = 128
BEAMS = 8

norm_eps = 1e-05
masked_score = -1e30
rope_base = 500000.0


def quotient(x, size):
    return x >> (size.bit_length() - 1) if size & (size - 1) == 0 else x // size


def remainder(x, size):
    return x & (size - 1) if size & (size - 1) == 0 else x % size


def permute_by(value, axis, distance):
    pairs = [(source, source ^ distance) for source in range(lax.axis_size(axis))]
    return lax.ppermute(value, axis, pairs)


def across(value, beam_distance, tp_distance):
    req, tp = lax.axis_size("req"), lax.axis_size("tp")
    pairs = [
        (r * tp + t, (r ^ beam_distance) * tp + (t ^ tp_distance))
        for r in range(req)
        for t in range(tp)
    ]
    return lax.ppermute(value, ("req", "tp"), pairs)


def lay_out(piece, place, gain, x_s, xn_ref, first):
    steps, own, part = piece.shape
    rows = steps * own
    for s in range(steps):
        x_s[pl.ds(s * own, own), :] = piece[s].astype(jnp.float32)
    mine = x_s[...]
    xn_ref[pl.ds(first, rows), place] = (mine * gain).astype(jnp.bfloat16)
    mine = mine * mine
    return sum(mine[:, c * HD : (c + 1) * HD] for c in range(part // HD))


def norm_scale(squares, width):
    return lax.rsqrt(jnp.sum(squares, axis=-1, keepdims=True) / width + norm_eps)


def block_of(distance, part):
    return pl.ds(pl.multiple_of((lax.axis_index("tp") ^ distance) * part, HD), part)


def rotate(x, cosine, sine):
    return (x * cosine + pltpu.roll(x, HD // 2, 1) * sine).astype(jnp.bfloat16)


def prepare_kernel(sizes, lengths, parents, gain, hidden, *refs):
    steps, own, tp, group, history, half_len, packed = sizes
    pieces = refs[: tp - 1]
    (
        gain_ref,
        xn_ref,
        scale_ref,
        key_cosine_ref,
        key_sine_ref,
        cosine_ref,
        sine_ref,
        bias_ref,
        lengths_s,
        parents_s,
        hidden_s,
        x_s,
        sems,
    ) = refs[tp - 1 :]
    rows = steps * own
    free = half_len // 2
    device = lax.axis_index("req")
    request = device // 2
    parity = device % 2

    copies = [
        pltpu.make_async_copy(source, target, sems.at[n])
        for n, (source, target) in enumerate(
            ((gain, gain_ref), (hidden, hidden_s), (lengths, lengths_s), (parents, parents_s))
        )
    ]
    for copy in copies:
        copy.start()
    for copy in copies:
        copy.wait()

    squares = []
    for t, piece in enumerate((hidden_s, *pieces)):
        place = block_of(t, piece.shape[-1])
        squares.append(lay_out(piece, place, gain_ref[:, place], x_s.at[t], xn_ref, 0))
    scale = norm_scale(sum(squares), xn_ref.shape[1])
    scale_ref[...] = jnp.broadcast_to(scale, scale_ref.shape)

    length = lengths_s[request]
    half_dim = HD // 2
    fall = -math.log(rope_base) / half_dim

    def angles(step, place):
        return (length + history + step).astype(jnp.float32) * jnp.exp(
            place.astype(jnp.float32) * fall
        )

    row = lax.broadcasted_iota(jnp.int32, (rows, HD), 0)
    lane = lax.broadcasted_iota(jnp.int32, (rows, HD), 1)
    angle = angles(quotient(row, own), remainder(lane, half_dim))
    key_cosine_ref[...] = jnp.cos(angle) * scale
    key_sine = jnp.sin(angle) * scale
    key_sine_ref[...] = jnp.where(lane < half_dim, -key_sine, key_sine)

    lanes = packed * group * 2 * rows
    place = lax.broadcasted_iota(jnp.int32, (half_dim, lanes), 0)
    lane = lax.broadcasted_iota(jnp.int32, (half_dim, lanes), 1)
    angle = angles(quotient(remainder(lane, rows), own), place)
    cosine_ref[...] = jnp.cos(angle)
    sine_ref[...] = jnp.sin(angle)

    def parent_of(s, beam):
        out = jnp.zeros_like(beam)
        for j in range(BEAMS):
            out = jnp.where(beam == j, parents_s[s, request * BEAMS + j], out)
        return out

    lane = lax.broadcasted_iota(jnp.int32, (8, lanes), 1)
    row_step = quotient(remainder(lane, rows), own)
    row_parity = jnp.where(lane < lanes // 2, parity, 1 - parity)
    beam = row_parity * own + remainder(lane, own)
    ancestors = [None] * steps
    at = beam
    for s in reversed(range(steps)):
        if s < steps - 1:
            at = jnp.where(row_step > s, parent_of(s + 1, at), beam)
        ancestors[s] = jnp.where(row_step >= s, at, -1)
    origin = parent_of(0, at)

    place = lax.broadcasted_iota(jnp.int32, (half_len - free, lanes), 0)
    place = parity * half_len + free + place
    bias_ref[pl.ds(0, half_len - free), :] = jnp.where(place < length, 0.0, masked_score)
    for n in range(own):
        seen = jnp.where(origin == parity * own + n, 0.0, masked_score)
        for c in range(0, history, 8):
            bias_ref[pl.ds(half_len - free + n * history + c, 8), :] = seen
    sublane = lax.broadcasted_iota(jnp.int32, (8, lanes), 0)
    for c in range(0, rows, 8):
        seen = jnp.full((8, lanes), masked_score, jnp.float32)
        for s in range(c // own, min((c + 8) // own, steps)):
            hit = (quotient(c + sublane, own) == s) & (
                ancestors[s] == parity * own + remainder(c + sublane, own)
            )
            seen = jnp.where(hit, 0.0, seen)
        bias_ref[pl.ds(half_len + own * history - free + c, 8), :] = seen


def fresh_kernel(
    xn_ref,
    scale_ref,
    key_cosine_ref,
    key_sine_ref,
    wk_ref,
    wv_ref,
    pv_ref,
    gv_ref,
    new_keys_ref,
    values_ref,
):
    rows = xn_ref.shape[0]
    half_len, width = pv_ref.shape[1:]
    old = values_ref.shape[1] - HD
    xn = xn_ref[...]
    keys = jnp.dot(xn, wk_ref[...], preferred_element_type=jnp.float32)
    values = jnp.dot(xn, wv_ref[...], preferred_element_type=jnp.float32)
    values_ref[:, pl.ds(0, half_len)] = pv_ref[0].T
    values_ref[:, pl.ds(half_len, old - half_len)] = gv_ref[...].reshape(-1, width).T
    for g in range(width // HD):
        cols = pl.ds(g * HD, HD)
        new_keys_ref[:, cols] = rotate(
            keys[:, g * HD : (g + 1) * HD], key_cosine_ref[...], key_sine_ref[...]
        )
    scale = scale_ref[...]
    values = [values[:, g * HD : (g + 1) * HD] * scale for g in range(width // HD)]
    values = jnp.concatenate(
        [jnp.concatenate(values, axis=1), jnp.zeros((HD - rows, width), jnp.float32)], axis=0
    )
    values_ref[:, pl.ds(old, HD)] = values.astype(jnp.bfloat16).T


def query_kernel(gain_ref, xn_ref, wq_ref, piece, product_ref, squares_ref, x_s, xn_s):
    rows = xn_ref.shape[0]
    place = block_of(0, piece.shape[-1])
    xn_s[pl.ds(0, rows), :] = xn_ref[:, place]
    squares_ref[...] = lay_out(piece, slice(None), gain_ref[:, place], x_s, xn_s, rows)
    product_ref[...] = jnp.dot(xn_s[...], wq_ref[place, :], preferred_element_type=jnp.float32)


def attend_kernel(
    sizes,
    gain_ref,
    xn_ref,
    scale_ref,
    new_keys_ref,
    values_ref,
    cosine_ref,
    sine_ref,
    bias_ref,
    wq_ref,
    pk_ref,
    gk_ref,
    product_ref,
    squares_ref,
    *refs,
):
    steps, own, tp, kv, group, packed = sizes
    pieces = refs[: tp - 1]
    kept_ref, kept_lse_ref, sent_ref, x_s, xn_s = refs[tp - 1 :]
    rows = steps * own
    part = pieces[0].shape[-1]
    packs = kv // packed
    each = packed * group
    size = each * HD
    lanes = each * 2 * rows
    keys_space = values_ref.shape[1]
    keys_count = keys_space - HD + rows
    free = keys_count - bias_ref.shape[0]
    lane = lax.broadcasted_iota(jnp.int32, (HD, lanes), 1)
    owner = quotient(remainder(lane, lanes // 2), group * rows)
    pad = jnp.zeros((keys_space - keys_count, lanes), jnp.bfloat16)

    squares = squares_ref[...]
    product = product_ref[...]
    for n, piece in enumerate(pieces):
        place = block_of(n + 1, part)
        xn_s[n, pl.ds(0, rows), :] = xn_ref[:, place]
        squares += lay_out(piece, slice(None), gain_ref[:, place], x_s.at[n], xn_s.at[n], rows)
        product += jnp.dot(xn_s[n], wq_ref[place, :], preferred_element_type=jnp.float32)
    scale = norm_scale(squares, xn_ref.shape[1])
    scale = jnp.concatenate([scale_ref[...], jnp.broadcast_to(scale, (rows, HD))], axis=0)
    scale = scale * HD**-0.5
    product = [product[:, h * HD : (h + 1) * HD] * scale for h in range(kv * group)]

    every = range(packs)
    cosine, sine = cosine_ref[...], sine_ref[...]
    scores = []
    for p in every:
        q = product[p * each : (p + 1) * each]
        q = jnp.concatenate([x[:rows] for x in q] + [x[rows:] for x in q], axis=0).T
        first, second = q[: HD // 2], q[HD // 2 :]
        q = jnp.concatenate(
            [first * cosine - second * sine, second * cosine + first * sine], axis=0
        )
        q = jnp.concatenate([jnp.where(owner == i, q, 0.0) for i in range(packed)], axis=0)
        cols = pl.ds(p * packed * HD, packed * HD)
        keys = jnp.concatenate(
            [
                pk_ref[0, :, cols],
                gk_ref[:, :, cols].reshape(-1, packed * HD),
                new_keys_ref[:, cols],
            ],
            axis=0,
        )
        score = jnp.dot(keys, q.astype(jnp.bfloat16), preferred_element_type=jnp.float32)
        scores.append(jnp.concatenate([score[:free], score[free:] + bias_ref[...]], axis=0))
    tops = [jnp.max(x, axis=0, keepdims=True) for x in scores]
    powers = [jnp.exp(x - top) for x, top in zip(scores, tops)]
    totals = [jnp.sum(x, axis=0, keepdims=True) for x in powers]
    mixed = [
        jnp.dot(
            values_ref[pl.ds(p * packed * HD, packed * HD), :],
            jnp.concatenate([powers[p].astype(jnp.bfloat16), pad], axis=0),
            preferred_element_type=jnp.float32,
        )
        for p in every
    ]
    results, logs = [], []
    for p in every:
        out = mixed[p][:HD]
        for i in range(1, packed):
            out = jnp.where(owner == i, mixed[p][i * HD : (i + 1) * HD], out)
        results.append(out * (1.0 / totals[p]))
        logs.append(jnp.broadcast_to(tops[p] + jnp.log(totals[p]), (8, lanes)))

    def sort(parts):
        half = lanes // 2
        if packs == 1:
            return parts[0][:, :half], parts[0][:, half:]
        low = lax.broadcasted_iota(jnp.int32, parts[0].shape, 1) < half
        first, second = parts
        return (
            jnp.where(low, first, pltpu.roll(second, half, 1)),
            jnp.where(low, pltpu.roll(first, half, 1), second),
        )

    kept_ref[...], sent = sort(results)
    kept_lse_ref[...], rest = sort(logs)
    sent_ref[pl.ds(0, HD), :] = sent.astype(jnp.bfloat16)
    rest = jnp.concatenate([rest] * (rows // 8), axis=0)
    sublane = lax.broadcasted_iota(jnp.int32, rest.shape, 0)
    terms = jnp.zeros(rest.shape, jnp.float32)
    for n in range(3):
        term = rest.astype(jnp.bfloat16).astype(jnp.float32)
        terms = jnp.where(sublane == n, term, terms)
        rest = rest - term
    sent_ref[pl.ds(HD, rows), :] = terms.astype(jnp.bfloat16)


def fetch_kernel(kept_lse_ref, w_out, kept_lse_out, w_out_ref, sems):
    tp, depth, part = w_out_ref.shape
    me_tp = lax.axis_index("tp")
    copies = []
    for d in range(1, tp):
        cols = pl.ds(pl.multiple_of((me_tp ^ d) * part, HD), part)
        for n in range(2):
            rows = pl.ds(n * (depth // 2), depth // 2)
            copies.append(
                pltpu.make_async_copy(
                    w_out.at[rows, cols], w_out_ref.at[d - 1, rows], sems.at[2 * d - 2 + n]
                )
            )
    for copy in copies:
        copy.start()
    kept_lse_out[...] = kept_lse_ref[...]
    for copy in copies:
        copy.wait()


def multiply_out(sizes, ctx, w_out_ref, first, out_ref):
    steps, own, chunk = sizes
    for lower in range(0, out_ref.shape[-1], chunk):
        place = pl.ds(pl.multiple_of(first + lower, HD), chunk)
        out = jnp.dot(ctx, w_out_ref[:, place], preferred_element_type=jnp.float32)
        for s in range(steps):
            out_ref[s, :, pl.ds(lower, chunk)] = out[s * own : (s + 1) * own].astype(out_ref.dtype)


def project_kernel(sizes, kept_ref, kept_lse_ref, got_ref, w_out_ref, ctx_ref, *outs):
    steps, own, tp, heads, chunk = sizes
    rows = steps * own
    terms = got_ref[pl.ds(HD, rows), :].astype(jnp.float32)
    lse_got = terms[0:1] + terms[1:2] + terms[2:3]
    lse_mine = kept_lse_ref[pl.ds(0, 1), :]
    top = jnp.maximum(lse_mine, lse_got)
    mine = jnp.exp(lse_mine - top)
    got = jnp.exp(lse_got - top)
    share = mine / (mine + got)
    ctx = kept_ref[...] * share + got_ref[pl.ds(0, HD), :].astype(jnp.float32) * (1.0 - share)
    ctx = ctx.T.astype(jnp.bfloat16)
    ctx = jnp.concatenate([ctx[h * rows : (h + 1) * rows] for h in range(heads)], axis=1)
    ctx_ref[...] = ctx
    for d in range(1, tp):
        multiply_out((steps, own, chunk), ctx, w_out_ref.at[d - 1], 0, outs[d - 1])


def project_own_kernel(sizes, ctx_ref, w_out_ref, out_ref):
    first = lax.axis_index("tp") * out_ref.shape[-1]
    multiply_out(sizes, ctx_ref[...], w_out_ref, first, out_ref)


def body(
    hidden_in,
    norm_gain,
    w_query,
    w_key,
    w_value,
    w_out,
    prompt_keys,
    prompt_values,
    gen_keys,
    gen_values,
    lengths,
    parents,
):
    steps, own, part = hidden_in.shape
    tp = lax.axis_size("tp")
    rows = steps * own
    width = w_query.shape[0]
    kv = w_key.shape[1] // HD
    group = w_query.shape[1] // w_key.shape[1]
    heads = kv * group
    history = gen_keys.shape[1]

    near_pieces = [across(hidden_in, 0, t) for t in range(1, tp)]
    tiny = jnp.cos(lax.broadcasted_iota(jnp.float32, (8, HD), 1))
    later = lax.optimization_barrier((hidden_in, tiny))[0]
    far_pieces = [across(hidden_in, 1, 0)] + [across(later, 1, t) for t in range(1, tp)]

    def in_hbm(x):
        return pltpu.with_memory_space_constraint(x, pltpu.HBM)

    def in_vmem(x):
        return pltpu.with_memory_space_constraint(x, pltpu.VMEM)

    vmem = pl.BlockSpec(memory_space=pltpu.VMEM)
    hbm = pl.BlockSpec(memory_space=pltpu.HBM)
    params = pltpu.CompilerParams(vmem_limit_bytes=16 * 2**20)
    f32, bf16 = jnp.float32, jnp.bfloat16
    half_len = prompt_keys.shape[1]
    old = half_len + own * history
    packed = 2 - kv % 2
    lanes = packed * group * 2 * rows
    gain, xn, scale, key_cosine, key_sine, cosine, sine, bias = pl.pallas_call(
        functools.partial(prepare_kernel, (steps, own, tp, group, history, half_len, packed)),
        out_shape=(
            jax.ShapeDtypeStruct((1, width), f32),
            jax.ShapeDtypeStruct((rows, width), bf16),
            jax.ShapeDtypeStruct((rows, HD), f32),
            jax.ShapeDtypeStruct((rows, HD), f32),
            jax.ShapeDtypeStruct((rows, HD), f32),
            jax.ShapeDtypeStruct((HD // 2, lanes), f32),
            jax.ShapeDtypeStruct((HD // 2, lanes), f32),
            jax.ShapeDtypeStruct((old + rows - half_len // 2, lanes), f32),
        ),
        in_specs=[hbm] * 4 + [vmem] * (tp - 1),
        out_specs=(vmem,) * 8,
        scratch_shapes=[
            pltpu.SMEM(lengths.shape, jnp.int32),
            pltpu.SMEM(parents.shape, jnp.int32),
            pltpu.VMEM(hidden_in.shape, bf16),
            pltpu.VMEM((tp, rows, part), f32),
            pltpu.SemaphoreType.DMA((4,)),
        ],
        compiler_params=params,
        cost_estimate=pl.CostEstimate(
            flops=2000 * 10**6, bytes_accessed=2**20, transcendentals=0
        ),
        name="prepare",
    )(*(in_hbm(x) for x in (lengths, parents, norm_gain[None, :], hidden_in)), *near_pieces)

    new_keys, values = pl.pallas_call(
        fresh_kernel,
        out_shape=(
            jax.ShapeDtypeStruct((rows, kv * HD), bf16),
            jax.ShapeDtypeStruct((kv * HD, old + HD), bf16),
        ),
        in_specs=[vmem] * 8,
        out_specs=(vmem,) * 2,
        compiler_params=params,
        name="fresh",
    )(
        xn,
        scale,
        key_cosine,
        key_sine,
        *(in_vmem(x) for x in (w_key, w_value, prompt_values, gen_values)),
    )

    w_query = in_vmem(w_query)
    product, squares = pl.pallas_call(
        query_kernel,
        out_shape=(
            jax.ShapeDtypeStruct((2 * rows, heads * HD), f32),
            jax.ShapeDtypeStruct((rows, HD), f32),
        ),
        in_specs=[vmem] * 4,
        out_specs=(vmem,) * 2,
        scratch_shapes=[pltpu.VMEM((rows, part), f32), pltpu.VMEM((2 * rows, part), bf16)],
        compiler_params=params,
        name="query",
    )(gain, xn, w_query, far_pieces[0])

    kept, kept_lse, sent = pl.pallas_call(
        functools.partial(attend_kernel, (steps, own, tp, kv, group, packed)),
        out_shape=(
            jax.ShapeDtypeStruct((HD, heads * rows), f32),
            jax.ShapeDtypeStruct((8, heads * rows), f32),
            jax.ShapeDtypeStruct((HD + rows, heads * rows), bf16),
        ),
        in_specs=[vmem] * (12 + tp),
        out_specs=(vmem,) * 3,
        scratch_shapes=[
            pltpu.VMEM((tp - 1, rows, part), f32),
            pltpu.VMEM((tp - 1, 2 * rows, part), bf16),
        ],
        compiler_params=params,
        name="attend",
    )(gain, xn, scale, new_keys, values, cosine, sine, bias, w_query, in_vmem(prompt_keys), in_vmem(gen_keys), product, squares, *far_pieces[1:])

    got = permute_by(sent, "req", 1)
    kept_lse, w_out_far = pl.pallas_call(
        fetch_kernel,
        out_shape=(
            jax.ShapeDtypeStruct((8, heads * rows), f32),
            jax.ShapeDtypeStruct((tp, heads * HD, part), bf16),
        ),
        in_specs=[vmem, hbm],
        out_specs=(vmem, vmem),
        scratch_shapes=[pltpu.SemaphoreType.DMA((2 * tp - 2,))],
        compiler_params=params,
        name="fetch",
    )(kept_lse, in_hbm(w_out))

    chunk = math.gcd(part, 512)
    ctx, *sums = pl.pallas_call(
        functools.partial(project_kernel, (steps, own, tp, heads, chunk)),
        out_shape=(
            jax.ShapeDtypeStruct((rows, heads * HD), bf16),
            *[jax.ShapeDtypeStruct((steps, own, part), bf16)] * (tp - 1),
        ),
        in_specs=[vmem] * 4,
        out_specs=(vmem,) * tp,
        compiler_params=params,
        name="project",
    )(kept, kept_lse, got, w_out_far)
    sums = [across(x, 0, t + 1) for t, x in enumerate(sums)]
    total = pl.pallas_call(
        functools.partial(project_own_kernel, (steps, own, chunk)),
        out_shape=jax.ShapeDtypeStruct((steps, own, part), f32),
        in_specs=[vmem] * 2,
        out_specs=vmem,
        compiler_params=params,
        name="project_own",
    )(ctx, in_vmem(w_out))
    for x in sums:
        total = total + x.astype(f32)
    return total.astype(bf16)


def solution(mesh):
    in_specs = (
        P(None, "req", "tp"),
        P(),
        P(None, "tp"),
        P(None, "tp"),
        P(None, "tp"),
        P("tp", None),
        P("req", None, "tp"),
        P("req", None, "tp"),
        P("req", None, "tp"),
        P("req", None, "tp"),
        P(),
        P(),
    )
    out_specs = P(None, "req", "tp")
    return jax.shard_map(body, mesh=mesh, in_specs=in_specs, out_specs=out_specs, check_vma=False)
```

```python
import functools
import math

import jax
import jax.numpy as jnp
from jax import lax
from jax.experimental import pallas as pl
from jax.experimental.pallas import tpu as pltpu
from jax.sharding import PartitionSpec as P

HD = 128
BEAMS = 8

norm_eps = 1e-05
masked_score = -1e30
rope_base = 500000.0


def quotient(x, size):
    return x >> (size.bit_length() - 1) if size & (size - 1) == 0 else x // size


def remainder(x, size):
    return x & (size - 1) if size & (size - 1) == 0 else x % size


def permute_by(value, axis, distance):
    pairs = [(source, source ^ distance) for source in range(lax.axis_size(axis))]
    return lax.ppermute(value, axis, pairs)


def across(value, beam_distance, tp_distance):
    req, tp = lax.axis_size("req"), lax.axis_size("tp")
    pairs = [
        (r * tp + t, (r ^ beam_distance) * tp + (t ^ tp_distance))
        for r in range(req)
        for t in range(tp)
    ]
    return lax.ppermute(value, ("req", "tp"), pairs)


def lay_out(piece, place, gain, x_s, xn_ref, first):
    steps, own, part = piece.shape
    rows = steps * own
    for s in range(steps):
        x_s[pl.ds(s * own, own), :] = piece[s].astype(jnp.float32)
    mine = x_s[...]
    xn_ref[pl.ds(first, rows), place] = (mine * gain).astype(jnp.bfloat16)
    mine = mine * mine
    return sum(mine[:, c * HD : (c + 1) * HD] for c in range(part // HD))


def norm_scale(squares, width):
    return lax.rsqrt(jnp.sum(squares, axis=-1, keepdims=True) / width + norm_eps)


def block_of(distance, part):
    return pl.ds(pl.multiple_of((lax.axis_index("tp") ^ distance) * part, HD), part)


def rotate(x, cosine, sine):
    return (x * cosine + pltpu.roll(x, HD // 2, 1) * sine).astype(jnp.bfloat16)


def prepare_kernel(sizes, lengths, parents, gain, hidden, *refs):
    steps, own, tp, group, history, half_len, packed = sizes
    pieces = refs[: tp - 1]
    (
        gain_ref,
        xn_ref,
        scale_ref,
        key_cosine_ref,
        key_sine_ref,
        cosine_ref,
        sine_ref,
        bias_ref,
        lengths_s,
        parents_s,
        hidden_s,
        x_s,
        sems,
    ) = refs[tp - 1 :]
    rows = steps * own
    free = half_len // 2
    device = lax.axis_index("req")
    request = device // 2
    parity = device % 2

    copies = [
        pltpu.make_async_copy(source, target, sems.at[n])
        for n, (source, target) in enumerate(
            ((gain, gain_ref), (hidden, hidden_s), (lengths, lengths_s), (parents, parents_s))
        )
    ]
    for copy in copies:
        copy.start()
    for copy in copies:
        copy.wait()

    squares = []
    for t, piece in enumerate((hidden_s, *pieces)):
        place = block_of(t, piece.shape[-1])
        squares.append(lay_out(piece, place, gain_ref[:, place], x_s.at[t], xn_ref, 0))
    scale = norm_scale(sum(squares), xn_ref.shape[1])
    scale_ref[...] = jnp.broadcast_to(scale, scale_ref.shape)

    length = lengths_s[request]
    half_dim = HD // 2
    fall = -math.log(rope_base) / half_dim

    def angles(step, place):
        return (length + history + step).astype(jnp.float32) * jnp.exp(
            place.astype(jnp.float32) * fall
        )

    row = lax.broadcasted_iota(jnp.int32, (rows, HD), 0)
    lane = lax.broadcasted_iota(jnp.int32, (rows, HD), 1)
    angle = angles(quotient(row, own), remainder(lane, half_dim))
    key_cosine_ref[...] = jnp.cos(angle) * scale
    key_sine = jnp.sin(angle) * scale
    key_sine_ref[...] = jnp.where(lane < half_dim, -key_sine, key_sine)

    lanes = packed * group * 2 * rows
    place = lax.broadcasted_iota(jnp.int32, (half_dim, lanes), 0)
    lane = lax.broadcasted_iota(jnp.int32, (half_dim, lanes), 1)
    angle = angles(quotient(remainder(lane, rows), own), place)
    cosine_ref[...] = jnp.cos(angle)
    sine_ref[...] = jnp.sin(angle)

    def parent_of(s, beam):
        out = jnp.zeros_like(beam)
        for j in range(BEAMS):
            out = jnp.where(beam == j, parents_s[s, request * BEAMS + j], out)
        return out

    lane = lax.broadcasted_iota(jnp.int32, (8, lanes), 1)
    row_step = quotient(remainder(lane, rows), own)
    row_parity = jnp.where(lane < lanes // 2, parity, 1 - parity)
    beam = row_parity * own + remainder(lane, own)
    ancestors = [None] * steps
    at = beam
    for s in reversed(range(steps)):
        if s < steps - 1:
            at = jnp.where(row_step > s, parent_of(s + 1, at), beam)
        ancestors[s] = jnp.where(row_step >= s, at, -1)
    origin = parent_of(0, at)

    place = lax.broadcasted_iota(jnp.int32, (half_len - free, lanes), 0)
    place = parity * half_len + free + place
    bias_ref[pl.ds(0, half_len - free), :] = jnp.where(place < length, 0.0, masked_score)
    for n in range(own):
        seen = jnp.where(origin == parity * own + n, 0.0, masked_score)
        for c in range(0, history, 8):
            bias_ref[pl.ds(half_len - free + n * history + c, 8), :] = seen
    sublane = lax.broadcasted_iota(jnp.int32, (8, lanes), 0)
    for c in range(0, rows, 8):
        seen = jnp.full((8, lanes), masked_score, jnp.float32)
        for s in range(c // own, min((c + 8) // own, steps)):
            hit = (quotient(c + sublane, own) == s) & (
                ancestors[s] == parity * own + remainder(c + sublane, own)
            )
            seen = jnp.where(hit, 0.0, seen)
        bias_ref[pl.ds(half_len + own * history - free + c, 8), :] = seen


def fresh_kernel(
    xn_ref,
    scale_ref,
    key_cosine_ref,
    key_sine_ref,
    wk_ref,
    wv_ref,
    pv_ref,
    gv_ref,
    new_keys_ref,
    values_ref,
):
    rows = xn_ref.shape[0]
    half_len, width = pv_ref.shape[1:]
    old = values_ref.shape[1] - HD
    xn = xn_ref[...]
    keys = jnp.dot(xn, wk_ref[...], preferred_element_type=jnp.float32)
    values = jnp.dot(xn, wv_ref[...], preferred_element_type=jnp.float32)
    values_ref[:, pl.ds(0, half_len)] = pv_ref[0].T
    values_ref[:, pl.ds(half_len, old - half_len)] = gv_ref[...].reshape(-1, width).T
    for g in range(width // HD):
        cols = pl.ds(g * HD, HD)
        new_keys_ref[:, cols] = rotate(
            keys[:, g * HD : (g + 1) * HD], key_cosine_ref[...], key_sine_ref[...]
        )
    scale = scale_ref[...]
    values = [values[:, g * HD : (g + 1) * HD] * scale for g in range(width // HD)]
    values = jnp.concatenate(
        [jnp.concatenate(values, axis=1), jnp.zeros((HD - rows, width), jnp.float32)], axis=0
    )
    values_ref[:, pl.ds(old, HD)] = values.astype(jnp.bfloat16).T


def query_kernel(gain_ref, xn_ref, wq_ref, piece, product_ref, squares_ref, x_s, xn_s):
    rows = xn_ref.shape[0]
    place = block_of(0, piece.shape[-1])
    xn_s[pl.ds(0, rows), :] = xn_ref[:, place]
    squares_ref[...] = lay_out(piece, slice(None), gain_ref[:, place], x_s, xn_s, rows)
    product_ref[...] = jnp.dot(xn_s[...], wq_ref[place, :], preferred_element_type=jnp.float32)


def attend_kernel(
    sizes,
    gain_ref,
    xn_ref,
    scale_ref,
    new_keys_ref,
    values_ref,
    cosine_ref,
    sine_ref,
    bias_ref,
    wq_ref,
    pk_ref,
    gk_ref,
    product_ref,
    squares_ref,
    *refs,
):
    steps, own, tp, kv, group, packed = sizes
    pieces = refs[: tp - 1]
    kept_ref, kept_lse_ref, sent_ref, x_s, xn_s = refs[tp - 1 :]
    rows = steps * own
    part = pieces[0].shape[-1]
    packs = kv // packed
    each = packed * group
    size = each * HD
    lanes = each * 2 * rows
    keys_space = values_ref.shape[1]
    keys_count = keys_space - HD + rows
    free = keys_count - bias_ref.shape[0]
    lane = lax.broadcasted_iota(jnp.int32, (HD, lanes), 1)
    owner = quotient(remainder(lane, lanes // 2), group * rows)
    pad = jnp.zeros((keys_space - keys_count, lanes), jnp.bfloat16)

    squares = squares_ref[...]
    product = product_ref[...]
    for n, piece in enumerate(pieces):
        place = block_of(n + 1, part)
        xn_s[n, pl.ds(0, rows), :] = xn_ref[:, place]
        squares += lay_out(piece, slice(None), gain_ref[:, place], x_s.at[n], xn_s.at[n], rows)
        product += jnp.dot(xn_s[n], wq_ref[place, :], preferred_element_type=jnp.float32)
    scale = norm_scale(squares, xn_ref.shape[1])
    scale = jnp.concatenate([scale_ref[...], jnp.broadcast_to(scale, (rows, HD))], axis=0)
    scale = scale * HD**-0.5
    product = [product[:, h * HD : (h + 1) * HD] * scale for h in range(kv * group)]

    every = range(packs)
    cosine, sine = cosine_ref[...], sine_ref[...]
    scores = []
    for p in every:
        q = product[p * each : (p + 1) * each]
        q = jnp.concatenate([x[:rows] for x in q] + [x[rows:] for x in q], axis=0).T
        first, second = q[: HD // 2], q[HD // 2 :]
        q = jnp.concatenate(
            [first * cosine - second * sine, second * cosine + first * sine], axis=0
        )
        q = jnp.concatenate([jnp.where(owner == i, q, 0.0) for i in range(packed)], axis=0)
        cols = pl.ds(p * packed * HD, packed * HD)
        keys = jnp.concatenate(
            [
                pk_ref[0, :, cols],
                gk_ref[:, :, cols].reshape(-1, packed * HD),
                new_keys_ref[:, cols],
            ],
            axis=0,
        )
        score = jnp.dot(keys, q.astype(jnp.bfloat16), preferred_element_type=jnp.float32)
        scores.append(jnp.concatenate([score[:free], score[free:] + bias_ref[...]], axis=0))
    tops = [jnp.max(x, axis=0, keepdims=True) for x in scores]
    powers = [jnp.exp(x - top) for x, top in zip(scores, tops)]
    totals = [jnp.sum(x, axis=0, keepdims=True) for x in powers]
    mixed = [
        jnp.dot(
            values_ref[pl.ds(p * packed * HD, packed * HD), :],
            jnp.concatenate([powers[p].astype(jnp.bfloat16), pad], axis=0),
            preferred_element_type=jnp.float32,
        )
        for p in every
    ]
    results, logs = [], []
    for p in every:
        out = mixed[p][:HD]
        for i in range(1, packed):
            out = jnp.where(owner == i, mixed[p][i * HD : (i + 1) * HD], out)
        results.append(out * (1.0 / totals[p]))
        logs.append(jnp.broadcast_to(tops[p] + jnp.log(totals[p]), (8, lanes)))

    def sort(parts):
        half = lanes // 2
        if packs == 1:
            return parts[0][:, :half], parts[0][:, half:]
        low = lax.broadcasted_iota(jnp.int32, parts[0].shape, 1) < half
        first, second = parts
        return (
            jnp.where(low, first, pltpu.roll(second, half, 1)),
            jnp.where(low, pltpu.roll(first, half, 1), second),
        )

    kept_ref[...], sent = sort(results)
    kept_lse_ref[...], rest = sort(logs)
    sent_ref[pl.ds(0, HD), :] = sent.astype(jnp.bfloat16)
    rest = jnp.concatenate([rest] * (rows // 8), axis=0)
    sublane = lax.broadcasted_iota(jnp.int32, rest.shape, 0)
    terms = jnp.zeros(rest.shape, jnp.float32)
    for n in range(3):
        term = rest.astype(jnp.bfloat16).astype(jnp.float32)
        terms = jnp.where(sublane == n, term, terms)
        rest = rest - term
    sent_ref[pl.ds(HD, rows), :] = terms.astype(jnp.bfloat16)


def fetch_kernel(kept_lse_ref, w_out, kept_lse_out, w_out_ref, sems):
    tp, depth, part = w_out_ref.shape
    me_tp = lax.axis_index("tp")
    copies = []
    for d in range(1, tp):
        cols = pl.ds(pl.multiple_of((me_tp ^ d) * part, HD), part)
        for n in range(2):
            rows = pl.ds(n * (depth // 2), depth // 2)
            copies.append(
                pltpu.make_async_copy(
                    w_out.at[rows, cols], w_out_ref.at[d - 1, rows], sems.at[2 * d - 2 + n]
                )
            )
    for copy in copies:
        copy.start()
    kept_lse_out[...] = kept_lse_ref[...]
    for copy in copies:
        copy.wait()


def multiply_out(sizes, ctx, w_out_ref, first, out_ref):
    steps, own, chunk = sizes
    for lower in range(0, out_ref.shape[-1], chunk):
        place = pl.ds(pl.multiple_of(first + lower, HD), chunk)
        out = jnp.dot(ctx, w_out_ref[:, place], preferred_element_type=jnp.float32)
        for s in range(steps):
            out_ref[s, :, pl.ds(lower, chunk)] = out[s * own : (s + 1) * own].astype(out_ref.dtype)


def project_kernel(sizes, kept_ref, kept_lse_ref, got_ref, w_out_ref, ctx_ref, *outs):
    steps, own, tp, heads, chunk = sizes
    rows = steps * own
    terms = got_ref[pl.ds(HD, rows), :].astype(jnp.float32)
    lse_got = terms[0:1] + terms[1:2] + terms[2:3]
    lse_mine = kept_lse_ref[pl.ds(0, 1), :]
    top = jnp.maximum(lse_mine, lse_got)
    mine = jnp.exp(lse_mine - top)
    got = jnp.exp(lse_got - top)
    share = mine / (mine + got)
    ctx = kept_ref[...] * share + got_ref[pl.ds(0, HD), :].astype(jnp.float32) * (1.0 - share)
    ctx = ctx.T.astype(jnp.bfloat16)
    ctx = jnp.concatenate([ctx[h * rows : (h + 1) * rows] for h in range(heads)], axis=1)
    ctx_ref[...] = ctx
    for d in range(1, tp):
        multiply_out((steps, own, chunk), ctx, w_out_ref.at[d - 1], 0, outs[d - 1])


def project_own_kernel(sizes, ctx_ref, w_out_ref, out_ref):
    first = lax.axis_index("tp") * out_ref.shape[-1]
    multiply_out(sizes, ctx_ref[...], w_out_ref, first, out_ref)


def body(
    hidden_in,
    norm_gain,
    w_query,
    w_key,
    w_value,
    w_out,
    prompt_keys,
    prompt_values,
    gen_keys,
    gen_values,
    lengths,
    parents,
):
    steps, own, part = hidden_in.shape
    tp = lax.axis_size("tp")
    rows = steps * own
    width = w_query.shape[0]
    kv = w_key.shape[1] // HD
    group = w_query.shape[1] // w_key.shape[1]
    heads = kv * group
    history = gen_keys.shape[1]

    near_pieces = [across(hidden_in, 0, t) for t in range(1, tp)]
    tiny = jnp.cos(lax.broadcasted_iota(jnp.float32, (8, HD), 1))
    later = lax.optimization_barrier((hidden_in, tiny))[0]
    far_pieces = [across(hidden_in, 1, 0)] + [across(later, 1, t) for t in range(1, tp)]

    def in_hbm(x):
        return pltpu.with_memory_space_constraint(x, pltpu.HBM)

    def in_vmem(x):
        return pltpu.with_memory_space_constraint(x, pltpu.VMEM)

    vmem = pl.BlockSpec(memory_space=pltpu.VMEM)
    hbm = pl.BlockSpec(memory_space=pltpu.HBM)
    params = pltpu.CompilerParams(vmem_limit_bytes=16 * 2**20)
    f32, bf16 = jnp.float32, jnp.bfloat16
    half_len = prompt_keys.shape[1]
    old = half_len + own * history
    packed = 2 - kv % 2
    lanes = packed * group * 2 * rows
    gain, xn, scale, key_cosine, key_sine, cosine, sine, bias = pl.pallas_call(
        functools.partial(prepare_kernel, (steps, own, tp, group, history, half_len, packed)),
        out_shape=(
            jax.ShapeDtypeStruct((1, width), f32),
            jax.ShapeDtypeStruct((rows, width), bf16),
            jax.ShapeDtypeStruct((rows, HD), f32),
            jax.ShapeDtypeStruct((rows, HD), f32),
            jax.ShapeDtypeStruct((rows, HD), f32),
            jax.ShapeDtypeStruct((HD // 2, lanes), f32),
            jax.ShapeDtypeStruct((HD // 2, lanes), f32),
            jax.ShapeDtypeStruct((old + rows - half_len // 2, lanes), f32),
        ),
        in_specs=[hbm] * 4 + [vmem] * (tp - 1),
        out_specs=(vmem,) * 8,
        scratch_shapes=[
            pltpu.SMEM(lengths.shape, jnp.int32),
            pltpu.SMEM(parents.shape, jnp.int32),
            pltpu.VMEM(hidden_in.shape, bf16),
            pltpu.VMEM((tp, rows, part), f32),
            pltpu.SemaphoreType.DMA((4,)),
        ],
        compiler_params=params,
        cost_estimate=pl.CostEstimate(
            flops=2000 * 10**6, bytes_accessed=2**20, transcendentals=0
        ),
        name="prepare",
    )(*(in_hbm(x) for x in (lengths, parents, norm_gain[None, :], hidden_in)), *near_pieces)

    new_keys, values = pl.pallas_call(
        fresh_kernel,
        out_shape=(
            jax.ShapeDtypeStruct((rows, kv * HD), bf16),
            jax.ShapeDtypeStruct((kv * HD, old + HD), bf16),
        ),
        in_specs=[vmem] * 8,
        out_specs=(vmem,) * 2,
        compiler_params=params,
        name="fresh",
    )(
        xn,
        scale,
        key_cosine,
        key_sine,
        *(in_vmem(x) for x in (w_key, w_value, prompt_values, gen_values)),
    )

    w_query = in_vmem(w_query)
    product, squares = pl.pallas_call(
        query_kernel,
        out_shape=(
            jax.ShapeDtypeStruct((2 * rows, heads * HD), f32),
            jax.ShapeDtypeStruct((rows, HD), f32),
        ),
        in_specs=[vmem] * 4,
        out_specs=(vmem,) * 2,
        scratch_shapes=[pltpu.VMEM((rows, part), f32), pltpu.VMEM((2 * rows, part), bf16)],
        compiler_params=params,
        name="query",
    )(gain, xn, w_query, far_pieces[0])

    kept, kept_lse, sent = pl.pallas_call(
        functools.partial(attend_kernel, (steps, own, tp, kv, group, packed)),
        out_shape=(
            jax.ShapeDtypeStruct((HD, heads * rows), f32),
            jax.ShapeDtypeStruct((8, heads * rows), f32),
            jax.ShapeDtypeStruct((HD + rows, heads * rows), bf16),
        ),
        in_specs=[vmem] * (12 + tp),
        out_specs=(vmem,) * 3,
        scratch_shapes=[
            pltpu.VMEM((tp - 1, rows, part), f32),
            pltpu.VMEM((tp - 1, 2 * rows, part), bf16),
        ],
        compiler_params=params,
        cost_estimate=pl.CostEstimate(
            flops=6000 * 10**6, bytes_accessed=2**20, transcendentals=2**18
        ),
        name="attend",
    )(gain, xn, scale, new_keys, values, cosine, sine, bias, w_query, in_vmem(prompt_keys), in_vmem(gen_keys), product, squares, *far_pieces[1:])

    got = permute_by(sent, "req", 1)
    kept_lse, w_out_far = pl.pallas_call(
        fetch_kernel,
        out_shape=(
            jax.ShapeDtypeStruct((8, heads * rows), f32),
            jax.ShapeDtypeStruct((tp, heads * HD, part), bf16),
        ),
        in_specs=[vmem, hbm],
        out_specs=(vmem, vmem),
        scratch_shapes=[pltpu.SemaphoreType.DMA((2 * tp - 2,))],
        compiler_params=params,
        name="fetch",
    )(kept_lse, in_hbm(w_out))

    chunk = math.gcd(part, 512)
    ctx, *sums = pl.pallas_call(
        functools.partial(project_kernel, (steps, own, tp, heads, chunk)),
        out_shape=(
            jax.ShapeDtypeStruct((rows, heads * HD), bf16),
            *[jax.ShapeDtypeStruct((steps, own, part), bf16)] * (tp - 1),
        ),
        in_specs=[vmem] * 4,
        out_specs=(vmem,) * tp,
        compiler_params=params,
        name="project",
    )(kept, kept_lse, got, w_out_far)
    sums = [across(x, 0, t + 1) for t, x in enumerate(sums)]
    total = pl.pallas_call(
        functools.partial(project_own_kernel, (steps, own, chunk)),
        out_shape=jax.ShapeDtypeStruct((steps, own, part), f32),
        in_specs=[vmem] * 2,
        out_specs=vmem,
        compiler_params=params,
        name="project_own",
    )(ctx, in_vmem(w_out))
    for x in sums:
        total = total + x.astype(f32)
    return total.astype(bf16)


def solution(mesh):
    in_specs = (
        P(None, "req", "tp"),
        P(),
        P(None, "tp"),
        P(None, "tp"),
        P(None, "tp"),
        P("tp", None),
        P("req", None, "tp"),
        P("req", None, "tp"),
        P("req", None, "tp"),
        P("req", None, "tp"),
        P(),
        P(),
    )
    out_specs = P(None, "req", "tp")
    return jax.shard_map(body, mesh=mesh, in_specs=in_specs, out_specs=out_specs, check_vma=False)
```

```python
import functools
import math

import jax
import jax.numpy as jnp
from jax import lax
from jax.experimental import pallas as pl
from jax.experimental.pallas import tpu as pltpu
from jax.sharding import PartitionSpec as P

HD = 128
BEAMS = 8

norm_eps = 1e-05
masked_score = -1e30
rope_base = 500000.0


def quotient(x, size):
    return x >> (size.bit_length() - 1) if size & (size - 1) == 0 else x // size


def remainder(x, size):
    return x & (size - 1) if size & (size - 1) == 0 else x % size


def permute_by(value, axis, distance):
    pairs = [(source, source ^ distance) for source in range(lax.axis_size(axis))]
    return lax.ppermute(value, axis, pairs)


def across(value, beam_distance, tp_distance):
    req, tp = lax.axis_size("req"), lax.axis_size("tp")
    pairs = [
        (r * tp + t, (r ^ beam_distance) * tp + (t ^ tp_distance))
        for r in range(req)
        for t in range(tp)
    ]
    return lax.ppermute(value, ("req", "tp"), pairs)


def lay_out(piece, place, gain, x_s, xn_ref, first):
    steps, own, part = piece.shape
    rows = steps * own
    for s in range(steps):
        x_s[pl.ds(s * own, own), :] = piece[s].astype(jnp.float32)
    mine = x_s[...]
    xn_ref[pl.ds(first, rows), place] = (mine * gain).astype(jnp.bfloat16)
    mine = mine * mine
    return sum(mine[:, c * HD : (c + 1) * HD] for c in range(part // HD))


def norm_scale(squares, width):
    return lax.rsqrt(jnp.sum(squares, axis=-1, keepdims=True) / width + norm_eps)


def block_of(distance, part):
    return pl.ds(pl.multiple_of((lax.axis_index("tp") ^ distance) * part, HD), part)


def rotate(x, cosine, sine):
    return (x * cosine + pltpu.roll(x, HD // 2, 1) * sine).astype(jnp.bfloat16)


def prepare_kernel(sizes, lengths, parents, gain, hidden, *refs):
    steps, own, tp, group, history, half_len, packed = sizes
    pieces = refs[: tp - 1]
    (
        gain_ref,
        xn_ref,
        scale_ref,
        key_cosine_ref,
        key_sine_ref,
        cosine_ref,
        sine_ref,
        bias_ref,
        lengths_s,
        parents_s,
        hidden_s,
        x_s,
        sems,
    ) = refs[tp - 1 :]
    rows = steps * own
    free = half_len // 2
    device = lax.axis_index("req")
    request = device // 2
    parity = device % 2

    copies = [
        pltpu.make_async_copy(source, target, sems.at[n])
        for n, (source, target) in enumerate(
            ((gain, gain_ref), (hidden, hidden_s), (lengths, lengths_s), (parents, parents_s))
        )
    ]
    for copy in copies:
        copy.start()
    for copy in copies:
        copy.wait()

    squares = []
    for t, piece in enumerate((hidden_s, *pieces)):
        place = block_of(t, piece.shape[-1])
        squares.append(lay_out(piece, place, gain_ref[:, place], x_s.at[t], xn_ref, 0))
    scale = norm_scale(sum(squares), xn_ref.shape[1])
    scale_ref[...] = jnp.broadcast_to(scale, scale_ref.shape)

    length = lengths_s[request]
    half_dim = HD // 2
    fall = -math.log(rope_base) / half_dim

    def angles(step, place):
        return (length + history + step).astype(jnp.float32) * jnp.exp(
            place.astype(jnp.float32) * fall
        )

    row = lax.broadcasted_iota(jnp.int32, (rows, HD), 0)
    lane = lax.broadcasted_iota(jnp.int32, (rows, HD), 1)
    angle = angles(quotient(row, own), remainder(lane, half_dim))
    key_cosine_ref[...] = jnp.cos(angle) * scale
    key_sine = jnp.sin(angle) * scale
    key_sine_ref[...] = jnp.where(lane < half_dim, -key_sine, key_sine)

    lanes = packed * group * 2 * rows
    place = lax.broadcasted_iota(jnp.int32, (half_dim, lanes), 0)
    lane = lax.broadcasted_iota(jnp.int32, (half_dim, lanes), 1)
    angle = angles(quotient(remainder(lane, rows), own), place)
    cosine_ref[...] = jnp.cos(angle)
    sine_ref[...] = jnp.sin(angle)

    def parent_of(s, beam):
        out = jnp.zeros_like(beam)
        for j in range(BEAMS):
            out = jnp.where(beam == j, parents_s[s, request * BEAMS + j], out)
        return out

    lane = lax.broadcasted_iota(jnp.int32, (8, lanes), 1)
    row_step = quotient(remainder(lane, rows), own)
    row_parity = jnp.where(lane < lanes // 2, parity, 1 - parity)
    beam = row_parity * own + remainder(lane, own)
    ancestors = [None] * steps
    at = beam
    for s in reversed(range(steps)):
        if s < steps - 1:
            at = jnp.where(row_step > s, parent_of(s + 1, at), beam)
        ancestors[s] = jnp.where(row_step >= s, at, -1)
    origin = parent_of(0, at)

    place = lax.broadcasted_iota(jnp.int32, (half_len - free, lanes), 0)
    place = parity * half_len + free + place
    bias_ref[pl.ds(0, half_len - free), :] = jnp.where(place < length, 0.0, masked_score)
    for n in range(own):
        seen = jnp.where(origin == parity * own + n, 0.0, masked_score)
        for c in range(0, history, 8):
            bias_ref[pl.ds(half_len - free + n * history + c, 8), :] = seen
    sublane = lax.broadcasted_iota(jnp.int32, (8, lanes), 0)
    for c in range(0, rows, 8):
        seen = jnp.full((8, lanes), masked_score, jnp.float32)
        for s in range(c // own, min((c + 8) // own, steps)):
            hit = (quotient(c + sublane, own) == s) & (
                ancestors[s] == parity * own + remainder(c + sublane, own)
            )
            seen = jnp.where(hit, 0.0, seen)
        bias_ref[pl.ds(half_len + own * history - free + c, 8), :] = seen


def fresh_kernel(
    xn_ref,
    scale_ref,
    key_cosine_ref,
    key_sine_ref,
    wk_ref,
    wv_ref,
    pv_ref,
    gv_ref,
    new_keys_ref,
    values_ref,
):
    rows = xn_ref.shape[0]
    half_len, width = pv_ref.shape[1:]
    old = values_ref.shape[1] - HD
    xn = xn_ref[...]
    keys = jnp.dot(xn, wk_ref[...], preferred_element_type=jnp.float32)
    values = jnp.dot(xn, wv_ref[...], preferred_element_type=jnp.float32)
    values_ref[:, pl.ds(0, half_len)] = pv_ref[0].T
    values_ref[:, pl.ds(half_len, old - half_len)] = gv_ref[...].reshape(-1, width).T
    for g in range(width // HD):
        cols = pl.ds(g * HD, HD)
        new_keys_ref[:, cols] = rotate(
            keys[:, g * HD : (g + 1) * HD], key_cosine_ref[...], key_sine_ref[...]
        )
    scale = scale_ref[...]
    values = [values[:, g * HD : (g + 1) * HD] * scale for g in range(width // HD)]
    values = jnp.concatenate(
        [jnp.concatenate(values, axis=1), jnp.zeros((HD - rows, width), jnp.float32)], axis=0
    )
    values_ref[:, pl.ds(old, HD)] = values.astype(jnp.bfloat16).T


def query_kernel(gain_ref, xn_ref, wq_ref, piece, product_ref, squares_ref, x_s, xn_s):
    rows = xn_ref.shape[0]
    place = block_of(0, piece.shape[-1])
    xn_s[pl.ds(0, rows), :] = xn_ref[:, place]
    squares_ref[...] = lay_out(piece, slice(None), gain_ref[:, place], x_s, xn_s, rows)
    product_ref[...] = jnp.dot(xn_s[...], wq_ref[place, :], preferred_element_type=jnp.float32)


def attend_kernel(
    sizes,
    gain_ref,
    xn_ref,
    scale_ref,
    new_keys_ref,
    values_ref,
    cosine_ref,
    sine_ref,
    bias_ref,
    wq_ref,
    pk_ref,
    gk_ref,
    product_ref,
    squares_ref,
    *refs,
):
    steps, own, tp, kv, group, packed = sizes
    pieces = refs[: tp - 1]
    kept_ref, kept_lse_ref, sent_ref, x_s, xn_s = refs[tp - 1 :]
    rows = steps * own
    part = pieces[0].shape[-1]
    packs = kv // packed
    each = packed * group
    size = each * HD
    lanes = each * 2 * rows
    keys_space = values_ref.shape[1]
    keys_count = keys_space - HD + rows
    free = keys_count - bias_ref.shape[0]
    lane = lax.broadcasted_iota(jnp.int32, (HD, lanes), 1)
    owner = quotient(remainder(lane, lanes // 2), group * rows)
    pad = jnp.zeros((keys_space - keys_count, lanes), jnp.bfloat16)

    squares = squares_ref[...]
    product = product_ref[...]
    for n, piece in enumerate(pieces):
        place = block_of(n + 1, part)
        xn_s[n, pl.ds(0, rows), :] = xn_ref[:, place]
        squares += lay_out(piece, slice(None), gain_ref[:, place], x_s.at[n], xn_s.at[n], rows)
        product += jnp.dot(xn_s[n], wq_ref[place, :], preferred_element_type=jnp.float32)
    scale = norm_scale(squares, xn_ref.shape[1])
    scale = jnp.concatenate([scale_ref[...], jnp.broadcast_to(scale, (rows, HD))], axis=0)
    scale = scale * HD**-0.5
    product = [product[:, h * HD : (h + 1) * HD] * scale for h in range(kv * group)]

    every = range(packs)
    cosine, sine = cosine_ref[...], sine_ref[...]
    scores = []
    for p in every:
        q = product[p * each : (p + 1) * each]
        q = jnp.concatenate([x[:rows] for x in q] + [x[rows:] for x in q], axis=0).T
        first, second = q[: HD // 2], q[HD // 2 :]
        q = jnp.concatenate(
            [first * cosine - second * sine, second * cosine + first * sine], axis=0
        )
        q = jnp.concatenate([jnp.where(owner == i, q, 0.0) for i in range(packed)], axis=0)
        cols = pl.ds(p * packed * HD, packed * HD)
        keys = jnp.concatenate(
            [
                pk_ref[0, :, cols],
                gk_ref[:, :, cols].reshape(-1, packed * HD),
                new_keys_ref[:, cols],
            ],
            axis=0,
        )
        score = jnp.dot(keys, q.astype(jnp.bfloat16), preferred_element_type=jnp.float32)
        scores.append(jnp.concatenate([score[:free], score[free:] + bias_ref[...]], axis=0))
    tops = [jnp.max(x, axis=0, keepdims=True) for x in scores]
    powers = [jnp.exp(x - top) for x, top in zip(scores, tops)]
    totals = [jnp.sum(x, axis=0, keepdims=True) for x in powers]
    mixed = [
        jnp.dot(
            values_ref[pl.ds(p * packed * HD, packed * HD), :],
            jnp.concatenate([powers[p].astype(jnp.bfloat16), pad], axis=0),
            preferred_element_type=jnp.float32,
        )
        for p in every
    ]
    results, logs = [], []
    for p in every:
        out = mixed[p][:HD]
        for i in range(1, packed):
            out = jnp.where(owner == i, mixed[p][i * HD : (i + 1) * HD], out)
        results.append(out * (1.0 / totals[p]))
        logs.append(jnp.broadcast_to(tops[p] + jnp.log(totals[p]), (8, lanes)))

    def sort(parts):
        half = lanes // 2
        if packs == 1:
            return parts[0][:, :half], parts[0][:, half:]
        low = lax.broadcasted_iota(jnp.int32, parts[0].shape, 1) < half
        first, second = parts
        return (
            jnp.where(low, first, pltpu.roll(second, half, 1)),
            jnp.where(low, pltpu.roll(first, half, 1), second),
        )

    kept_ref[...], sent = sort(results)
    kept_lse_ref[...], rest = sort(logs)
    sent_ref[pl.ds(0, HD), :] = sent.astype(jnp.bfloat16)
    rest = jnp.concatenate([rest] * (rows // 8), axis=0)
    sublane = lax.broadcasted_iota(jnp.int32, rest.shape, 0)
    terms = jnp.zeros(rest.shape, jnp.float32)
    for n in range(3):
        term = rest.astype(jnp.bfloat16).astype(jnp.float32)
        terms = jnp.where(sublane == n, term, terms)
        rest = rest - term
    sent_ref[pl.ds(HD, rows), :] = terms.astype(jnp.bfloat16)


def fetch_kernel(kept_lse_ref, w_out, kept_lse_out, w_out_ref, sems):
    tp, depth, part = w_out_ref.shape
    me_tp = lax.axis_index("tp")
    copies = []
    for d in range(1, tp):
        cols = pl.ds(pl.multiple_of((me_tp ^ d) * part, HD), part)
        for n in range(2):
            rows = pl.ds(n * (depth // 2), depth // 2)
            copies.append(
                pltpu.make_async_copy(
                    w_out.at[rows, cols], w_out_ref.at[d - 1, rows], sems.at[2 * d - 2 + n]
                )
            )
    for copy in copies:
        copy.start()
    kept_lse_out[...] = kept_lse_ref[...]
    for copy in copies:
        copy.wait()


def multiply_out(sizes, ctx, w_out_ref, first, out_ref):
    steps, own, chunk = sizes
    for lower in range(0, out_ref.shape[-1], chunk):
        place = pl.ds(pl.multiple_of(first + lower, HD), chunk)
        out = jnp.dot(ctx, w_out_ref[:, place], preferred_element_type=jnp.float32)
        for s in range(steps):
            out_ref[s, :, pl.ds(lower, chunk)] = out[s * own : (s + 1) * own].astype(out_ref.dtype)


def project_kernel(sizes, kept_ref, kept_lse_ref, got_ref, w_out_ref, ctx_ref, *outs):
    steps, own, tp, heads, chunk = sizes
    rows = steps * own
    terms = got_ref[pl.ds(HD, rows), :].astype(jnp.float32)
    lse_got = terms[0:1] + terms[1:2] + terms[2:3]
    lse_mine = kept_lse_ref[pl.ds(0, 1), :]
    top = jnp.maximum(lse_mine, lse_got)
    mine = jnp.exp(lse_mine - top)
    got = jnp.exp(lse_got - top)
    share = mine / (mine + got)
    ctx = kept_ref[...] * share + got_ref[pl.ds(0, HD), :].astype(jnp.float32) * (1.0 - share)
    ctx = ctx.T.astype(jnp.bfloat16)
    ctx = jnp.concatenate([ctx[h * rows : (h + 1) * rows] for h in range(heads)], axis=1)
    ctx_ref[...] = ctx
    for d in range(1, tp):
        multiply_out((steps, own, chunk), ctx, w_out_ref.at[d - 1], 0, outs[d - 1])


def project_own_kernel(sizes, ctx_ref, w_out_ref, out_ref):
    first = lax.axis_index("tp") * out_ref.shape[-1]
    multiply_out(sizes, ctx_ref[...], w_out_ref, first, out_ref)


def body(
    hidden_in,
    norm_gain,
    w_query,
    w_key,
    w_value,
    w_out,
    prompt_keys,
    prompt_values,
    gen_keys,
    gen_values,
    lengths,
    parents,
):
    steps, own, part = hidden_in.shape
    tp = lax.axis_size("tp")
    rows = steps * own
    width = w_query.shape[0]
    kv = w_key.shape[1] // HD
    group = w_query.shape[1] // w_key.shape[1]
    heads = kv * group
    history = gen_keys.shape[1]

    near_pieces = [across(hidden_in, 0, t) for t in range(1, tp)]
    tiny = jnp.cos(lax.broadcasted_iota(jnp.float32, (8, HD), 1))
    later = lax.optimization_barrier((hidden_in, tiny))[0]
    far_pieces = [across(hidden_in, 1, 0)] + [across(later, 1, t) for t in range(1, tp)]

    def in_hbm(x):
        return pltpu.with_memory_space_constraint(x, pltpu.HBM)

    def in_vmem(x):
        return pltpu.with_memory_space_constraint(x, pltpu.VMEM)

    vmem = pl.BlockSpec(memory_space=pltpu.VMEM)
    hbm = pl.BlockSpec(memory_space=pltpu.HBM)
    params = pltpu.CompilerParams(vmem_limit_bytes=16 * 2**20)
    f32, bf16 = jnp.float32, jnp.bfloat16
    half_len = prompt_keys.shape[1]
    old = half_len + own * history
    packed = 2 - kv % 2
    lanes = packed * group * 2 * rows
    gain, xn, scale, key_cosine, key_sine, cosine, sine, bias = pl.pallas_call(
        functools.partial(prepare_kernel, (steps, own, tp, group, history, half_len, packed)),
        out_shape=(
            jax.ShapeDtypeStruct((1, width), f32),
            jax.ShapeDtypeStruct((rows, width), bf16),
            jax.ShapeDtypeStruct((rows, HD), f32),
            jax.ShapeDtypeStruct((rows, HD), f32),
            jax.ShapeDtypeStruct((rows, HD), f32),
            jax.ShapeDtypeStruct((HD // 2, lanes), f32),
            jax.ShapeDtypeStruct((HD // 2, lanes), f32),
            jax.ShapeDtypeStruct((old + rows - half_len // 2, lanes), f32),
        ),
        in_specs=[hbm] * 4 + [vmem] * (tp - 1),
        out_specs=(vmem,) * 8,
        scratch_shapes=[
            pltpu.SMEM(lengths.shape, jnp.int32),
            pltpu.SMEM(parents.shape, jnp.int32),
            pltpu.VMEM(hidden_in.shape, bf16),
            pltpu.VMEM((tp, rows, part), f32),
            pltpu.SemaphoreType.DMA((4,)),
        ],
        compiler_params=params,
        cost_estimate=pl.CostEstimate(
            flops=2000 * 10**6, bytes_accessed=2**20, transcendentals=0
        ),
        name="prepare",
    )(*(in_hbm(x) for x in (lengths, parents, norm_gain[None, :], hidden_in)), *near_pieces)

    new_keys, values = pl.pallas_call(
        fresh_kernel,
        out_shape=(
            jax.ShapeDtypeStruct((rows, kv * HD), bf16),
            jax.ShapeDtypeStruct((kv * HD, old + HD), bf16),
        ),
        in_specs=[vmem] * 8,
        out_specs=(vmem,) * 2,
        compiler_params=params,
        name="fresh",
    )(
        xn,
        scale,
        key_cosine,
        key_sine,
        *(in_vmem(x) for x in (w_key, w_value, prompt_values, gen_values)),
    )

    w_query = in_vmem(w_query)
    product, squares = pl.pallas_call(
        query_kernel,
        out_shape=(
            jax.ShapeDtypeStruct((2 * rows, heads * HD), f32),
            jax.ShapeDtypeStruct((rows, HD), f32),
        ),
        in_specs=[vmem] * 4,
        out_specs=(vmem,) * 2,
        scratch_shapes=[pltpu.VMEM((rows, part), f32), pltpu.VMEM((2 * rows, part), bf16)],
        compiler_params=params,
        name="query",
    )(gain, xn, w_query, far_pieces[0])

    kept, kept_lse, sent = pl.pallas_call(
        functools.partial(attend_kernel, (steps, own, tp, kv, group, packed)),
        out_shape=(
            jax.ShapeDtypeStruct((HD, heads * rows), f32),
            jax.ShapeDtypeStruct((8, heads * rows), f32),
            jax.ShapeDtypeStruct((HD + rows, heads * rows), bf16),
        ),
        in_specs=[vmem] * (12 + tp),
        out_specs=(vmem,) * 3,
        scratch_shapes=[
            pltpu.VMEM((tp - 1, rows, part), f32),
            pltpu.VMEM((tp - 1, 2 * rows, part), bf16),
        ],
        compiler_params=params,
        name="attend",
    )(gain, xn, scale, new_keys, values, cosine, sine, bias, w_query, in_vmem(prompt_keys), in_vmem(gen_keys), product, squares, *far_pieces[1:])

    got = permute_by(sent, "req", 1)
    kept_lse, w_out_far = pl.pallas_call(
        fetch_kernel,
        out_shape=(
            jax.ShapeDtypeStruct((8, heads * rows), f32),
            jax.ShapeDtypeStruct((tp, heads * HD, part), bf16),
        ),
        in_specs=[vmem, hbm],
        out_specs=(vmem, vmem),
        scratch_shapes=[pltpu.SemaphoreType.DMA((2 * tp - 2,))],
        compiler_params=params,
        name="fetch",
    )(kept_lse, in_hbm(w_out))

    chunk = math.gcd(part, 1536)
    ctx, *sums = pl.pallas_call(
        functools.partial(project_kernel, (steps, own, tp, heads, chunk)),
        out_shape=(
            jax.ShapeDtypeStruct((rows, heads * HD), bf16),
            *[jax.ShapeDtypeStruct((steps, own, part), bf16)] * (tp - 1),
        ),
        in_specs=[vmem] * 4,
        out_specs=(vmem,) * tp,
        compiler_params=params,
        name="project",
    )(kept, kept_lse, got, w_out_far)
    sums = [across(x, 0, t + 1) for t, x in enumerate(sums)]
    total = pl.pallas_call(
        functools.partial(project_own_kernel, (steps, own, chunk)),
        out_shape=jax.ShapeDtypeStruct((steps, own, part), f32),
        in_specs=[vmem] * 2,
        out_specs=vmem,
        compiler_params=params,
        name="project_own",
    )(ctx, in_vmem(w_out))
    for x in sums:
        total = total + x.astype(f32)
    return total.astype(bf16)


def solution(mesh):
    in_specs = (
        P(None, "req", "tp"),
        P(),
        P(None, "tp"),
        P(None, "tp"),
        P(None, "tp"),
        P("tp", None),
        P("req", None, "tp"),
        P("req", None, "tp"),
        P("req", None, "tp"),
        P("req", None, "tp"),
        P(),
        P(),
    )
    out_specs = P(None, "req", "tp")
    return jax.shard_map(body, mesh=mesh, in_specs=in_specs, out_specs=out_specs, check_vma=False)
```
